32 devices in a mesh: grp: 2 (over y), pan: 16 (over z, x, core).
Axes of the slice: x: 2, y: 2, z: 4, core: 2. Of those that a mesh axis runs over, the one named last changes fastest.
Arguments:
- blocks: bfloat16 [1280, 512, 128], P(('grp', 'pan')), parts along dimension 0, may hold values from -6 to 6
- first_block: int32 [1280], P(('grp', 'pan')), parts along dimension 0, may hold values from 0 to 751
- second_block: int32 [1280], P(('grp', 'pan')), parts along dimension 0, may hold values from 0 to 1503
- slot_counts: int32 [32], P(('grp', 'pan')), parts along dimension 0, may hold values from 1 to 40, 240 in all
- ket_first: int32 [8], P('grp'), parts along dimension 0, may hold values from 0 to 751
- ket_second: int32 [8], P('grp'), parts along dimension 0, may hold values from 0 to 1503
- coefficients: bfloat16 [24064, 2000], P(('grp', 'pan')), parts along dimension 0, may hold values from -2 to 2
- mo_index: int32 [128], P('grp'), parts along dimension 0, may hold values from 0 to 1999, as said below
Outputs:
- integrals: float32 [8192, 4096], P(('grp', 'pan')), parts along dimension 0
The draws below stay inside these ranges and needn't reach their ends.
There are 2 independent parts, one for each index of `grp`. The reference program is written for one: setup_inputs(seed, part) draws one part's arguments, and reference() takes and returns one part's arrays. A program takes and returns all parts, laid end to end along the dimension named above; each array names one. Nothing has to cross between parts.
Inputs may be any that keep to these rules, and one draw needn't show every extreme that they name: `slot_counts`: the counts sum to 240; the largest is exactly 40. `mo_index`: distinct orbital numbers.
All inputs are finite; a program needn't handle non-finite values. No bound on the sum of `slot_counts` on one device may be relied on, other than what follows from the above.
Results may differ from the reference program's by a relative error of at most 0.005.
Values may be sent and summed in bfloat16 or wider, within the bound.
No kernel may reach another device: no remote copies, remote signals or barrier semaphores. Data moves between devices by JAX's collectives and lax.ppermute only.
A program may use at most 128 MiB of HBM per device.

```python
import math
import jax
import jax.numpy as jnp
import numpy as np
from jax import lax

NAO = 12032
NMO = 2000
NB = 64
KP = 512
CAP = 40
TOTAL = 240
SLOTS = 640
KETB = 4
N_PAN = 16


def draw_mo_index(key, part):
    key = jax.random.fold_in(key, 7)
    return jax.random.permutation(key, NMO)[:NB].astype(jnp.int32)


def set_ends(entries, stream_key, low, top_value):
    spot = [jax.random.randint(jax.random.fold_in(stream_key, axis), (), 0, length) for axis, length in enumerate(entries.shape)]
    longest = entries.shape.index(max(entries.shape))
    beside = spot[:longest] + [(spot[longest] + 1) % entries.shape[longest]] + spot[longest + 1:]
    return entries.at[tuple(spot)].set(low).at[tuple(beside)].set(top_value)


def levels(own_key, extent, split, low, largest):
    factor_of, own = 1.0, jax.random.fold_in(own_key, 6)
    for axis_at, blocks in split:
        draws = jnp.exp(jax.random.uniform(jax.random.fold_in(own, axis_at), (blocks,), jnp.float32, low / len(split), largest / len(split)))
        factor_of = factor_of * jnp.repeat(draws, extent[axis_at] // blocks).reshape([-1 if axis == axis_at else 1 for axis in range(len(extent))])
    return factor_of


def split_up(count, total, reach, slope):
    weights = [(1 << 20) // math.isqrt(standing ** slope) + 1 for standing in range(2, count + 1)]
    surplus, holding = total - reach - (count - 1), [1] * (count - 1)
    while surplus > 0:
        movable = [i for i in range(count - 1) if holding[i] < reach]
        whole, remaining = sum([weights[i] for i in movable]), surplus
        for i in movable:
            more = min(reach - holding[i], max(1, remaining * weights[i] // whole), surplus)
            holding[i] = holding[i] + more
            surplus = surplus - more
    return np.array([reach] + holding)


def ragged_sizes(stream_key, number_of, total, most, slope):
    if number_of == 2:
        one = jax.random.randint(stream_key, (), max(1, total - most), min(most, total - 1) + 1)
        return jnp.stack([one, total - one])
    tallies = jnp.asarray(split_up(number_of, total, most, slope), jnp.int32)
    pairs = (number_of - 1) // 2
    source_of, sink = tallies[1:1 + 2 * pairs:2], tallies[2:2 + 2 * pairs:2]
    margin = jnp.minimum(source_of - 1, most - sink)
    moved = jax.random.randint(jax.random.fold_in(stream_key, 1), (pairs,), 0, 1 << 20) % (margin + 1)
    tallies = tallies.at[1:1 + 2 * pairs:2].set(source_of - moved).at[2:2 + 2 * pairs:2].set(sink + moved)
    return tallies[jax.random.permutation(jax.random.fold_in(stream_key, 2), number_of)]


def scatter_about(key, dims, deviation, bound, split=(), kind=jnp.bfloat16):
    result = deviation * jax.random.normal(key, dims, jnp.float32)
    if split:
        result = result * levels(key, dims, split, -0.22, 0.18)
    return jnp.clip(result, -bound, bound).astype(kind)


def setup_inputs(seed: int = 0, part: int = 0) -> dict:
    streams_of = jax.random.split(jax.random.key(seed), 9)
    part_keys = jax.random.split(jax.random.fold_in(streams_of[8], part), 9)
    return {
        "blocks": scatter_about(part_keys[0], (SLOTS, KP, 128), 1.0, 6.0, ((0, 16),)),
        "first_block": set_ends(jax.random.randint(part_keys[1], (SLOTS,), 0, NAO // 16), jax.random.fold_in(part_keys[1], 1), 0, (NAO // 16) - 1).astype(jnp.int32),
        "second_block": set_ends(jax.random.randint(part_keys[2], (SLOTS,), 0, NAO // 8), jax.random.fold_in(part_keys[2], 1), 0, (NAO // 8) - 1).astype(jnp.int32),
        "slot_counts": ragged_sizes(part_keys[3], N_PAN, TOTAL, CAP, 2).astype(jnp.int32),
        "ket_first": set_ends(jax.random.randint(part_keys[4], (KETB,), 0, NAO // 16), jax.random.fold_in(part_keys[4], 1), 0, (NAO // 16) - 1).astype(jnp.int32),
        "ket_second": set_ends(jax.random.randint(part_keys[5], (KETB,), 0, NAO // 8), jax.random.fold_in(part_keys[5], 1), 0, (NAO // 8) - 1).astype(jnp.int32),
        "coefficients": scatter_about(part_keys[6], (NAO, NMO), ((128 * KP * TOTAL) ** -0.125), 2.0, ((0, 16),)),
        "mo_index": draw_mo_index(jax.random.fold_in(jax.random.fold_in(streams_of[8], part), 71), part),
    }


def block_rows(chosen, numbers, span_width):
    offsets = jnp.arange(span_width, dtype=jnp.int32)
    row_numbers = (numbers.astype(jnp.int32)[:, None] * span_width + offsets[None, :]).astype(jnp.int32)
    return jnp.take(chosen, row_numbers, axis=0)


def ket_table(chosen, ket_first, ket_second):
    lambda_rows = block_rows(chosen, ket_first, 16).astype(jnp.float32)
    sigma_rows = block_rows(chosen, ket_second, 8).astype(jnp.float32)
    block_count = lambda_rows.shape[0]
    orbitals = lambda_rows.shape[2]
    product_table = lambda_rows[:, :, None, :, None] * sigma_rows[:, None, :, None, :]
    return product_table.reshape(block_count * 128, orbitals * orbitals).astype(jnp.bfloat16)


def live_slots(counts, capacity, overall):
    counts = counts.astype(jnp.int32)
    block_ends = jnp.cumsum(counts).astype(jnp.int32)
    starts = (block_ends - counts).astype(jnp.int32)
    target = jnp.arange(overall, dtype=jnp.int32)
    owners = jnp.sum((block_ends[None, :] <= target[:, None]).astype(jnp.int32), axis=1).astype(jnp.int32)
    within = (target - jnp.take(starts, owners)).astype(jnp.int32)
    return (owners * capacity + within).astype(jnp.int32)


def reference(blocks, first_block, second_block, slot_counts, ket_first, ket_second, coefficients, mo_index):
    chosen = jnp.take(coefficients, mo_index.astype(jnp.int32), axis=1)
    product_table = ket_table(chosen, ket_first, ket_second)
    picked = live_slots(slot_counts, CAP, TOTAL)
    group_size = math.gcd(TOTAL, 16)
    turn_count = TOTAL // group_size
    picked = picked.reshape(turn_count, group_size)

    def advance(running, slot_ids):
        block_data = jnp.take(blocks, slot_ids, axis=0).astype(jnp.float32).reshape(group_size, KP, 16, 8)
        first_rows = block_rows(chosen, jnp.take(first_block, slot_ids), 16).astype(jnp.float32)
        second_rows = block_rows(chosen, jnp.take(second_block, slot_ids), 8).astype(jnp.float32)
        halfway = lax.dot_general(block_data, first_rows, (((2,), (1,)), ((0,), (0,))), precision=lax.Precision.HIGHEST, preferred_element_type=jnp.float32)
        halfway = lax.optimization_barrier(halfway.astype(jnp.bfloat16)).astype(jnp.float32)
        product = lax.dot_general(halfway, second_rows, (((0, 2), (0, 1)), ((), ())), precision=lax.Precision.HIGHEST, preferred_element_type=jnp.float32)
        return running + product, None

    running, unused = lax.scan(advance, jnp.zeros((KP, NB, NB), jnp.float32), picked)
    half_rounded = running.reshape(KP, NB * NB).astype(jnp.bfloat16)
    return lax.dot_general(half_rounded.astype(jnp.float32), product_table.astype(jnp.float32), (((0,), (0,)), ((), ())), precision=lax.Precision.HIGHEST, preferred_element_type=jnp.float32)
```

```python
import functools

import jax
import jax.numpy as jnp
from jax import lax
from jax.experimental import pallas as pl
from jax.experimental.pallas import tpu as pltpu
from jax.sharding import PartitionSpec as P

GROUP = 32
LANES = 128
UNIT = 16384
BF = jnp.bfloat16
F32 = jnp.float32


def spread(kind):
    row = lax.broadcasted_iota(jnp.int32, (LANES, LANES), 0)
    col = lax.broadcasted_iota(jnp.int32, (LANES, LANES), 1)
    source = col // 8 if kind == "a" else col % 8
    return (row == source).astype(F32).astype(BF)


def table_piece(table, code, target):
    unit = code // UNIT
    lane = code % UNIT
    start = pl.multiple_of((lane // LANES) * LANES, LANES)
    piece = table[unit, :, pl.ds(start, LANES)].astype(F32)
    shift = lax.rem(target - lane % LANES + 2 * LANES, LANES)
    return pltpu.roll(piece, shift, 1)


def load_table(parts, table, sems):
    copies = []
    at = 0
    for n, part in enumerate(parts):
        units = part.shape[0]
        copies.append(pltpu.make_async_copy(part, table.at[pl.ds(at, units)], sems.at[n]))
        at += units
    return copies


def bra_kernel(part_count, chunk, fcode, scode, info, *refs):
    parts, refs = refs[:part_count], refs[part_count:]
    own, other = refs[:2]
    out_count = len(refs) - 2 - 8
    outs = refs[2 : 2 + out_count]
    table, blk, wide, half, second, total, table_sems, block_sems = refs[2 + out_count :]
    orbitals = table.shape[1]
    capacity = own.shape[0]
    kh = blk.shape[1]
    width = chunk * out_count
    own_live, other_live = info[0], info[1]
    k_start = pl.multiple_of(info[2], 128)
    live = own_live + other_live

    copies = load_table(parts, table, table_sems)
    for copy in copies:
        copy.start()

    def own_copy(n):
        return pltpu.make_async_copy(
            own.at[n, pl.ds(k_start, kh)], blk.at[n], block_sems.at[n // GROUP]
        )

    def other_copy(n):
        return pltpu.make_async_copy(
            other.at[n - own_live], blk.at[n], block_sems.at[n // GROUP]
        )

    def start_own(n, carry):
        own_copy(n).start()
        return carry

    def start_other(n, carry):
        other_copy(n).start()
        return carry

    lax.fori_loop(0, own_live, start_own, 0)
    lax.fori_loop(own_live, live, start_other, 0)
    total[...] = jnp.zeros_like(total)
    half[...] = jnp.zeros_like(half)
    lanes = lax.broadcasted_iota(jnp.int32, (8, LANES), 1)
    diagonal = (lanes % 8 == lax.broadcasted_iota(jnp.int32, (8, LANES), 0)).astype(F32)
    spread_a = spread("a")
    for copy in copies:
        copy.wait()

    def do_group(g, carry):
        base = g * GROUP
        count = jnp.minimum(live - base, GROUP)

        def wait_one(n, carry):
            pltpu.make_async_copy(
                own.at[0, pl.ds(0, kh)], blk.at[n], block_sems.at[g]
            ).wait()
            return carry

        lax.fori_loop(base, base + count, wait_one, 0)
        second[...] = jnp.zeros_like(second)

        def do_pair(p, carry):
            results = []
            for u in range(2):
                place = 2 * p + u
                n = jnp.minimum(base + place, live - 1)
                slot = jnp.where(n < own_live, n, capacity + n - own_live)
                piece = table_piece(table, fcode[slot], 0)
                wide[u] = jnp.dot(piece.astype(BF), spread_a, preferred_element_type=F32)
                rows = []
                for q in range(out_count):
                    start = pl.multiple_of(info[3 + q], 8)
                    for r in range(chunk):
                        row = wide[u, pl.ds(start + r, 1), :]
                        rows.append(jnp.broadcast_to(row, (8, LANES)) * diagonal)
                factor = jnp.concatenate(rows, axis=0).astype(BF)
                result = lax.dot_general(
                    factor, blk[n], (((1,), (1,)), ((), ())), preferred_element_type=F32
                )
                results.append(result.reshape(width, 8, kh))
                piece = table_piece(table, scode[slot], 8 * lax.rem(place, 16))
                side = place // 16
                low = 8 * lax.rem(place, 16)
                wanted = lax.broadcasted_iota(jnp.int32, (orbitals, LANES), 1)
                keep = (wanted >= low) & (wanted < low + 8) & (base + place < live)
                second[side] = jnp.where(keep, piece, second[side])
            both = jnp.concatenate(results, axis=1).astype(BF)
            half[:, pl.ds(pl.multiple_of(p * 16, 16), 16), :] = both
            return carry

        lax.fori_loop(0, (count + 1) // 2, do_pair, 0)
        weights = jnp.concatenate([second[0], second[1]], axis=1).astype(BF)
        for i in range(width):
            rows = pl.ds(i * orbitals, orbitals)
            total[rows, :] += jnp.dot(weights, half[i], preferred_element_type=F32)
        return carry

    lax.fori_loop(0, (live + GROUP - 1) // GROUP, do_group, 0)
    size = chunk * orbitals
    for q in range(out_count):
        outs[q][...] = total[q * size : (q + 1) * size, :].astype(outs[q].dtype)


def bra_transform(parts, own, other, fcode, scode, info, chunk, out_count, out_type):
    orbitals = parts[0].shape[1]
    capacity, kp, pair = own.shape
    kh = other.shape[1]
    units = sum(part.shape[0] for part in parts)
    groups = -(-2 * capacity // GROUP)
    rows = chunk * orbitals
    anywhere = pl.BlockSpec(memory_space=pl.ANY)
    width = chunk * out_count
    return pl.pallas_call(
        functools.partial(bra_kernel, len(parts), chunk),
        out_shape=[jax.ShapeDtypeStruct((rows, kh), out_type)] * out_count,
        grid_spec=pltpu.PrefetchScalarGridSpec(
            num_scalar_prefetch=3,
            grid=(),
            in_specs=[anywhere] * (len(parts) + 2),
            out_specs=[pl.BlockSpec(memory_space=pltpu.VMEM)] * out_count,
            scratch_shapes=[
                pltpu.VMEM((units, orbitals, parts[0].shape[2]), BF),
                pltpu.VMEM((2 * capacity, kh, pair), BF),
                pltpu.VMEM((2, orbitals, LANES), F32),
                pltpu.VMEM((width, 8 * GROUP, kh), BF),
                pltpu.VMEM((2, orbitals, LANES), F32),
                pltpu.VMEM((rows * out_count, kh), F32),
                pltpu.SemaphoreType.DMA((len(parts),)),
                pltpu.SemaphoreType.DMA((groups,)),
            ],
        ),
        compiler_params=pltpu.CompilerParams(vmem_limit_bytes=40 * 2**20),
        cost_estimate=pl.CostEstimate(
            flops=2 * 2 * capacity * 8 * width * pair * kh, bytes_accessed=8 * 2**20, transcendentals=0
        ),
        name="bra_transform",
    )(fcode, scode, info, *parts, own, other)


def ket_kernel(part_count, code1, code2, *refs):
    parts = refs[:part_count]
    out, table, first, sems = refs[part_count:]
    orbitals = table.shape[1]
    copies = load_table(parts, table, sems)
    for copy in copies:
        copy.start()
    for copy in copies:
        copy.wait()
    for kb in range(out.shape[1] // LANES):
        piece = table_piece(table, code1[kb], 0)
        first[...] = jnp.dot(piece.astype(BF), spread("a"), preferred_element_type=F32)
        piece = table_piece(table, code2[kb], 0)
        last = jnp.dot(piece.astype(BF), spread("b"), preferred_element_type=F32)
        for r in range(orbitals):
            row = jnp.broadcast_to(first[r : r + 1, :], (orbitals, LANES))
            rows = pl.ds(r * orbitals, orbitals)
            out[rows, kb * LANES : (kb + 1) * LANES] = (row * last).astype(BF)


def ket_table(parts, code1, code2):
    orbitals = parts[0].shape[1]
    units = sum(part.shape[0] for part in parts)
    shape = (orbitals * orbitals, code1.shape[0] * LANES)
    return pl.pallas_call(
        functools.partial(ket_kernel, len(parts)),
        out_shape=jax.ShapeDtypeStruct(shape, BF),
        grid_spec=pltpu.PrefetchScalarGridSpec(
            num_scalar_prefetch=2,
            grid=(),
            in_specs=[pl.BlockSpec(memory_space=pl.ANY)] * len(parts),
            out_specs=pl.BlockSpec(memory_space=pltpu.VMEM),
            scratch_shapes=[
                pltpu.VMEM((units, orbitals, parts[0].shape[2]), BF),
                pltpu.VMEM((orbitals, LANES), F32),
                pltpu.SemaphoreType.DMA((len(parts),)),
            ],
        ),
        compiler_params=pltpu.CompilerParams(vmem_limit_bytes=24 * 2**20),
        cost_estimate=pl.CostEstimate(
            flops=2 * 2**20, bytes_accessed=6 * 2**20, transcendentals=0
        ),
        name="ket_table",
    )(code1, code2, *parts)


def permute(array, mask, count):
    return lax.ppermute(array, "pan", [(i, i ^ mask) for i in range(count)])


def added(*arrays):
    result = arrays[0].astype(F32)
    for array in arrays[1:]:
        result = result + array.astype(F32)
    return result.astype(BF)


def shards(
    count, blocks, first_block, second_block, slot_counts, ket_first, ket_second, coefficients, mo_index
):
    me = lax.axis_index("pan").astype(jnp.int32)
    core = me % 2
    capacity, kp, pair = blocks.shape
    kh = kp // 2
    own_ao, nmo = coefficients.shape
    swap = functools.partial(permute, mask=1, count=count)

    picks = (mo_index[:, None] == jnp.arange(nmo, dtype=jnp.int32)[None, :]).astype(BF)
    mine = lax.dot_general(
        picks, coefficients, (((1,), (1,)), ((), ())), preferred_element_type=F32
    ).astype(BF)
    orbitals = mine.shape[0]

    leaving = lax.dynamic_slice_in_dim(blocks, (1 - core) * kh, kh, axis=1)
    other = swap(leaving)
    numbers = jnp.concatenate([first_block, second_block, slot_counts])
    other_numbers = swap(numbers)
    firsts = jnp.concatenate([first_block, other_numbers[:capacity]]) * 16
    seconds = jnp.concatenate([second_block, other_numbers[capacity : 2 * capacity]]) * 8
    lives = [slot_counts[0], other_numbers[2 * capacity]]

    small = count == 16 and own_ao % 16 == 0
    if small:
        mine = jnp.pad(mine, ((0, 0), (0, -own_ao % LANES)))
        along_z = [None, None, None, None]
        for s in (3, 2, 1):
            along_z[s] = permute(mine, 4 * s, count)
        along_z[0] = mine
        near = jnp.stack(along_z)
        far = permute(near, 2, count)
        parts = [near, swap(near), far, swap(far)]

        def encode(rows):
            away = (rows // own_ao) ^ me
            unit = ((away >> 1) & 1) * 8 + (away & 1) * 4 + (away >> 2)
            return unit * UNIT + rows % own_ao
    else:
        parts = [lax.all_gather(mine, "pan", axis=1, tiled=True)[None]]

        def encode(rows):
            return rows

    fcode, scode = encode(firsts), encode(seconds)
    ahead = jnp.arange(ket_first.shape[0], dtype=jnp.int32)
    turned = (ahead + core * (ket_first.shape[0] // 2)) % ket_first.shape[0]
    table = ket_table(
        parts,
        encode(jnp.take(ket_first, turned) * 16),
        encode(jnp.take(ket_second, turned) * 8),
    )

    if small:
        my_z, my_x = me // 4, (me // 2) % 2
        order = (3, 2, 1, 0)
        chunk = orbitals // 8
        results = []
        for x in (1 - my_x, my_x):
            starts = [((my_z ^ s) * 2 + x) * chunk for s in order]
            info = jnp.stack([*lives, core * kh, *starts]).astype(jnp.int32)
            results.append(
                bra_transform(parts, blocks, other, fcode, scode, info, chunk, 4, BF)
            )
        arrived = [permute(piece, 2, count) for piece in results[0]]
        kept = results[1]
        three = permute(added(kept[0], arrived[0]), 4, count)
        two = permute(added(kept[1], arrived[1], three), 8, count)
        one = permute(added(kept[2], arrived[2]), 4, count)
        done = added(kept[3], arrived[3], one, two)
    else:
        info = jnp.stack([*lives, core * kh, jnp.int32(0)]).astype(jnp.int32)
        (partial,) = bra_transform(parts, blocks, other, fcode, scode, info, orbitals, 1, F32)
        sides = [list(range(c, count, 2)) for c in range(2)]
        done = lax.psum_scatter(
            partial, "pan", scatter_dimension=0, tiled=True, axis_index_groups=sides
        ).astype(BF)
    rows = done.shape[0] // 2
    keep = lax.dynamic_slice_in_dim(done, core * rows, rows, axis=0)
    give = lax.dynamic_slice_in_dim(done, (1 - core) * rows, rows, axis=0)
    half_rounded = jnp.concatenate([keep, swap(give)], axis=1)
    return lax.dot_general(
        half_rounded, table, (((1,), (1,)), ((), ())), preferred_element_type=F32
    )


def solution(mesh):
    placed = (
        P(("grp", "pan"), None, None),
        P(("grp", "pan")),
        P(("grp", "pan")),
        P(("grp", "pan")),
        P("grp"),
        P("grp"),
        P(("grp", "pan"), None),
        P("grp"),
    )
    return jax.shard_map(
        functools.partial(shards, mesh.shape["pan"]),
        mesh=mesh,
        in_specs=placed,
        out_specs=P(("grp", "pan"), None),
        check_vma=False,
    )
```

```python
import functools

import jax
import jax.numpy as jnp
from jax import lax
from jax.experimental import pallas as pl
from jax.experimental.pallas import tpu as pltpu
from jax.sharding import PartitionSpec as P

GROUP = 32
STEP = 8
LANES = 128
BF = jnp.bfloat16
F32 = jnp.float32


def spread(kind):
    row = lax.broadcasted_iota(jnp.int32, (LANES, LANES), 0)
    col = lax.broadcasted_iota(jnp.int32, (LANES, LANES), 1)
    source = col // 8 if kind == "a" else col % 8
    return (row == source).astype(F32).astype(BF)


def table_piece(table, place, target):
    core, z, x, lane = place
    start = pl.multiple_of((lane // LANES) * LANES, LANES)
    piece = table[core, z, x, :, pl.ds(start, LANES)].astype(F32)
    shift = lax.rem(target - lane % LANES + 2 * LANES, LANES)
    return pltpu.roll(piece, shift, 1)


def load_table(regions, parts, table, sems):
    return [
        pltpu.make_async_copy(part, table.at[region], sems.at[n])
        for n, (region, part) in enumerate(zip(regions, parts))
    ]


def bra_kernel(regions, locate, chunk, pieces, me_ref, x_ref, mine, theirs, *refs):
    parts, refs = refs[: len(regions)], refs[len(regions) :]
    own, other = refs[:2]
    outs = refs[2 : 2 + len(pieces)]
    table, blk, picked, wide, half, second, ready, table_sems, block_sems, out_sems = refs[
        2 + len(pieces) :
    ]
    orbitals = second.shape[1]
    capacity = own.shape[0]
    kh = blk.shape[1]
    chunks = ready.shape[0]
    width = chunk * chunks
    me = me_ref[0]
    own_live, other_live = mine[2 * capacity], theirs[2 * capacity]
    k_start = pl.multiple_of(lax.rem(me, 2) * kh, LANES)
    live = own_live + other_live

    copies = load_table(regions, parts, table, table_sems)
    for copy in copies:
        copy.start()

    def start_own(n, carry):
        pltpu.make_async_copy(
            own.at[n, pl.ds(k_start, kh)], blk.at[n], block_sems.at[n // STEP]
        ).start()
        return carry

    def start_other(n, carry):
        pltpu.make_async_copy(
            other.at[n - own_live], blk.at[n], block_sems.at[n // STEP]
        ).start()
        return carry

    lax.fori_loop(0, own_live, start_own, 0)
    lax.fori_loop(own_live, live, start_other, 0)
    lanes = lax.broadcasted_iota(jnp.int32, (8, LANES), 1)
    diagonal = (lanes % 8 == lax.broadcasted_iota(jnp.int32, (8, LANES), 0)).astype(F32)
    empty = jnp.zeros((8, LANES), F32)
    spread_a = spread("a")
    groups = (live + GROUP - 1) // GROUP
    steps = (live + STEP - 1) // STEP
    second[...] = jnp.zeros_like(second)
    if chunks == 1:
        starts = [0]
    else:
        starts = [((me // 4) ^ s) * 2 * chunk + x_ref[0] * chunk for s in range(chunks)]
        starts = [pl.multiple_of(start, chunk) for start in starts]

    def number(n, column):
        ours = mine[column * capacity + jnp.minimum(n, own_live - 1)]
        partners = theirs[column * capacity + jnp.maximum(n - own_live, 0)]
        return jnp.where(n < own_live, ours, partners)

    for copy in copies:
        copy.wait()

    def do_step(o, carry):
        start = o * STEP

        def wait_one(n, carry):
            pltpu.make_async_copy(other.at[0], blk.at[n], block_sems.at[o]).wait()
            return carry

        lax.fori_loop(start, jnp.minimum(start + STEP, live), wait_one, 0)
        slots = [jnp.minimum(start + u, live - 1) for u in range(STEP)]
        for u, n in enumerate(slots):
            piece = table_piece(table, locate(number(n, 0) * 16, me), 0)
            picked[u * orbitals : (u + 1) * orbitals] = piece.astype(BF)
        wide[...] = jnp.dot(picked[...], spread_a, preferred_element_type=F32)

        cover = 8 * STEP
        parity = lax.rem(o, LANES // cover)
        wanted = lax.broadcasted_iota(jnp.int32, (orbitals, LANES), 1)
        place = (wanted % cover) // 8
        merged = jnp.zeros((orbitals, LANES), F32)
        for u, n in enumerate(slots):
            where = locate(number(n, 1) * 8, me)
            piece = table_piece(table, where, parity * cover + 8 * u)
            merged = jnp.where(place == u, piece, merged)
        keep = (wanted // cover == parity) & (start + place < live)
        at = o // (LANES // cover)
        second[at] = jnp.where(keep, merged, second[at])

        for p in range(STEP // 2):
            rows = []
            for q in range(chunks):
                for r in range(chunk):
                    x, y = (
                        jnp.broadcast_to(
                            wide[pl.ds((2 * p + u) * orbitals + starts[q] + r, 1), :], (8, LANES)
                        )
                        * diagonal
                        for u in range(2)
                    )
                    rows.append(jnp.concatenate([x, empty], axis=1))
                    rows.append(jnp.concatenate([empty, y], axis=1))
            factor = jnp.concatenate(rows, axis=0).astype(BF)
            data = jnp.concatenate([blk[slots[2 * p]], blk[slots[2 * p + 1]]], axis=1)
            result = lax.dot_general(
                factor, data, (((1,), (1,)), ((), ())), preferred_element_type=F32
            )
            at = pl.multiple_of(o * cover + 16 * p, 16)
            half[:, pl.ds(at, 16), :] = result.astype(BF).reshape(width, 16, kh)
        return carry

    lax.fori_loop(0, steps, do_step, 0)

    def clear(o, carry):
        at = pl.multiple_of(o * 8 * STEP, 8 * STEP)
        half[:, pl.ds(at, 8 * STEP), :] = jnp.zeros((width, 8 * STEP, kh), BF)
        return carry

    lax.fori_loop(steps, groups * (GROUP // STEP), clear, 0)

    def leave(n):
        s, low, high = pieces[n]
        return pltpu.make_async_copy(
            ready.at[s, :, pl.ds(low, high - low)], outs[n], out_sems.at[n]
        )

    def finish(count):
        weights = jnp.concatenate([second[n] for n in range(2 * count)], axis=1).astype(BF)
        for s in sorted({piece[0] for piece in pieces}, reverse=True):
            for r in range(chunk):
                piece = half[s * chunk + r, 0 : 8 * GROUP * count, :]
                ready[s, r * orbitals : (r + 1) * orbitals, :] = jnp.dot(
                    weights, piece, preferred_element_type=F32
                ).astype(ready.dtype)
            for n in range(len(pieces)):
                if pieces[n][0] == s:
                    leave(n).start()

    for count in range(1, half.shape[1] // (8 * GROUP) + 1):
        pl.when(groups == count)(functools.partial(finish, count))
    for n in range(len(pieces)):
        leave(n).wait()


def bra_transform(regions, locate, parts, own, other, numbers, me, x, chunk, chunks, pieces, kind):
    orbitals = chunk if chunks == 1 else 2 * chunk * chunks
    capacity, kp, pair = own.shape
    kh = other.shape[1]
    groups = -(-2 * capacity // GROUP)
    rows = chunk * orbitals
    hbm = pl.BlockSpec(memory_space=pltpu.HBM)
    width = chunk * chunks
    return pl.pallas_call(
        functools.partial(bra_kernel, regions, locate, chunk, pieces),
        out_shape=[jax.ShapeDtypeStruct((rows, high - low), kind) for _, low, high in pieces],
        grid_spec=pltpu.PrefetchScalarGridSpec(
            num_scalar_prefetch=4,
            grid=(),
            in_specs=[hbm] * (len(parts) + 2),
            out_specs=[hbm] * len(pieces),
            scratch_shapes=[
                pltpu.VMEM(table_shape(parts, orbitals), BF),
                pltpu.VMEM((2 * capacity, kh, pair), BF),
                pltpu.VMEM((STEP * orbitals, LANES), BF),
                pltpu.VMEM((STEP * orbitals, LANES), F32),
                pltpu.VMEM((width, 8 * GROUP * groups, kh), BF),
                pltpu.VMEM((2 * groups, orbitals, LANES), F32),
                pltpu.VMEM((chunks, rows, kh), kind),
                pltpu.SemaphoreType.DMA((len(parts),)),
                pltpu.SemaphoreType.DMA((-(-2 * capacity // STEP),)),
                pltpu.SemaphoreType.DMA((len(pieces),)),
            ],
        ),
        compiler_params=pltpu.CompilerParams(vmem_limit_bytes=(28 if chunks > 1 else 56) * 2**20),
        cost_estimate=pl.CostEstimate(
            flops=4 * capacity * 8 * width * pair * kh, bytes_accessed=8 * 2**20, transcendentals=0
        ),
        name="bra_transform",
    )(me, x, *numbers, *parts, own, other)


def table_shape(parts, orbitals):
    if len(parts) == 1:
        return (1, 1, 1, orbitals, parts[0].shape[-1])
    return (2, 4, 2, orbitals, parts[0].shape[-1])


def ket_kernel(regions, locate, me_ref, firsts, seconds, *refs):
    parts = refs[: len(regions)]
    out, table, first, sems = refs[len(regions) :]
    orbitals = first.shape[0]
    me = me_ref[0]
    copies = load_table(regions, parts, table, sems)
    for copy in copies:
        copy.start()
    for copy in copies:
        copy.wait()
    count = out.shape[1] // LANES
    for n in range(count):
        kb = lax.rem(n + lax.rem(me, 2) * (count // 2), count)
        piece = table_piece(table, locate(firsts[kb] * 16, me), 0)
        first[...] = jnp.dot(piece.astype(BF), spread("a"), preferred_element_type=F32)
        piece = table_piece(table, locate(seconds[kb] * 8, me), 0)
        last = jnp.dot(piece.astype(BF), spread("b"), preferred_element_type=F32)
        for r in range(orbitals):
            row = jnp.broadcast_to(first[r : r + 1, :], (orbitals, LANES))
            rows = pl.ds(r * orbitals, orbitals)
            out[rows, n * LANES : (n + 1) * LANES] = (row * last).astype(BF)


def ket_table(regions, locate, parts, ket_first, ket_second, me, orbitals):
    shape = (orbitals * orbitals, ket_first.shape[0] * LANES)
    return pl.pallas_call(
        functools.partial(ket_kernel, regions, locate),
        out_shape=jax.ShapeDtypeStruct(shape, BF),
        grid_spec=pltpu.PrefetchScalarGridSpec(
            num_scalar_prefetch=3,
            grid=(),
            in_specs=[pl.BlockSpec(memory_space=pltpu.HBM)] * len(parts),
            out_specs=pl.BlockSpec(memory_space=pltpu.VMEM),
            scratch_shapes=[
                pltpu.VMEM(table_shape(parts, orbitals), BF),
                pltpu.VMEM((orbitals, LANES), F32),
                pltpu.SemaphoreType.DMA((len(parts),)),
            ],
        ),
        compiler_params=pltpu.CompilerParams(vmem_limit_bytes=24 * 2**20),
        cost_estimate=pl.CostEstimate(
            flops=2 * 2**20, bytes_accessed=6 * 2**20, transcendentals=0
        ),
        name="ket_table",
    )(me, ket_first, ket_second, *parts)


def permute(array, mask, count):
    return lax.ppermute(array, "pan", [(i, i ^ mask) for i in range(count)])


def added(*arrays):
    result = arrays[0].astype(F32)
    for array in arrays[1:]:
        result = result + array.astype(F32)
    return result.astype(BF)


def after(array, *others):
    return lax.optimization_barrier((array, *others))[0]


def gather_small(mine, count):
    middle = mine.shape[0] // 2
    a, b = mine[:middle], mine[middle:]
    b_x = permute(b, 2, count)
    a_z = {s: permute(a, 4 * s, count) for s in (3, 2, 1)}
    b_pair = jnp.stack([b, b_x])
    b_z = {s: permute(b_pair, 4 * s, count) for s in (3, 2, 1)}
    near = jnp.stack([a, a_z[1], a_z[2], a_z[3]])
    far = permute(near, 2, count)
    rest = jnp.stack([b_pair, b_z[1], b_z[2], b_z[3]])
    upper, lower = pl.ds(0, middle), pl.ds(middle, middle)
    everything = slice(None)
    parts, regions = [], []
    for x, part in ((0, near), (1, far)):
        for core in range(2):
            parts.append(permute(part, 1, count) if core else part)
            regions.append((core, everything, x, upper))
    for core in range(2):
        parts.append(permute(rest, 1, count) if core else rest)
        regions.append((core, everything, everything, lower))
    return parts, regions


def shards(
    count, blocks, first_block, second_block, slot_counts, ket_first, ket_second, coefficients, mo_index
):
    me = lax.axis_index("pan").astype(jnp.int32)
    core = me % 2
    me_array = me.reshape(1)
    capacity, kp, pair = blocks.shape
    kh = kp // 2
    own_ao, nmo = coefficients.shape
    swap = functools.partial(permute, mask=1, count=count)

    numbers = jnp.concatenate([first_block, second_block, slot_counts])
    other_numbers = swap(numbers)
    picks = (mo_index[:, None] == jnp.arange(nmo, dtype=jnp.int32)[None, :]).astype(BF)
    mine = lax.dot_general(
        picks, coefficients, (((1,), (1,)), ((), ())), preferred_element_type=F32
    ).astype(BF)
    orbitals = mine.shape[0]

    small = count == 16 and own_ao % 16 == 0
    if small:
        mine = jnp.pad(mine, ((0, 0), (0, -own_ao % LANES)))
        parts, regions = gather_small(mine, count)

        def locate(row, me):
            away = (row // own_ao) ^ me
            return away & 1, away >> 2, (away >> 1) & 1, lax.rem(row, own_ao)
    else:
        parts = [lax.all_gather(mine, "pan", axis=1, tiled=True)]
        regions = [(0, 0, 0)]

        def locate(row, me):
            return 0, 0, 0, row

    leaving = lax.dynamic_slice_in_dim(after(blocks, mine), (1 - core) * kh, kh, axis=1)
    other = swap(leaving)
    bra = functools.partial(
        bra_transform, regions, locate, parts, blocks, other, (numbers, other_numbers), me_array
    )
    table = ket_table(regions, locate, parts, ket_first, ket_second, me_array, orbitals)

    if small:
        my_x = (me // 2) % 2
        chunk, side = orbitals // 8, kh // 2
        pieces = ((3, 0, side), (2, 0, side), (3, side, kh), (2, side, kh), (1, 0, kh), (0, 0, kh))
        first = bra((1 - my_x).reshape(1), chunk, 4, pieces, BF)
        arrived = [permute(piece, 2, count) for piece in first]
        kept = list(bra(my_x.reshape(1), chunk, 4, pieces, BF))
        whole = []
        for n in range(2):
            three = permute(added(kept[2 * n], arrived[2 * n]), 4, count)
            if n == 0:
                kept[3] = after(kept[3], table)
            whole.append(
                permute(added(kept[2 * n + 1], arrived[2 * n + 1], three), 8, count)
            )
        one = permute(added(kept[4], arrived[4]), 4, count)
        done = added(kept[5], arrived[5], one, jnp.concatenate(whole, axis=1))
    else:
        (partial,) = bra(jnp.zeros((1,), jnp.int32), orbitals, 1, ((0, 0, kh),), F32)
        sides = [list(range(c, count, 2)) for c in range(2)]
        done = lax.psum_scatter(
            partial, "pan", scatter_dimension=0, tiled=True, axis_index_groups=sides
        ).astype(BF)
    rows = done.shape[0] // 2
    keep = lax.dynamic_slice_in_dim(done, core * rows, rows, axis=0)
    give = lax.dynamic_slice_in_dim(done, (1 - core) * rows, rows, axis=0)
    half_rounded = jnp.concatenate([keep, swap(give)], axis=1)
    return lax.dot_general(
        half_rounded, table, (((1,), (1,)), ((), ())), preferred_element_type=F32
    )


def solution(mesh):
    placed = (
        P(("grp", "pan"), None, None),
        P(("grp", "pan")),
        P(("grp", "pan")),
        P(("grp", "pan")),
        P("grp"),
        P("grp"),
        P(("grp", "pan"), None),
        P("grp"),
    )
    return jax.shard_map(
        functools.partial(shards, mesh.shape["pan"]),
        mesh=mesh,
        in_specs=placed,
        out_specs=P(("grp", "pan"), None),
        check_vma=False,
    )
```

```python
import functools

import jax
import jax.numpy as jnp
from jax import lax
from jax.experimental import pallas as pl
from jax.experimental.pallas import tpu as pltpu
from jax.sharding import PartitionSpec as P

GROUP = 32
STEP = 8
LANES = 128
BF = jnp.bfloat16
F32 = jnp.float32
VMEM_LIMIT = 59 * 2**20


def spread(kind):
    row = lax.broadcasted_iota(jnp.int32, (LANES, LANES), 0)
    col = lax.broadcasted_iota(jnp.int32, (LANES, LANES), 1)
    source = col // 8 if kind == "a" else col % 8
    return (row == source).astype(F32).astype(BF)


def table_piece(table, place, target):
    core, z, x, lane = place
    inside = lane & (LANES - 1)
    start = pl.multiple_of(lane - inside, LANES)
    piece = table[core, z, x, :, pl.ds(start, LANES)].astype(F32)
    return pltpu.roll(piece, (target - inside) & (LANES - 1), 1)


def load_table(regions, parts, table, sems):
    return [
        pltpu.make_async_copy(part, table.at[region], sems.at[n])
        for n, (region, part) in enumerate(zip(regions, parts))
    ]


def bra_kernel(regions, locate, chunk, pieces, me_ref, mine, theirs, *refs):
    parts, refs = refs[: len(regions)], refs[len(regions) :]
    own, other = refs[:2]
    outs = refs[2 : 2 + len(pieces)]
    table, blk, picked, wide, half, second, ready, table_sems, block_sems, out_sems = refs[
        2 + len(pieces) :
    ]
    orbitals = second.shape[1]
    capacity = own.shape[0]
    kh = blk.shape[1]
    me = me_ref[0]
    own_live, other_live = mine[2 * capacity], theirs[2 * capacity]
    k_start = pl.multiple_of((me & 1) * kh, LANES)
    live = own_live + other_live

    copies = load_table(regions, parts, table, table_sems)
    for copy in copies:
        copy.start()

    def start_own(n, carry):
        pltpu.make_async_copy(
            own.at[n, pl.ds(k_start, kh)], blk.at[n], block_sems.at[n // STEP]
        ).start()
        return carry

    def start_other(n, carry):
        pltpu.make_async_copy(
            other.at[n - own_live], blk.at[n], block_sems.at[n // STEP]
        ).start()
        return carry

    lax.fori_loop(0, own_live, start_own, 0)
    lax.fori_loop(own_live, live, start_other, 0)
    lanes = lax.broadcasted_iota(jnp.int32, (8, LANES), 1)
    diagonal = (lanes % 8 == lax.broadcasted_iota(jnp.int32, (8, LANES), 0)).astype(F32)
    empty = jnp.zeros((8, LANES), F32)
    spread_a = spread("a")
    groups = (live + GROUP - 1) // GROUP
    steps = (live + STEP - 1) // STEP
    second[...] = jnp.zeros_like(second)

    def number(n, column):
        ours = mine[column * capacity + jnp.minimum(n, own_live - 1)]
        partners = theirs[column * capacity + jnp.maximum(n - own_live, 0)]
        return jnp.where(n < own_live, ours, partners)

    for copy in copies:
        copy.wait()

    def do_step(o, carry):
        start = o * STEP

        def wait_one(n, carry):
            pltpu.make_async_copy(other.at[0], blk.at[n], block_sems.at[o]).wait()
            return carry

        lax.fori_loop(start, jnp.minimum(start + STEP, live), wait_one, 0)
        slots = [jnp.minimum(start + u, live - 1) for u in range(STEP)]
        for u, n in enumerate(slots):
            piece = table_piece(table, locate(number(n, 0) * 2, me), 0)
            picked[u * orbitals : (u + 1) * orbitals] = piece.astype(BF)
        wide[...] = jnp.dot(picked[...], spread_a, preferred_element_type=F32)

        cover = 8 * STEP
        parity = o & (LANES // cover - 1)
        wanted = lax.broadcasted_iota(jnp.int32, (orbitals, LANES), 1)
        place = (wanted % cover) // 8
        merged = jnp.zeros((orbitals, LANES), F32)
        for u, n in enumerate(slots):
            where = locate(number(n, 1), me)
            piece = table_piece(table, where, parity * cover + 8 * u)
            merged = jnp.where(place == u, piece, merged)
        keep = (wanted // cover == parity) & (start + place < live)
        at = o // (LANES // cover)
        second[at] = jnp.where(keep, merged, second[at])

        for p in range(STEP // 2):
            rows = []
            for i in range(orbitals):
                x, y = (
                    jnp.broadcast_to(wide[u * orbitals + i : u * orbitals + i + 1, :], (8, LANES))
                    * diagonal
                    for u in (2 * p, 2 * p + 1)
                )
                rows.append(jnp.concatenate([x, empty], axis=1))
                rows.append(jnp.concatenate([empty, y], axis=1))
            factor = jnp.concatenate(rows, axis=0).astype(BF)
            data = jnp.concatenate([blk[slots[2 * p]], blk[slots[2 * p + 1]]], axis=1)
            result = lax.dot_general(
                factor, data, (((1,), (1,)), ((), ())), preferred_element_type=F32
            )
            at = pl.multiple_of(o * cover + 16 * p, 16)
            half[:, pl.ds(at, 16), :] = result.astype(BF).reshape(orbitals, 16, kh)
        return carry

    lax.fori_loop(0, steps, do_step, 0)

    def clear(o, carry):
        at = pl.multiple_of(o * 8 * STEP, 8 * STEP)
        half[:, pl.ds(at, 8 * STEP), :] = jnp.zeros((orbitals, 8 * STEP, kh), BF)
        return carry

    lax.fori_loop(steps, groups * (GROUP // STEP), clear, 0)

    def leave(n):
        s, low, high = pieces[n]
        return pltpu.make_async_copy(
            ready.at[s, :, pl.ds(low, high - low)], outs[n], out_sems.at[n]
        )

    def finish(count):
        weights = jnp.concatenate([second[n] for n in range(2 * count)], axis=1).astype(BF)
        for s in dict.fromkeys(piece[0] for piece in pieces):
            first = 0
            if len(pieces) > 1:
                first = ((me >> 2) ^ (s & 3)) * 2 * chunk + (((me >> 1) & 1) ^ (1 - (s >> 2))) * chunk
            for r in range(chunk):
                piece = half[first + r, 0 : 8 * GROUP * count, :]
                ready[s, r * orbitals : (r + 1) * orbitals, :] = jnp.dot(
                    weights, piece, preferred_element_type=F32
                ).astype(ready.dtype)
            for n in range(len(pieces)):
                if pieces[n][0] == s:
                    leave(n).start()

    for count in range(1, half.shape[1] // (8 * GROUP) + 1):
        pl.when(groups == count)(functools.partial(finish, count))
    for n in range(len(pieces)):
        leave(n).wait()


def bra_transform(regions, locate, parts, own, other, numbers, me, orbitals, chunk, pieces, kind):
    capacity, kp, pair = own.shape
    kh = other.shape[1]
    groups = -(-2 * capacity // GROUP)
    rows = chunk * orbitals
    hbm = pl.BlockSpec(memory_space=pltpu.HBM)
    return pl.pallas_call(
        functools.partial(bra_kernel, regions, locate, chunk, pieces),
        out_shape=[jax.ShapeDtypeStruct((rows, high - low), kind) for _, low, high in pieces],
        grid_spec=pltpu.PrefetchScalarGridSpec(
            num_scalar_prefetch=3,
            grid=(),
            in_specs=[hbm] * (len(parts) + 2),
            out_specs=[hbm] * len(pieces),
            scratch_shapes=[
                pltpu.VMEM(table_shape(parts, orbitals), BF),
                pltpu.VMEM((2 * capacity, kh, pair), BF),
                pltpu.VMEM((STEP * orbitals, LANES), BF),
                pltpu.VMEM((STEP * orbitals, LANES), F32),
                pltpu.VMEM((orbitals, 8 * GROUP * groups, kh), BF),
                pltpu.VMEM((2 * groups, orbitals, LANES), F32),
                pltpu.VMEM((orbitals // chunk, rows, kh), kind),
                pltpu.SemaphoreType.DMA((len(parts),)),
                pltpu.SemaphoreType.DMA((-(-2 * capacity // STEP),)),
                pltpu.SemaphoreType.DMA((len(pieces),)),
            ],
        ),
        compiler_params=pltpu.CompilerParams(vmem_limit_bytes=VMEM_LIMIT),
        cost_estimate=pl.CostEstimate(
            flops=4 * capacity * 8 * orbitals * pair * kh, bytes_accessed=8 * 2**20, transcendentals=0
        ),
        name="bra_transform",
    )(me, *numbers, *parts, own, other)


def leaving_kernel(me_ref, first, blocks, out, sem):
    kh = out.shape[1]
    start = pl.multiple_of((1 - (me_ref[0] & 1)) * kh, LANES)
    copy = pltpu.make_async_copy(blocks.at[:, pl.ds(start, kh)], out, sem)
    copy.start()
    copy.wait()


def leaving_half(me, first, blocks):
    capacity, kp, pair = blocks.shape
    hbm = pl.BlockSpec(memory_space=pltpu.HBM)
    return pl.pallas_call(
        leaving_kernel,
        out_shape=jax.ShapeDtypeStruct((capacity, kp // 2, pair), BF),
        grid_spec=pltpu.PrefetchScalarGridSpec(
            num_scalar_prefetch=1,
            grid=(),
            in_specs=[hbm, hbm],
            out_specs=hbm,
            scratch_shapes=[pltpu.SemaphoreType.DMA(())],
        ),
        compiler_params=pltpu.CompilerParams(vmem_limit_bytes=VMEM_LIMIT),
        name="leaving_half",
    )(me, first, blocks)


def table_shape(parts, orbitals):
    if len(parts) == 1:
        return (1, 1, 1, orbitals, parts[0].shape[-1])
    return (2, 4, 2, orbitals, parts[0].shape[-1])


def ket_kernel(regions, locate, me_ref, firsts, seconds, before, *refs):
    parts = refs[: len(regions)]
    out, table, first, sems = refs[len(regions) :]
    orbitals = first.shape[0]
    me = me_ref[0]
    copies = load_table(regions, parts, table, sems)
    for copy in copies:
        copy.start()
    for copy in copies:
        copy.wait()
    count = out.shape[1] // LANES
    for n in range(count):
        kb = lax.rem(n + lax.rem(me, 2) * (count // 2), count)
        piece = table_piece(table, locate(firsts[kb] * 2, me), 0)
        first[...] = jnp.dot(piece.astype(BF), spread("a"), preferred_element_type=F32)
        piece = table_piece(table, locate(seconds[kb], me), 0)
        last = jnp.dot(piece.astype(BF), spread("b"), preferred_element_type=F32)
        for r in range(orbitals):
            row = jnp.broadcast_to(first[r : r + 1, :], (orbitals, LANES))
            rows = pl.ds(r * orbitals, orbitals)
            out[rows, n * LANES : (n + 1) * LANES] = (row * last).astype(BF)


def ket_table(regions, locate, parts, ket_first, ket_second, me, orbitals, before):
    shape = (orbitals * orbitals, ket_first.shape[0] * LANES)
    return pl.pallas_call(
        functools.partial(ket_kernel, regions, locate),
        out_shape=jax.ShapeDtypeStruct(shape, BF),
        grid_spec=pltpu.PrefetchScalarGridSpec(
            num_scalar_prefetch=3,
            grid=(),
            in_specs=[pl.BlockSpec(memory_space=pltpu.HBM)] * (1 + len(parts)),
            out_specs=pl.BlockSpec(memory_space=pltpu.VMEM),
            scratch_shapes=[
                pltpu.VMEM(table_shape(parts, orbitals), BF),
                pltpu.VMEM((orbitals, LANES), F32),
                pltpu.SemaphoreType.DMA((len(parts),)),
            ],
        ),
        compiler_params=pltpu.CompilerParams(vmem_limit_bytes=24 * 2**20),
        cost_estimate=pl.CostEstimate(
            flops=2 * 2**20, bytes_accessed=6 * 2**20, transcendentals=0
        ),
        name="ket_table",
    )(me, ket_first, ket_second, before, *parts)


def last_kernel(own, other, table, out):
    kh = own.shape[1]
    contract = (((1,), (1,)), ((), ()))
    out[...] = lax.dot_general(
        own[...], table[:, :kh], contract, preferred_element_type=F32
    ) + lax.dot_general(other[...], table[:, kh:], contract, preferred_element_type=F32)


def last_step(own, other, table):
    rows, kh = own.shape
    columns = table.shape[0]
    tile = 512
    return pl.pallas_call(
        last_kernel,
        out_shape=jax.ShapeDtypeStruct((rows, columns), F32),
        grid=(columns // tile,),
        in_specs=[
            pl.BlockSpec((rows, kh), lambda n: (0, 0)),
            pl.BlockSpec((rows, kh), lambda n: (0, 0)),
            pl.BlockSpec((tile, 2 * kh), lambda n: (n, 0)),
        ],
        out_specs=pl.BlockSpec((rows, tile), lambda n: (0, n)),
        name="last_step",
    )(own, other, table)


def permute(array, mask, count):
    return lax.ppermute(array, "pan", [(i, i ^ mask) for i in range(count)])


def added(*arrays):
    result = arrays[0].astype(F32)
    for array in arrays[1:]:
        result = result + array.astype(F32)
    return result.astype(BF)


def gather_small(mine, nothing, count):
    middle = mine.shape[0] // 2
    a, b = mine[:middle], mine[middle:]
    b_x = permute(b, 2, count)
    a_z = {s: permute(a, 4 * s, count) for s in (3, 2, 1)}
    b_pair = jnp.stack([b, b_x])
    b_z = {s: permute(b_pair, 4 * s, count) for s in (3, 2, 1)}
    near = jnp.stack([a, a_z[1], a_z[2], a_z[3]]) + nothing
    far = permute(near, 2, count)
    rest = jnp.stack([b_pair, b_z[1], b_z[2], b_z[3]])
    upper, lower = pl.ds(0, middle), pl.ds(middle, middle)
    everything = slice(None)
    parts, regions = [], []
    for x, part in ((0, near), (1, far)):
        for core in range(2):
            parts.append(permute(part, 1, count) if core else part)
            regions.append((core, everything, x, upper))
    for core in range(2):
        parts.append(permute(rest, 1, count) if core else rest)
        regions.append((core, everything, everything, lower))
    return parts, regions


def shards(
    count, blocks, first_block, second_block, slot_counts, ket_first, ket_second, coefficients, mo_index
):
    me = lax.axis_index("pan").astype(jnp.int32)
    core = me % 2
    me_array = me.reshape(1)
    capacity, kp, pair = blocks.shape
    kh = kp // 2
    own_ao, nmo = coefficients.shape
    swap = functools.partial(permute, mask=1, count=count)

    numbers = jnp.concatenate([first_block, second_block, slot_counts])
    other_numbers = swap(numbers)
    picks = (mo_index[:, None] == jnp.arange(nmo, dtype=jnp.int32)[None, :]).astype(BF)
    mine = lax.dot_general(
        picks, coefficients, (((1,), (1,)), ((), ())), preferred_element_type=F32
    ).astype(BF)
    orbitals = mine.shape[0]

    units = own_ao // 8
    factor = -(-(2**20) // max(units, 1))
    leaving = leaving_half(me_array, mine, blocks)
    other = swap(leaving)

    small = count == 16 and own_ao % 16 == 0
    if small:
        nothing = (other_numbers[0] < 0).astype(BF)
        mine = jnp.pad(mine, ((0, 0), (0, -own_ao % LANES)))
        parts, regions = gather_small(mine, nothing, count)

        def locate(unit, me):
            owner = (unit * factor) >> 20
            away = owner ^ me
            return away & 1, away >> 2, (away >> 1) & 1, (unit - owner * units) * 8
    else:
        parts = [lax.all_gather(mine, "pan", axis=1, tiled=True)]
        regions = [(0, 0, 0)]

        def locate(unit, me):
            return 0, 0, 0, unit * 8

    bra = functools.partial(
        bra_transform, regions, locate, parts, blocks, other, (numbers, other_numbers), me_array
    )
    ket = functools.partial(
        ket_table, regions, locate, parts, ket_first, ket_second, me_array, orbitals
    )

    if small:
        chunk, side = orbitals // 8, kh // 2
        low, high = slice(0, side), slice(side, kh)
        pieces = ((3, 0, side), (2, 0, side), (3, side, kh), (2, side, kh), (1, 0, kh), (0, 0, kh))
        pieces += tuple((s, 0, kh) for s in (7, 6, 5, 4))
        partial = bra(orbitals, chunk, pieces, BF)
        arrived = [permute(piece, 2, count) for piece in partial[:6]]
        kept = partial[6:]
        three = permute(added(kept[0][:, low], arrived[0]), 4, count)
        left = permute(added(kept[1][:, low], arrived[1], three), 8, count)
        table = ket(three)
        nothing = (table[0, 0] != table[0, 0]).astype(F32)
        three = permute(added(kept[0][:, high], arrived[2]), 4, count)
        right = permute(added(kept[1][:, high], arrived[3], three, nothing), 8, count)
        one = permute(added(kept[2], arrived[4]), 4, count)
        done = added(kept[3], arrived[5], one, jnp.concatenate([left, right], axis=1))
    else:
        (partial,) = bra(orbitals, orbitals, ((0, 0, kh),), F32)
        sides = [list(range(c, count, 2)) for c in range(2)]
        done = lax.psum_scatter(
            partial, "pan", scatter_dimension=0, tiled=True, axis_index_groups=sides
        ).astype(BF)
        table = ket(done)
    rows = done.shape[0] // 2
    keep = lax.dynamic_slice_in_dim(done, core * rows, rows, axis=0)
    give = lax.dynamic_slice_in_dim(done, (1 - core) * rows, rows, axis=0)
    return last_step(keep, swap(give), table)


def solution(mesh):
    placed = (
        P(("grp", "pan"), None, None),
        P(("grp", "pan")),
        P(("grp", "pan")),
        P(("grp", "pan")),
        P("grp"),
        P("grp"),
        P(("grp", "pan"), None),
        P("grp"),
    )
    return jax.shard_map(
        functools.partial(shards, mesh.shape["pan"]),
        mesh=mesh,
        in_specs=placed,
        out_specs=P(("grp", "pan"), None),
        check_vma=False,
    )
```

```python
import functools

import jax
import jax.numpy as jnp
from jax import lax
from jax.experimental import pallas as pl
from jax.experimental.pallas import tpu as pltpu
from jax.sharding import PartitionSpec as P

GROUP = 32
STEP = 8
LANES = 128
BF = jnp.bfloat16
F32 = jnp.float32
VMEM_LIMIT = 59 * 2**20


def spread(kind):
    row = lax.broadcasted_iota(jnp.int32, (LANES, LANES), 0)
    col = lax.broadcasted_iota(jnp.int32, (LANES, LANES), 1)
    source = col // 8 if kind == "a" else col % 8
    return (row == source).astype(F32).astype(BF)


def table_piece(table, place, target):
    core, z, x, lane = place
    inside = lane & (LANES - 1)
    start = pl.multiple_of(lane - inside, LANES)
    piece = table[core, z, x, :, pl.ds(start, LANES)].astype(F32)
    return pltpu.roll(piece, (target - inside) & (LANES - 1), 1)


def load_table(regions, parts, table, sems):
    return [
        pltpu.make_async_copy(part, table.at[region], sems.at[n])
        for n, (region, part) in enumerate(zip(regions, parts))
    ]


def bra_kernel(regions, locate, chunk, pieces, me_ref, mine, theirs, firsts, seconds, *refs):
    parts, refs = refs[: len(regions)], refs[len(regions) :]
    own, other = refs[:2]
    outs, ket = refs[2 : 2 + len(pieces)], refs[2 + len(pieces)]
    table, blk, picked, wide, half, second, ready, table_sems, block_sems, out_sems = refs[
        3 + len(pieces) :
    ]
    orbitals = second.shape[1]
    capacity = own.shape[0]
    kh = blk.shape[1]
    me = me_ref[0]
    own_live, other_live = mine[2 * capacity], theirs[2 * capacity]
    k_start = pl.multiple_of((me & 1) * kh, LANES)
    live = own_live + other_live

    copies = load_table(regions, parts, table, table_sems)
    for copy in copies:
        copy.start()

    def start_own(n, carry):
        pltpu.make_async_copy(
            own.at[n, pl.ds(k_start, kh)], blk.at[n], block_sems.at[n // STEP]
        ).start()
        return carry

    def start_other(n, carry):
        pltpu.make_async_copy(
            other.at[n - own_live, pl.ds(k_start, kh)], blk.at[n], block_sems.at[n // STEP]
        ).start()
        return carry

    lax.fori_loop(0, own_live, start_own, 0)
    lax.fori_loop(own_live, live, start_other, 0)
    lanes = lax.broadcasted_iota(jnp.int32, (8, LANES), 1)
    diagonal = (lanes % 8 == lax.broadcasted_iota(jnp.int32, (8, LANES), 0)).astype(F32)
    empty = jnp.zeros((8, LANES), F32)
    spread_a = spread("a")
    groups = (live + GROUP - 1) // GROUP
    steps = (live + STEP - 1) // STEP
    second[...] = jnp.zeros_like(second)

    def number(n, column):
        ours = mine[column * capacity + jnp.minimum(n, own_live - 1)]
        partners = theirs[column * capacity + jnp.maximum(n - own_live, 0)]
        return jnp.where(n < own_live, ours, partners)

    for copy in copies:
        copy.wait()

    count = ket.shape[1]
    for n in range(count):
        kb = (n + (me & 1) * (count // 2)) & (count - 1)
        piece = table_piece(table, locate(firsts[kb] * 2, me), 0)
        ket[0, n] = jnp.dot(piece.astype(BF), spread_a, preferred_element_type=F32)
        piece = table_piece(table, locate(seconds[kb], me), 0)
        ket[1, n] = jnp.dot(piece.astype(BF), spread("b"), preferred_element_type=F32)

    def do_step(o, carry):
        start = o * STEP

        def wait_one(n, carry):
            pltpu.make_async_copy(
                own.at[0, pl.ds(k_start, kh)], blk.at[n], block_sems.at[o]
            ).wait()
            return carry

        lax.fori_loop(start, jnp.minimum(start + STEP, live), wait_one, 0)
        slots = [jnp.minimum(start + u, live - 1) for u in range(STEP)]
        for u, n in enumerate(slots):
            piece = table_piece(table, locate(number(n, 0) * 2, me), 0)
            picked[u * orbitals : (u + 1) * orbitals] = piece.astype(BF)
        wide[...] = jnp.dot(picked[...], spread_a, preferred_element_type=F32)

        cover = 8 * STEP
        parity = o & (LANES // cover - 1)
        wanted = lax.broadcasted_iota(jnp.int32, (orbitals, LANES), 1)
        place = (wanted % cover) // 8
        merged = jnp.zeros((orbitals, LANES), F32)
        for u, n in enumerate(slots):
            where = locate(number(n, 1), me)
            piece = table_piece(table, where, parity * cover + 8 * u)
            merged = jnp.where(place == u, piece, merged)
        keep = (wanted // cover == parity) & (start + place < live)
        at = o // (LANES // cover)
        second[at] = jnp.where(keep, merged, second[at])

        for p in range(STEP // 2):
            rows = []
            for i in range(orbitals):
                x, y = (
                    jnp.broadcast_to(wide[u * orbitals + i : u * orbitals + i + 1, :], (8, LANES))
                    * diagonal
                    for u in (2 * p, 2 * p + 1)
                )
                rows.append(jnp.concatenate([x, empty], axis=1))
                rows.append(jnp.concatenate([empty, y], axis=1))
            factor = jnp.concatenate(rows, axis=0).astype(BF)
            data = jnp.concatenate([blk[slots[2 * p]], blk[slots[2 * p + 1]]], axis=1)
            result = lax.dot_general(
                factor, data, (((1,), (1,)), ((), ())), preferred_element_type=F32
            )
            at = pl.multiple_of(o * cover + 16 * p, 16)
            half[:, pl.ds(at, 16), :] = result.astype(BF).reshape(orbitals, 16, kh)
        return carry

    lax.fori_loop(0, steps, do_step, 0)

    def clear(o, carry):
        at = pl.multiple_of(o * 8 * STEP, 8 * STEP)
        half[:, pl.ds(at, 8 * STEP), :] = jnp.zeros((orbitals, 8 * STEP, kh), BF)
        return carry

    lax.fori_loop(steps, groups * (GROUP // STEP), clear, 0)

    def leave(n):
        s, low, high = pieces[n]
        return pltpu.make_async_copy(
            ready.at[s, :, pl.ds(low, high - low)], outs[n], out_sems.at[n]
        )

    def finish(count):
        weights = jnp.concatenate([second[n] for n in range(2 * count)], axis=1).astype(BF)
        for s in dict.fromkeys(piece[0] for piece in pieces):
            first = 0
            if len(pieces) > 1:
                first = ((me >> 2) ^ (s & 3)) * 2 * chunk + (((me >> 1) & 1) ^ (1 - (s >> 2))) * chunk
            for r in range(chunk):
                piece = half[first + r, 0 : 8 * GROUP * count, :]
                ready[s, r * orbitals : (r + 1) * orbitals, :] = jnp.dot(
                    weights, piece, preferred_element_type=F32
                ).astype(ready.dtype)
            for n in range(len(pieces)):
                if pieces[n][0] == s:
                    leave(n).start()

    for count in range(1, half.shape[1] // (8 * GROUP) + 1):
        pl.when(groups == count)(functools.partial(finish, count))
    for n in range(len(pieces)):
        leave(n).wait()


def bra_transform(
    regions, locate, parts, own, other, numbers, ket_numbers, me, orbitals, chunk, pieces, kind
):
    capacity, kp, pair = own.shape
    kh = kp // 2
    groups = -(-2 * capacity // GROUP)
    rows = chunk * orbitals
    hbm = pl.BlockSpec(memory_space=pltpu.HBM)
    return pl.pallas_call(
        functools.partial(bra_kernel, regions, locate, chunk, pieces),
        out_shape=[jax.ShapeDtypeStruct((rows, high - low), kind) for _, low, high in pieces]
        + [jax.ShapeDtypeStruct((2, kp // LANES, orbitals, LANES), F32)],
        grid_spec=pltpu.PrefetchScalarGridSpec(
            num_scalar_prefetch=5,
            grid=(),
            in_specs=[hbm] * (len(parts) + 2),
            out_specs=[hbm] * len(pieces) + [pl.BlockSpec(memory_space=pltpu.VMEM)],
            scratch_shapes=[
                pltpu.VMEM(table_shape(parts, orbitals), BF),
                pltpu.VMEM((2 * capacity, kh, pair), BF),
                pltpu.VMEM((STEP * orbitals, LANES), BF),
                pltpu.VMEM((STEP * orbitals, LANES), F32),
                pltpu.VMEM((orbitals, 8 * GROUP * groups, kh), BF),
                pltpu.VMEM((2 * groups, orbitals, LANES), F32),
                pltpu.VMEM((orbitals // chunk, rows, kh), kind),
                pltpu.SemaphoreType.DMA((len(parts),)),
                pltpu.SemaphoreType.DMA((-(-2 * capacity // STEP),)),
                pltpu.SemaphoreType.DMA((len(pieces),)),
            ],
        ),
        compiler_params=pltpu.CompilerParams(vmem_limit_bytes=VMEM_LIMIT),
        cost_estimate=pl.CostEstimate(
            flops=4 * capacity * 8 * orbitals * pair * kh, bytes_accessed=8 * 2**20, transcendentals=0
        ),
        name="bra_transform",
    )(me, *numbers, *ket_numbers, *parts, own, other)


def table_shape(parts, orbitals):
    if len(parts) == 1:
        return (1, 1, 1, orbitals, parts[0].shape[-1])
    return (2, 4, 2, orbitals, parts[0].shape[-1])


def last_kernel(own, other, ket, out, tiles, results, sems):
    count, orbitals = ket.shape[1:3]
    group = tiles.shape[1] // orbitals
    half_rounded = jnp.concatenate([own[...], other[...]], axis=1)
    copies = []
    for t in range(orbitals // group):
        tile = tiles.at[t % 2]
        for n in range(count):
            last = ket[1, n]
            for r in range(group):
                row = jnp.broadcast_to(ket[0, n, t * group + r : t * group + r + 1, :], last.shape)
                tile[r * orbitals : (r + 1) * orbitals, n * LANES : (n + 1) * LANES] = (
                    row * last
                ).astype(BF)
        results[t] = lax.dot_general(
            half_rounded, tile[...], (((1,), (1,)), ((), ())), preferred_element_type=F32
        )
        columns = group * orbitals
        copies.append(
            pltpu.make_async_copy(
                results.at[t], out.at[:, pl.ds(t * columns, columns)], sems.at[t]
            )
        )
        copies[-1].start()
    for copy in copies:
        copy.wait()


def last_step(own, other, ket):
    rows, kh = own.shape
    orbitals = ket.shape[2]
    group = 8
    count = orbitals // group
    vmem = pl.BlockSpec(memory_space=pltpu.VMEM)
    return pl.pallas_call(
        last_kernel,
        out_shape=jax.ShapeDtypeStruct((rows, orbitals * orbitals), F32),
        in_specs=[vmem] * 3,
        out_specs=pl.BlockSpec(memory_space=pltpu.HBM),
        scratch_shapes=[
            pltpu.VMEM((2, group * orbitals, 2 * kh), BF),
            pltpu.VMEM((count, rows, group * orbitals), F32),
            pltpu.SemaphoreType.DMA((count,)),
        ],
        compiler_params=pltpu.CompilerParams(vmem_limit_bytes=16 * 2**20),
        name="last_step",
    )(own, other, ket)


def permute(array, mask, count):
    return lax.ppermute(array, "pan", [(i, i ^ mask) for i in range(count)])


def added(*arrays):
    result = arrays[0].astype(F32)
    for array in arrays[1:]:
        result = result + array.astype(F32)
    return result.astype(BF)


def gather_small(mine, nothing, count):
    middle = mine.shape[0] // 2
    a, b = mine[:middle], mine[middle:]
    b_x = permute(b, 2, count)
    a_z = {s: permute(a, 4 * s, count) for s in (3, 2, 1)}
    b_pair = jnp.stack([b, b_x])
    b_z = {s: permute(b_pair, 4 * s, count) for s in (3, 2, 1)}
    near = jnp.stack([a, a_z[1], a_z[2], a_z[3]]) + nothing
    far = permute(near, 2, count)
    rest = jnp.stack([b_pair, b_z[1], b_z[2], b_z[3]])
    upper, lower = pl.ds(0, middle), pl.ds(middle, middle)
    everything = slice(None)
    parts, regions = [], []
    for x, part in ((0, near), (1, far)):
        for core in range(2):
            parts.append(permute(part, 1, count) if core else part)
            regions.append((core, everything, x, upper))
    for core in range(2):
        parts.append(permute(rest, 1, count) if core else rest)
        regions.append((core, everything, everything, lower))
    return parts, regions


def shards(
    count, blocks, first_block, second_block, slot_counts, ket_first, ket_second, coefficients, mo_index
):
    me = lax.axis_index("pan").astype(jnp.int32)
    core = me % 2
    me_array = me.reshape(1)
    capacity, kp, pair = blocks.shape
    kh = kp // 2
    own_ao, nmo = coefficients.shape
    swap = functools.partial(permute, mask=1, count=count)

    numbers = jnp.concatenate([first_block, second_block, slot_counts])
    other_numbers = swap(numbers)
    picks = (mo_index[:, None] == jnp.arange(nmo, dtype=jnp.int32)[None, :]).astype(BF)
    mine = lax.dot_general(
        picks, coefficients, (((1,), (1,)), ((), ())), preferred_element_type=F32
    ).astype(BF)
    orbitals = mine.shape[0]

    units = own_ao // 8
    factor = -(-(2**20) // max(units, 1))
    other = swap(blocks)

    small = count == 16 and own_ao % 16 == 0
    if small:
        nothing = (other_numbers[0] < 0).astype(BF)
        mine = jnp.pad(mine, ((0, 0), (0, -own_ao % LANES)))
        parts, regions = gather_small(mine, nothing, count)

        def locate(unit, me):
            owner = (unit * factor) >> 20
            away = owner ^ me
            return away & 1, away >> 2, (away >> 1) & 1, (unit - owner * units) * 8
    else:
        parts = [lax.all_gather(mine, "pan", axis=1, tiled=True)]
        regions = [(0, 0, 0)]

        def locate(unit, me):
            return 0, 0, 0, unit * 8

    bra = functools.partial(
        bra_transform,
        regions,
        locate,
        parts,
        blocks,
        other,
        (numbers, other_numbers),
        (ket_first, ket_second),
        me_array,
        orbitals,
    )

    if small:
        chunk, side = orbitals // 8, kh // 2
        order = ((3, 0, side), (2, 0, side), (3, side, kh), (2, side, kh), (1, 0, kh), (0, 0, kh))
        pieces = order + tuple((s + 4, a, b) for s, a, b in order)
        *partial, ket = bra(chunk, pieces, BF)
        arrived = [permute(piece, 2, count) for piece in partial[:6]]
        kept = partial[6:]
        whole = []
        for n in (0, 2):
            three = permute(added(kept[n], arrived[n]), 4, count)
            whole.append(permute(added(kept[n + 1], arrived[n + 1], three), 8, count))
        one = permute(added(kept[4], arrived[4]), 4, count)
        done = added(kept[5], arrived[5], one, jnp.concatenate(whole, axis=1))
    else:
        partial, ket = bra(orbitals, ((0, 0, kh),), F32)
        sides = [list(range(c, count, 2)) for c in range(2)]
        done = lax.psum_scatter(
            partial, "pan", scatter_dimension=0, tiled=True, axis_index_groups=sides
        ).astype(BF)
    rows = done.shape[0] // 2
    keep = lax.dynamic_slice_in_dim(done, core * rows, rows, axis=0)
    give = lax.dynamic_slice_in_dim(done, (1 - core) * rows, rows, axis=0)
    return last_step(keep, swap(give), ket)


def solution(mesh):
    placed = (
        P(("grp", "pan"), None, None),
        P(("grp", "pan")),
        P(("grp", "pan")),
        P(("grp", "pan")),
        P("grp"),
        P("grp"),
        P(("grp", "pan"), None),
        P("grp"),
    )
    return jax.shard_map(
        functools.partial(shards, mesh.shape["pan"]),
        mesh=mesh,
        in_specs=placed,
        out_specs=P(("grp", "pan"), None),
        check_vma=False,
    )
```

```python
import functools

import jax
import jax.numpy as jnp
from jax import lax
from jax.experimental import pallas as pl
from jax.experimental.pallas import tpu as pltpu
from jax.sharding import PartitionSpec as P

GROUP = 32
STEP = 8
LANES = 128
BF = jnp.bfloat16
F32 = jnp.float32
VMEM_LIMIT = 59 * 2**20


def spread(kind):
    row = lax.broadcasted_iota(jnp.int32, (LANES, LANES), 0)
    col = lax.broadcasted_iota(jnp.int32, (LANES, LANES), 1)
    source = col // 8 if kind == "a" else col % 8
    return (row == source).astype(F32).astype(BF)


def table_piece(table, place, target):
    core, z, x, lane = place
    inside = lane & (LANES - 1)
    start = pl.multiple_of(lane - inside, LANES)
    piece = table[core, z, x, :, pl.ds(start, LANES)].astype(F32)
    return pltpu.roll(piece, (target - inside) & (LANES - 1), 1)


def load_table(regions, parts, table, sems):
    return [
        pltpu.make_async_copy(part, table.at[region], sems.at[n])
        for n, (region, part) in enumerate(zip(regions, parts))
    ]


def bra_kernel(regions, locate, chunk, pieces, me_ref, mine, theirs, firsts, seconds, *refs):
    parts, refs = refs[: len(regions)], refs[len(regions) :]
    own, other = refs[:2]
    outs, ket = refs[2 : 2 + len(pieces)], refs[2 + len(pieces)]
    table, blk, picked, wide, half, second, ready, table_sems, block_sems, out_sems = refs[
        3 + len(pieces) :
    ]
    orbitals = second.shape[1]
    capacity = own.shape[0]
    kh = blk.shape[1]
    me = me_ref[0]
    own_live, other_live = mine[2 * capacity], theirs[2 * capacity]
    k_start = pl.multiple_of((me & 1) * kh, LANES)
    live = own_live + other_live

    copies = load_table(regions, parts, table, table_sems)
    for copy in copies:
        copy.start()

    def start_own(n, carry):
        pltpu.make_async_copy(
            own.at[n, pl.ds(k_start, kh)], blk.at[n], block_sems.at[n // STEP]
        ).start()
        return carry

    def start_other(n, carry):
        pltpu.make_async_copy(
            other.at[n - own_live, pl.ds(k_start, kh)], blk.at[n], block_sems.at[n // STEP]
        ).start()
        return carry

    lax.fori_loop(0, own_live, start_own, 0)
    lax.fori_loop(own_live, live, start_other, 0)
    lanes = lax.broadcasted_iota(jnp.int32, (8, LANES), 1)
    diagonal = (lanes % 8 == lax.broadcasted_iota(jnp.int32, (8, LANES), 0)).astype(F32)
    empty = jnp.zeros((8, LANES), F32)
    spread_a = spread("a")
    groups = (live + GROUP - 1) // GROUP
    steps = (live + STEP - 1) // STEP
    second[...] = jnp.zeros_like(second)

    def number(n, column):
        ours = mine[column * capacity + jnp.minimum(n, own_live - 1)]
        partners = theirs[column * capacity + jnp.maximum(n - own_live, 0)]
        return jnp.where(n < own_live, ours, partners)

    for copy in copies:
        copy.wait()

    count = ket.shape[1]
    for n in range(count):
        kb = (n + (me & 1) * (count // 2)) & (count - 1)
        piece = table_piece(table, locate(firsts[kb] * 2, me), 0)
        ket[0, n] = jnp.dot(piece.astype(BF), spread_a, preferred_element_type=F32)
        piece = table_piece(table, locate(seconds[kb], me), 0)
        ket[1, n] = jnp.dot(piece.astype(BF), spread("b"), preferred_element_type=F32)

    def do_step(o, carry):
        start = o * STEP

        def wait_one(n, carry):
            pltpu.make_async_copy(
                own.at[0, pl.ds(k_start, kh)], blk.at[n], block_sems.at[o]
            ).wait()
            return carry

        lax.fori_loop(start, jnp.minimum(start + STEP, live), wait_one, 0)
        slots = [jnp.minimum(start + u, live - 1) for u in range(STEP)]
        for u, n in enumerate(slots):
            piece = table_piece(table, locate(number(n, 0) * 2, me), 0)
            picked[u * orbitals : (u + 1) * orbitals] = piece.astype(BF)
        wide[...] = jnp.dot(picked[...], spread_a, preferred_element_type=F32)

        cover = 8 * STEP
        parity = o & (LANES // cover - 1)
        wanted = lax.broadcasted_iota(jnp.int32, (orbitals, LANES), 1)
        place = (wanted % cover) // 8
        merged = jnp.zeros((orbitals, LANES), F32)
        for u, n in enumerate(slots):
            where = locate(number(n, 1), me)
            piece = table_piece(table, where, parity * cover + 8 * u)
            merged = jnp.where(place == u, piece, merged)
        keep = (wanted // cover == parity) & (start + place < live)
        at = o // (LANES // cover)
        second[at] = jnp.where(keep, merged, second[at])

        for p in range(STEP // 2):
            rows = []
            for i in range(orbitals):
                x, y = (
                    jnp.broadcast_to(wide[u * orbitals + i : u * orbitals + i + 1, :], (8, LANES))
                    * diagonal
                    for u in (2 * p, 2 * p + 1)
                )
                rows.append(jnp.concatenate([x, empty], axis=1))
                rows.append(jnp.concatenate([empty, y], axis=1))
            factor = jnp.concatenate(rows, axis=0).astype(BF)
            data = jnp.concatenate([blk[slots[2 * p]], blk[slots[2 * p + 1]]], axis=1)
            result = lax.dot_general(
                factor, data, (((1,), (1,)), ((), ())), preferred_element_type=F32
            )
            at = pl.multiple_of(o * cover + 16 * p, 16)
            half[:, pl.ds(at, 16), :] = result.astype(BF).reshape(orbitals, 16, kh)
        return carry

    lax.fori_loop(0, steps, do_step, 0)

    def clear(o, carry):
        at = pl.multiple_of(o * 8 * STEP, 8 * STEP)
        half[:, pl.ds(at, 8 * STEP), :] = jnp.zeros((orbitals, 8 * STEP, kh), BF)
        return carry

    lax.fori_loop(steps, groups * (GROUP // STEP), clear, 0)

    def leave(n):
        s, low, high = pieces[n]
        return pltpu.make_async_copy(
            ready.at[s, :, pl.ds(low, high - low)], outs[n], out_sems.at[n]
        )

    def finish(count):
        weights = jnp.concatenate([second[n] for n in range(2 * count)], axis=1).astype(BF)
        for s in dict.fromkeys(piece[0] for piece in pieces):
            first = 0
            if len(pieces) > 1:
                first = ((me >> 2) ^ (s & 3)) * 2 * chunk + (((me >> 1) & 1) ^ (1 - (s >> 2))) * chunk
            here = [n for n in range(len(pieces)) if pieces[n][0] == s]
            for r in range(chunk):
                piece = half[first + r, 0 : 8 * GROUP * count, :]
                rows = slice(r * orbitals, (r + 1) * orbitals)
                result = jnp.dot(weights, piece, preferred_element_type=F32).astype(ready.dtype)
                if s < ready.shape[0]:
                    ready[s, rows, :] = result
                else:
                    for n in here:
                        outs[n][rows, :] = result[:, pieces[n][1] : pieces[n][2]]
            if s < ready.shape[0]:
                for n in here:
                    leave(n).start()

    for count in range(1, half.shape[1] // (8 * GROUP) + 1):
        pl.when(groups == count)(functools.partial(finish, count))
    for n in range(len(pieces)):
        if pieces[n][0] < ready.shape[0]:
            leave(n).wait()


def bra_transform(
    regions, locate, parts, own, other, numbers, ket_numbers, me, orbitals, chunk, pieces, kind
):
    capacity, kp, pair = own.shape
    kh = kp // 2
    groups = -(-2 * capacity // GROUP)
    rows = chunk * orbitals
    hbm = pl.BlockSpec(memory_space=pltpu.HBM)
    vmem = pl.BlockSpec(memory_space=pltpu.VMEM)
    leaving = max(1, orbitals // chunk // 2)
    return pl.pallas_call(
        functools.partial(bra_kernel, regions, locate, chunk, pieces),
        out_shape=[jax.ShapeDtypeStruct((rows, high - low), kind) for _, low, high in pieces]
        + [jax.ShapeDtypeStruct((2, kp // LANES, orbitals, LANES), F32)],
        grid_spec=pltpu.PrefetchScalarGridSpec(
            num_scalar_prefetch=5,
            grid=(),
            in_specs=[hbm] * (len(parts) + 2),
            out_specs=[hbm if s < leaving else vmem for s, _, _ in pieces] + [vmem],
            scratch_shapes=[
                pltpu.VMEM(table_shape(parts, orbitals), BF),
                pltpu.VMEM((2 * capacity, kh, pair), BF),
                pltpu.VMEM((STEP * orbitals, LANES), BF),
                pltpu.VMEM((STEP * orbitals, LANES), F32),
                pltpu.VMEM((orbitals, 8 * GROUP * groups, kh), BF),
                pltpu.VMEM((2 * groups, orbitals, LANES), F32),
                pltpu.VMEM((leaving, rows, kh), kind),
                pltpu.SemaphoreType.DMA((len(parts),)),
                pltpu.SemaphoreType.DMA((-(-2 * capacity // STEP),)),
                pltpu.SemaphoreType.DMA((len(pieces),)),
            ],
        ),
        compiler_params=pltpu.CompilerParams(vmem_limit_bytes=VMEM_LIMIT),
        cost_estimate=pl.CostEstimate(
            flops=4 * capacity * 8 * orbitals * pair * kh, bytes_accessed=8 * 2**20, transcendentals=0
        ),
        name="bra_transform",
    )(me, *numbers, *ket_numbers, *parts, own, other)


def table_shape(parts, orbitals):
    if len(parts) == 1:
        return (1, 1, 1, orbitals, parts[0].shape[-1])
    return (2, 4, 2, orbitals, parts[0].shape[-1])


def last_kernel(own, other, ket, out, tiles, results, sems):
    count, orbitals = ket.shape[1:3]
    group = tiles.shape[1] // orbitals
    half_rounded = jnp.concatenate([own[...], other[...]], axis=1)
    copies = []
    for t in range(orbitals // group):
        tile = tiles.at[t % 2]
        for n in range(count):
            last = ket[1, n]
            for r in range(group):
                row = jnp.broadcast_to(ket[0, n, t * group + r : t * group + r + 1, :], last.shape)
                tile[r * orbitals : (r + 1) * orbitals, n * LANES : (n + 1) * LANES] = (
                    row * last
                ).astype(BF)
        results[t] = lax.dot_general(
            half_rounded, tile[...], (((1,), (1,)), ((), ())), preferred_element_type=F32
        )
        columns = group * orbitals
        copies.append(
            pltpu.make_async_copy(
                results.at[t], out.at[:, pl.ds(t * columns, columns)], sems.at[t]
            )
        )
        copies[-1].start()
    for copy in copies:
        copy.wait()


def last_step(own, other, ket):
    rows, kh = own.shape
    orbitals = ket.shape[2]
    group = 8
    count = orbitals // group
    vmem = pl.BlockSpec(memory_space=pltpu.VMEM)
    return pl.pallas_call(
        last_kernel,
        out_shape=jax.ShapeDtypeStruct((rows, orbitals * orbitals), F32),
        in_specs=[vmem] * 3,
        out_specs=pl.BlockSpec(memory_space=pltpu.HBM),
        scratch_shapes=[
            pltpu.VMEM((2, group * orbitals, 2 * kh), BF),
            pltpu.VMEM((count, rows, group * orbitals), F32),
            pltpu.SemaphoreType.DMA((count,)),
        ],
        compiler_params=pltpu.CompilerParams(vmem_limit_bytes=16 * 2**20),
        name="last_step",
    )(own, other, ket)


def permute(array, mask, count):
    return lax.ppermute(array, "pan", [(i, i ^ mask) for i in range(count)])


def add_kernel(count, *refs):
    total = refs[0][...].astype(F32)
    for ref in refs[1:count]:
        total = total + ref[...].astype(F32)
    refs[-1][...] = total.astype(BF)


def added(*arrays, later=None):
    vmem, anywhere = pl.BlockSpec(memory_space=pltpu.VMEM), pl.BlockSpec(memory_space=pl.ANY)
    shape = jax.ShapeDtypeStruct(arrays[0].shape, BF)
    more = [] if later is None else [later]

    def kernel(*refs):
        add_kernel(len(arrays), *refs)

    results = pl.pallas_call(
        kernel,
        out_shape=[jax.ShapeDtypeStruct(array.shape, array.dtype) for array in more] + [shape],
        in_specs=[vmem] * len(arrays) + [anywhere] * len(more),
        out_specs=[anywhere] * len(more) + [vmem],
        input_output_aliases={len(arrays): 0} if more else {},
        cost_estimate=pl.CostEstimate(
            flops=len(arrays) * shape.size, bytes_accessed=0, transcendentals=0
        ),
        name="added",
    )(*arrays, *more)
    return (results[1], results[0]) if more else results[0]


def done_kernel(me_ref, kept, arrived, one, left, right, keep, give):
    core = me_ref[0] & 1
    rows = keep.shape[0]
    for out, at in ((keep, core), (give, 1 - core)):
        part = pl.ds(pl.multiple_of(at * rows, rows), rows)
        total = kept[part, :].astype(F32) + arrived[part, :].astype(F32) + one[part, :].astype(F32)
        hops = jnp.concatenate([left[part, :].astype(F32), right[part, :].astype(F32)], axis=1)
        out[...] = (total + hops).astype(BF)


def done_sum(me, kept, arrived, one, left, right):
    rows, kh = kept.shape
    vmem = pl.BlockSpec(memory_space=pltpu.VMEM)
    return pl.pallas_call(
        done_kernel,
        out_shape=[jax.ShapeDtypeStruct((rows // 2, kh), BF)] * 2,
        grid_spec=pltpu.PrefetchScalarGridSpec(
            num_scalar_prefetch=1, grid=(), in_specs=[vmem] * 5, out_specs=[vmem] * 2
        ),
        cost_estimate=pl.CostEstimate(flops=5 * rows * kh, bytes_accessed=0, transcendentals=0),
        name="done_sum",
    )(me, kept, arrived, one, left, right)


def gather_small(mine, nothing, count):
    middle = mine.shape[0] // 2
    a, b = mine[:middle], mine[middle:]
    b_x = permute(b, 2, count)
    a_z = {s: permute(a, 4 * s, count) for s in (3, 2, 1)}
    b_pair = jnp.stack([b, b_x])
    b_z = {s: permute(b_pair, 4 * s, count) for s in (3, 2, 1)}
    near = jnp.stack([a, a_z[1], a_z[2], a_z[3]]) + nothing
    far = permute(near, 2, count)
    rest = jnp.stack([b_pair, b_z[1], b_z[2], b_z[3]])
    upper, lower = pl.ds(0, middle), pl.ds(middle, middle)
    everything = slice(None)
    parts, regions = [], []
    for x, part in ((0, near), (1, far)):
        for core in range(2):
            parts.append(permute(part, 1, count) if core else part)
            regions.append((core, everything, x, upper))
    for core in range(2):
        parts.append(permute(rest, 1, count) if core else rest)
        regions.append((core, everything, everything, lower))
    return parts, regions


def shards(
    count, blocks, first_block, second_block, slot_counts, ket_first, ket_second, coefficients, mo_index
):
    me = lax.axis_index("pan").astype(jnp.int32)
    core = me % 2
    me_array = me.reshape(1)
    capacity, kp, pair = blocks.shape
    kh = kp // 2
    own_ao, nmo = coefficients.shape
    swap = functools.partial(permute, mask=1, count=count)

    numbers = jnp.concatenate([first_block, second_block, slot_counts])
    other_numbers = swap(numbers)
    picks = (mo_index[:, None] == jnp.arange(nmo, dtype=jnp.int32)[None, :]).astype(BF)
    mine = lax.dot_general(
        picks, coefficients, (((1,), (1,)), ((), ())), preferred_element_type=F32
    ).astype(BF)
    orbitals = mine.shape[0]

    units = own_ao // 8
    factor = -(-(2**20) // max(units, 1))
    other = swap(blocks)

    small = count == 16 and own_ao % 16 == 0
    if small:
        nothing = (other_numbers[0] < 0).astype(BF)
        mine = jnp.pad(mine, ((0, 0), (0, -own_ao % LANES)))
        parts, regions = gather_small(mine, nothing, count)

        def locate(unit, me):
            owner = (unit * factor) >> 20
            away = owner ^ me
            return away & 1, away >> 2, (away >> 1) & 1, (unit - owner * units) * 8
    else:
        parts = [lax.all_gather(mine, "pan", axis=1, tiled=True)]
        regions = [(0, 0, 0)]

        def locate(unit, me):
            return 0, 0, 0, unit * 8

    bra = functools.partial(
        bra_transform,
        regions,
        locate,
        parts,
        blocks,
        other,
        (numbers, other_numbers),
        (ket_first, ket_second),
        me_array,
        orbitals,
    )

    if small:
        chunk, side = orbitals // 8, kh // 2
        order = ((3, 0, side), (2, 0, side), (3, side, kh), (2, side, kh), (1, 0, kh), (0, 0, kh))
        pieces = order + tuple((s + 4, a, b) for s, a, b in order)
        *partial, ket = bra(chunk, pieces, BF)
        kept = partial[6:]
        arrived = [permute(piece, 2, count) for piece in partial[:5]]
        three_a = permute(added(kept[0], arrived[0]), 4, count)
        three_b = permute(added(kept[2], arrived[2]), 4, count)
        total, last = added(kept[1], arrived[1], three_a, later=partial[5])
        left = permute(total, 8, count)
        arrived.append(permute(last, 2, count))
        right = permute(added(kept[3], arrived[3], three_b), 8, count)
        one = permute(added(kept[4], arrived[4]), 4, count)
        keep, give = done_sum(me_array, kept[5], arrived[5], one, left, right)
    else:
        partial, ket = bra(orbitals, ((0, 0, kh),), F32)
        sides = [list(range(c, count, 2)) for c in range(2)]
        done = lax.psum_scatter(
            partial, "pan", scatter_dimension=0, tiled=True, axis_index_groups=sides
        ).astype(BF)
        rows = done.shape[0] // 2
        keep = lax.dynamic_slice_in_dim(done, core * rows, rows, axis=0)
        give = lax.dynamic_slice_in_dim(done, (1 - core) * rows, rows, axis=0)
    return last_step(keep, swap(give), ket)


def solution(mesh):
    placed = (
        P(("grp", "pan"), None, None),
        P(("grp", "pan")),
        P(("grp", "pan")),
        P(("grp", "pan")),
        P("grp"),
        P("grp"),
        P(("grp", "pan"), None),
        P("grp"),
    )
    return jax.shard_map(
        functools.partial(shards, mesh.shape["pan"]),
        mesh=mesh,
        in_specs=placed,
        out_specs=P(("grp", "pan"), None),
        check_vma=False,
    )
```

```python
import functools

import jax
import jax.numpy as jnp
from jax import lax
from jax.experimental import pallas as pl
from jax.experimental.pallas import tpu as pltpu
from jax.sharding import PartitionSpec as P

GROUP = 32
STEP = 8
LANES = 128
BF = jnp.bfloat16
F32 = jnp.float32
VMEM_LIMIT = 58 * 2**20


def spread(kind):
    row = lax.broadcasted_iota(jnp.int32, (LANES, LANES), 0)
    col = lax.broadcasted_iota(jnp.int32, (LANES, LANES), 1)
    source = col // 8 if kind == "a" else col % 8
    return (row == source).astype(F32).astype(BF)


def table_piece(table, place, target):
    core, z, x, lane = place
    inside = lane & (LANES - 1)
    start = pl.multiple_of(lane - inside, LANES)
    piece = table[core, z, x, :, pl.ds(start, LANES)].astype(F32)
    return pltpu.roll(piece, (target - inside) & (LANES - 1), 1)


def load_table(regions, parts, table, sems):
    return [
        pltpu.make_async_copy(part, table.at[region], sems.at[n])
        for n, (region, part) in enumerate(zip(regions, parts))
    ]


def bra_kernel(regions, locate, chunk, pieces, me_ref, mine, theirs, firsts, seconds, *refs):
    parts, refs = refs[: len(regions)], refs[len(regions) :]
    own, other = refs[:2]
    outs, ket = refs[2 : 2 + len(pieces)], refs[2 + len(pieces)]
    table, blk, picked, wide, half, second, ready, table_sems, block_sems, out_sems = refs[
        3 + len(pieces) :
    ]
    orbitals = second.shape[1]
    capacity = own.shape[0]
    kh = blk.shape[1]
    me = me_ref[0]
    own_live, other_live = mine[2 * capacity], theirs[2 * capacity]
    k_start = pl.multiple_of((me & 1) * kh, LANES)
    live = own_live + other_live

    copies = load_table(regions, parts, table, table_sems)
    for copy in copies:
        copy.start()

    def start_own(n, carry):
        pltpu.make_async_copy(
            own.at[n, pl.ds(k_start, kh)], blk.at[n], block_sems.at[n // STEP]
        ).start()
        return carry

    def start_other(n, carry):
        pltpu.make_async_copy(
            other.at[n - own_live, pl.ds(k_start, kh)], blk.at[n], block_sems.at[n // STEP]
        ).start()
        return carry

    lax.fori_loop(0, own_live, start_own, 0)
    lax.fori_loop(own_live, live, start_other, 0)
    lanes = lax.broadcasted_iota(jnp.int32, (8, LANES), 1)
    diagonal = (lanes % 8 == lax.broadcasted_iota(jnp.int32, (8, LANES), 0)).astype(F32)
    empty = jnp.zeros((8, LANES), F32)
    spread_a = spread("a")
    groups = (live + GROUP - 1) // GROUP
    steps = (live + STEP - 1) // STEP
    second[...] = jnp.zeros_like(second)

    def number(n, column):
        ours = mine[column * capacity + jnp.minimum(n, own_live - 1)]
        partners = theirs[column * capacity + jnp.maximum(n - own_live, 0)]
        return jnp.where(n < own_live, ours, partners)

    for copy in copies:
        copy.wait()

    count = ket.shape[1]
    for n in range(count):
        kb = (n + (me & 1) * (count // 2)) & (count - 1)
        piece = table_piece(table, locate(firsts[kb] * 2, me), 0)
        ket[0, n] = jnp.dot(piece.astype(BF), spread_a, preferred_element_type=F32)
        piece = table_piece(table, locate(seconds[kb], me), 0)
        ket[1, n] = jnp.dot(piece.astype(BF), spread("b"), preferred_element_type=F32)

    def do_step(o, carry):
        start = o * STEP

        def wait_one(n, carry):
            pltpu.make_async_copy(
                own.at[0, pl.ds(k_start, kh)], blk.at[n], block_sems.at[o]
            ).wait()
            return carry

        lax.fori_loop(start, jnp.minimum(start + STEP, live), wait_one, 0)
        slots = [jnp.minimum(start + u, live - 1) for u in range(STEP)]
        for u, n in enumerate(slots):
            piece = table_piece(table, locate(number(n, 0) * 2, me), 0)
            picked[u * orbitals : (u + 1) * orbitals] = piece.astype(BF)
        wide[...] = jnp.dot(picked[...], spread_a, preferred_element_type=F32)

        cover = 8 * STEP
        parity = o & (LANES // cover - 1)
        wanted = lax.broadcasted_iota(jnp.int32, (orbitals, LANES), 1)
        place = (wanted % cover) // 8
        merged = jnp.zeros((orbitals, LANES), F32)
        for u, n in enumerate(slots):
            where = locate(number(n, 1), me)
            piece = table_piece(table, where, parity * cover + 8 * u)
            merged = jnp.where(place == u, piece, merged)
        keep = (wanted // cover == parity) & (start + place < live)
        at = o // (LANES // cover)
        second[at] = jnp.where(keep, merged, second[at])

        for p in range(STEP // 2):
            rows = []
            for i in range(orbitals):
                x, y = (
                    jnp.broadcast_to(wide[u * orbitals + i : u * orbitals + i + 1, :], (8, LANES))
                    * diagonal
                    for u in (2 * p, 2 * p + 1)
                )
                rows.append(jnp.concatenate([x, empty], axis=1))
                rows.append(jnp.concatenate([empty, y], axis=1))
            factor = jnp.concatenate(rows, axis=0).astype(BF)
            data = jnp.concatenate([blk[slots[2 * p]], blk[slots[2 * p + 1]]], axis=1)
            result = lax.dot_general(
                factor, data, (((1,), (1,)), ((), ())), preferred_element_type=F32
            )
            at = pl.multiple_of(o * cover + 16 * p, 16)
            half[:, pl.ds(at, 16), :] = result.astype(BF).reshape(orbitals, 16, kh)
        return carry

    lax.fori_loop(0, steps, do_step, 0)

    def clear(o, carry):
        at = pl.multiple_of(o * 8 * STEP, 8 * STEP)
        half[:, pl.ds(at, 8 * STEP), :] = jnp.zeros((orbitals, 8 * STEP, kh), BF)
        return carry

    lax.fori_loop(steps, groups * (GROUP // STEP), clear, 0)

    def leave(n):
        s, low, high = pieces[n]
        return pltpu.make_async_copy(
            ready.at[s, :, pl.ds(low, high - low)], outs[n], out_sems.at[n]
        )

    def finish(count):
        weights = jnp.concatenate([second[n] for n in range(2 * count)], axis=1).astype(BF)
        for s in dict.fromkeys(piece[0] for piece in pieces):
            first = 0
            if len(pieces) > 1:
                first = ((me >> 2) ^ (s & 3)) * 2 * chunk + (((me >> 1) & 1) ^ (1 - (s >> 2))) * chunk
            for r in range(chunk):
                piece = half[first + r, 0 : 8 * GROUP * count, :]
                ready[s, r * orbitals : (r + 1) * orbitals, :] = jnp.dot(
                    weights, piece, preferred_element_type=F32
                ).astype(ready.dtype)
            for n in range(len(pieces)):
                if pieces[n][0] == s:
                    leave(n).start()

    for count in range(1, half.shape[1] // (8 * GROUP) + 1):
        pl.when(groups == count)(functools.partial(finish, count))
    for n in range(len(pieces)):
        leave(n).wait()


def bra_transform(
    regions, locate, parts, own, other, numbers, ket_numbers, me, orbitals, chunk, pieces, kind
):
    capacity, kp, pair = own.shape
    kh = kp // 2
    groups = -(-2 * capacity // GROUP)
    rows = chunk * orbitals
    hbm = pl.BlockSpec(memory_space=pltpu.HBM)
    return pl.pallas_call(
        functools.partial(bra_kernel, regions, locate, chunk, pieces),
        out_shape=[jax.ShapeDtypeStruct((rows, high - low), kind) for _, low, high in pieces]
        + [jax.ShapeDtypeStruct((2, kp // LANES, orbitals, LANES), F32)],
        grid_spec=pltpu.PrefetchScalarGridSpec(
            num_scalar_prefetch=5,
            grid=(),
            in_specs=[hbm] * (len(parts) + 2),
            out_specs=[hbm] * len(pieces) + [pl.BlockSpec(memory_space=pltpu.VMEM)],
            scratch_shapes=[
                pltpu.VMEM(table_shape(parts, orbitals), BF),
                pltpu.VMEM((2 * capacity, kh, pair), BF),
                pltpu.VMEM((STEP * orbitals, LANES), BF),
                pltpu.VMEM((STEP * orbitals, LANES), F32),
                pltpu.VMEM((orbitals, 8 * GROUP * groups, kh), BF),
                pltpu.VMEM((2 * groups, orbitals, LANES), F32),
                pltpu.VMEM((orbitals // chunk, rows, kh), kind),
                pltpu.SemaphoreType.DMA((len(parts),)),
                pltpu.SemaphoreType.DMA((-(-2 * capacity // STEP),)),
                pltpu.SemaphoreType.DMA((len(pieces),)),
            ],
        ),
        compiler_params=pltpu.CompilerParams(vmem_limit_bytes=VMEM_LIMIT),
        cost_estimate=pl.CostEstimate(
            flops=4 * capacity * 8 * orbitals * pair * kh, bytes_accessed=8 * 2**20, transcendentals=0
        ),
        name="bra_transform",
    )(me, *numbers, *ket_numbers, *parts, own, other)


def table_shape(parts, orbitals):
    if len(parts) == 1:
        return (1, 1, 1, orbitals, parts[0].shape[-1])
    return (2, 4, 2, orbitals, parts[0].shape[-1])


def last_kernel(own, other, ket, out, tiles, results, sems):
    count, orbitals = ket.shape[1:3]
    group = tiles.shape[1] // orbitals
    half_rounded = jnp.concatenate([own[...], other[...]], axis=1)
    copies = []
    for t in range(orbitals // group):
        tile = tiles.at[t % 2]
        for n in range(count):
            last = ket[1, n]
            for r in range(group):
                row = jnp.broadcast_to(ket[0, n, t * group + r : t * group + r + 1, :], last.shape)
                tile[r * orbitals : (r + 1) * orbitals, n * LANES : (n + 1) * LANES] = (
                    row * last
                ).astype(BF)
        results[t] = lax.dot_general(
            half_rounded, tile[...], (((1,), (1,)), ((), ())), preferred_element_type=F32
        )
        columns = group * orbitals
        copies.append(
            pltpu.make_async_copy(
                results.at[t], out.at[:, pl.ds(t * columns, columns)], sems.at[t]
            )
        )
        copies[-1].start()
    for copy in copies:
        copy.wait()


def last_step(own, other, ket):
    rows, kh = own.shape
    orbitals = ket.shape[2]
    group = 8
    count = orbitals // group
    vmem = pl.BlockSpec(memory_space=pltpu.VMEM)
    return pl.pallas_call(
        last_kernel,
        out_shape=jax.ShapeDtypeStruct((rows, orbitals * orbitals), F32),
        in_specs=[vmem] * 3,
        out_specs=pl.BlockSpec(memory_space=pltpu.HBM),
        scratch_shapes=[
            pltpu.VMEM((2, group * orbitals, 2 * kh), BF),
            pltpu.VMEM((count, rows, group * orbitals), F32),
            pltpu.SemaphoreType.DMA((count,)),
        ],
        compiler_params=pltpu.CompilerParams(vmem_limit_bytes=16 * 2**20),
        name="last_step",
    )(own, other, ket)


def permute(array, mask, count):
    return lax.ppermute(array, "pan", [(i, i ^ mask) for i in range(count)])


def added(*arrays):
    result = arrays[0].astype(F32)
    for array in arrays[1:]:
        result = result + array.astype(F32)
    return result.astype(BF)


def gather_small(mine, nothing, count):
    middle = mine.shape[0] // 2
    a, b = mine[:middle], mine[middle:]
    b_x = permute(b, 2, count)
    a_z = {s: permute(a, 4 * s, count) for s in (3, 2, 1)}
    b_pair = jnp.stack([b, b_x])
    b_z = {s: permute(b_pair, 4 * s, count) for s in (3, 2, 1)}
    near = jnp.stack([a, a_z[1], a_z[2], a_z[3]]) + nothing
    far = permute(near, 2, count)
    rest = jnp.stack([b_pair, b_z[1], b_z[2], b_z[3]])
    upper, lower = pl.ds(0, middle), pl.ds(middle, middle)
    everything = slice(None)
    parts, regions = [], []
    for x, part in ((0, near), (1, far)):
        for core in range(2):
            parts.append(permute(part, 1, count) if core else part)
            regions.append((core, everything, x, upper))
    for core in range(2):
        parts.append(permute(rest, 1, count) if core else rest)
        regions.append((core, everything, everything, lower))
    return parts, regions


def shards(
    count, blocks, first_block, second_block, slot_counts, ket_first, ket_second, coefficients, mo_index
):
    me = lax.axis_index("pan").astype(jnp.int32)
    core = me % 2
    me_array = me.reshape(1)
    capacity, kp, pair = blocks.shape
    kh = kp // 2
    own_ao, nmo = coefficients.shape
    swap = functools.partial(permute, mask=1, count=count)

    numbers = jnp.concatenate([first_block, second_block, slot_counts])
    other_numbers = swap(numbers)
    picks = (mo_index[:, None] == jnp.arange(nmo, dtype=jnp.int32)[None, :]).astype(BF)
    mine = lax.dot_general(
        picks, coefficients, (((1,), (1,)), ((), ())), preferred_element_type=F32
    ).astype(BF)
    orbitals = mine.shape[0]

    units = own_ao // 8
    factor = -(-(2**20) // max(units, 1))
    other = swap(blocks)

    small = count == 16 and own_ao % 16 == 0
    if small:
        nothing = (other_numbers[0] < 0).astype(BF)
        mine = jnp.pad(mine, ((0, 0), (0, -own_ao % LANES)))
        parts, regions = gather_small(mine, nothing, count)

        def locate(unit, me):
            owner = (unit * factor) >> 20
            away = owner ^ me
            return away & 1, away >> 2, (away >> 1) & 1, (unit - owner * units) * 8
    else:
        parts = [lax.all_gather(mine, "pan", axis=1, tiled=True)]
        regions = [(0, 0, 0)]

        def locate(unit, me):
            return 0, 0, 0, unit * 8

    bra = functools.partial(
        bra_transform,
        regions,
        locate,
        parts,
        blocks,
        other,
        (numbers, other_numbers),
        (ket_first, ket_second),
        me_array,
        orbitals,
    )

    if small:
        chunk, side = orbitals // 8, kh // 2
        order = ((3, 0, side), (2, 0, side), (3, side, kh), (2, side, kh), (1, 0, kh), (0, 0, kh))
        pieces = order + tuple((s + 4, a, b) for s, a, b in order)
        *partial, ket = bra(chunk, pieces, BF)
        there, here = partial[:6], partial[6:]
        one = permute(here[4], 4, count)
        three_a = added(here[0], permute(there[0], 2, count))
        two_a = added(here[1], permute(there[1], 2, count), permute(three_a, 4, count))
        three_b = added(here[2], permute(there[2], 2, count))
        two_b = added(here[3], permute(there[3], 2, count), permute(three_b, 4, count))
        nothing = (three_a[0, 0] != three_a[0, 0]).astype(BF)
        other_one = permute(there[4] + nothing, 4, count)
        zero = permute(added(there[5], other_one), 2, count)
        two = jnp.concatenate([permute(two_a, 8, count), permute(two_b, 8, count)], axis=1)
        done = added(here[5], zero, one, two)
    else:
        partial, ket = bra(orbitals, ((0, 0, kh),), F32)
        sides = [list(range(c, count, 2)) for c in range(2)]
        done = lax.psum_scatter(
            partial, "pan", scatter_dimension=0, tiled=True, axis_index_groups=sides
        ).astype(BF)
    rows = done.shape[0] // 2
    keep = lax.dynamic_slice_in_dim(done, core * rows, rows, axis=0)
    give = lax.dynamic_slice_in_dim(done, (1 - core) * rows, rows, axis=0)
    return last_step(keep, swap(give), ket)


def solution(mesh):
    placed = (
        P(("grp", "pan"), None, None),
        P(("grp", "pan")),
        P(("grp", "pan")),
        P(("grp", "pan")),
        P("grp"),
        P("grp"),
        P(("grp", "pan"), None),
        P("grp"),
    )
    return jax.shard_map(
        functools.partial(shards, mesh.shape["pan"]),
        mesh=mesh,
        in_specs=placed,
        out_specs=P(("grp", "pan"), None),
        check_vma=False,
    )
```

```python
import functools

import jax
import jax.numpy as jnp
from jax import lax
from jax.experimental import pallas as pl
from jax.experimental.pallas import tpu as pltpu
from jax.sharding import PartitionSpec as P

GROUP = 32
STEP = 8
LANES = 128
BF = jnp.bfloat16
F32 = jnp.float32
VMEM_LIMIT = 51 * 2**20


def spread(kind):
    row = lax.broadcasted_iota(jnp.int32, (LANES, LANES), 0)
    col = lax.broadcasted_iota(jnp.int32, (LANES, LANES), 1)
    source = col // 8 if kind == "a" else col % 8
    return (row == source).astype(F32).astype(BF)


def table_piece(table, place, target):
    core, z, x, lane = place
    inside = lane & (LANES - 1)
    start = pl.multiple_of(lane - inside, LANES)
    piece = table[core, z, x, :, pl.ds(start, LANES)].astype(F32)
    return pltpu.roll(piece, (target - inside) & (LANES - 1), 1)


def load_table(regions, parts, table, sems):
    return [
        pltpu.make_async_copy(part, table.at[region], sems.at[n])
        for n, (region, part) in enumerate(zip(regions, parts))
    ]


def bra_kernel(regions, locate, chunk, pieces, me_ref, mine, theirs, firsts, seconds, *refs):
    parts, refs = refs[: len(regions)], refs[len(regions) :]
    own, other = refs[:2]
    outs, ket = refs[2 : 2 + len(pieces)], refs[2 + len(pieces)]
    table, blk, picked, wide, half, second, ready, table_sems, block_sems, out_sems = refs[
        3 + len(pieces) :
    ]
    orbitals = second.shape[1]
    capacity = own.shape[0]
    kh = blk.shape[1]
    me = me_ref[0]
    own_live, other_live = mine[2 * capacity], theirs[2 * capacity]
    k_start = pl.multiple_of((me & 1) * kh, LANES)
    live = own_live + other_live

    copies = load_table(regions, parts, table, table_sems)
    for copy in copies:
        copy.start()

    def start_own(n, carry):
        pltpu.make_async_copy(
            own.at[n, pl.ds(k_start, kh)], blk.at[n], block_sems.at[n // STEP]
        ).start()
        return carry

    def start_other(n, carry):
        pltpu.make_async_copy(
            other.at[n - own_live, pl.ds(k_start, kh)], blk.at[n], block_sems.at[n // STEP]
        ).start()
        return carry

    lax.fori_loop(0, own_live, start_own, 0)
    lax.fori_loop(own_live, live, start_other, 0)
    lanes = lax.broadcasted_iota(jnp.int32, (8, LANES), 1)
    diagonal = (lanes % 8 == lax.broadcasted_iota(jnp.int32, (8, LANES), 0)).astype(F32)
    empty = jnp.zeros((8, LANES), F32)
    spread_a = spread("a")
    groups = (live + GROUP - 1) // GROUP
    steps = (live + STEP - 1) // STEP
    second[...] = jnp.zeros_like(second)

    def number(n, column):
        ours = mine[column * capacity + jnp.minimum(n, own_live - 1)]
        partners = theirs[column * capacity + jnp.maximum(n - own_live, 0)]
        return jnp.where(n < own_live, ours, partners)

    for copy in copies:
        copy.wait()

    count = ket.shape[1]
    for n in range(count):
        kb = (n + (me & 1) * (count // 2)) & (count - 1)
        piece = table_piece(table, locate(firsts[kb] * 2, me), 0)
        ket[0, n] = jnp.dot(piece.astype(BF), spread_a, preferred_element_type=F32)
        piece = table_piece(table, locate(seconds[kb], me), 0)
        ket[1, n] = jnp.dot(piece.astype(BF), spread("b"), preferred_element_type=F32)

    def do_step(o, carry):
        start = o * STEP

        def wait_one(n, carry):
            pltpu.make_async_copy(
                own.at[0, pl.ds(k_start, kh)], blk.at[n], block_sems.at[o]
            ).wait()
            return carry

        lax.fori_loop(start, jnp.minimum(start + STEP, live), wait_one, 0)
        slots = [jnp.minimum(start + u, live - 1) for u in range(STEP)]
        for u, n in enumerate(slots):
            piece = table_piece(table, locate(number(n, 0) * 2, me), 0)
            picked[u * orbitals : (u + 1) * orbitals] = piece.astype(BF)
        wide[...] = jnp.dot(picked[...], spread_a, preferred_element_type=F32)

        cover = 8 * STEP
        parity = o & (LANES // cover - 1)
        wanted = lax.broadcasted_iota(jnp.int32, (orbitals, LANES), 1)
        place = (wanted % cover) // 8
        merged = jnp.zeros((orbitals, LANES), F32)
        for u, n in enumerate(slots):
            where = locate(number(n, 1), me)
            piece = table_piece(table, where, parity * cover + 8 * u)
            merged = jnp.where(place == u, piece, merged)
        keep = (wanted // cover == parity) & (start + place < live)
        at = o // (LANES // cover)
        second[at] = jnp.where(keep, merged, second[at])

        for p in range(STEP // 2):
            rows = []
            for i in range(orbitals):
                x, y = (
                    jnp.broadcast_to(wide[u * orbitals + i : u * orbitals + i + 1, :], (8, LANES))
                    * diagonal
                    for u in (2 * p, 2 * p + 1)
                )
                rows.append(jnp.concatenate([x, empty], axis=1))
                rows.append(jnp.concatenate([empty, y], axis=1))
            factor = jnp.concatenate(rows, axis=0).astype(BF)
            data = jnp.concatenate([blk[slots[2 * p]], blk[slots[2 * p + 1]]], axis=1)
            result = lax.dot_general(
                factor, data, (((1,), (1,)), ((), ())), preferred_element_type=F32
            )
            at = pl.multiple_of(o * cover + 16 * p, 16)
            half[:, pl.ds(at, 16), :] = result.astype(BF).reshape(orbitals, 16, kh)
        return carry

    lax.fori_loop(0, steps, do_step, 0)

    def clear(o, carry):
        at = pl.multiple_of(o * 8 * STEP, 8 * STEP)
        half[:, pl.ds(at, 8 * STEP), :] = jnp.zeros((orbitals, 8 * STEP, kh), BF)
        return carry

    lax.fori_loop(steps, groups * (GROUP // STEP), clear, 0)

    def leave(n):
        s, low, high = pieces[n]
        return pltpu.make_async_copy(
            ready.at[s, :, pl.ds(low, high - low)], outs[n], out_sems.at[n]
        )

    def finish(count):
        weights = jnp.concatenate([second[n] for n in range(2 * count)], axis=1).astype(BF)
        for s in dict.fromkeys(piece[0] for piece in pieces):
            first = 0
            if len(pieces) > 1:
                first = ((me >> 2) ^ (s & 3)) * 2 * chunk + (((me >> 1) & 1) ^ (1 - (s >> 2))) * chunk
            for r in range(chunk):
                piece = half[first + r, 0 : 8 * GROUP * count, :]
                ready[s, r * orbitals : (r + 1) * orbitals, :] = jnp.dot(
                    weights, piece, preferred_element_type=F32
                ).astype(ready.dtype)
            for n in range(len(pieces)):
                if pieces[n][0] == s:
                    leave(n).start()

    for count in range(1, half.shape[1] // (8 * GROUP) + 1):
        pl.when(groups == count)(functools.partial(finish, count))
    for n in range(len(pieces)):
        leave(n).wait()


def bra_transform(
    regions, locate, parts, own, other, numbers, ket_numbers, me, orbitals, chunk, pieces, kind
):
    capacity, kp, pair = own.shape
    kh = kp // 2
    groups = -(-2 * capacity // GROUP)
    rows = chunk * orbitals
    hbm = pl.BlockSpec(memory_space=pltpu.HBM)
    return pl.pallas_call(
        functools.partial(bra_kernel, regions, locate, chunk, pieces),
        out_shape=[jax.ShapeDtypeStruct((rows, high - low), kind) for _, low, high in pieces]
        + [jax.ShapeDtypeStruct((2, kp // LANES, orbitals, LANES), F32)],
        grid_spec=pltpu.PrefetchScalarGridSpec(
            num_scalar_prefetch=5,
            grid=(),
            in_specs=[hbm] * (len(parts) + 2),
            out_specs=[hbm] * len(pieces) + [pl.BlockSpec(memory_space=pltpu.VMEM)],
            scratch_shapes=[
                pltpu.VMEM(table_shape(parts, orbitals), BF),
                pltpu.VMEM((2 * capacity, kh, pair), BF),
                pltpu.VMEM((STEP * orbitals, LANES), BF),
                pltpu.VMEM((STEP * orbitals, LANES), F32),
                pltpu.VMEM((orbitals, 8 * GROUP * groups, kh), BF),
                pltpu.VMEM((2 * groups, orbitals, LANES), F32),
                pltpu.VMEM((orbitals // chunk, rows, kh), kind),
                pltpu.SemaphoreType.DMA((len(parts),)),
                pltpu.SemaphoreType.DMA((-(-2 * capacity // STEP),)),
                pltpu.SemaphoreType.DMA((len(pieces),)),
            ],
        ),
        compiler_params=pltpu.CompilerParams(vmem_limit_bytes=VMEM_LIMIT),
        cost_estimate=pl.CostEstimate(
            flops=4 * capacity * 8 * orbitals * pair * kh, bytes_accessed=8 * 2**20, transcendentals=0
        ),
        name="bra_transform",
    )(me, *numbers, *ket_numbers, *parts, own, other)


def table_shape(parts, orbitals):
    if len(parts) == 1:
        return (1, 1, 1, orbitals, parts[0].shape[-1])
    return (2, 4, 2, orbitals, parts[0].shape[-1])


def last_kernel(own, other, ket, out, tiles, results, sems):
    count, orbitals = ket.shape[1:3]
    group = tiles.shape[1] // orbitals
    half_rounded = jnp.concatenate([own[...], other[...]], axis=1)
    copies = []
    for t in range(orbitals // group):
        tile = tiles.at[t % 2]
        for n in range(count):
            last = ket[1, n]
            for r in range(group):
                row = jnp.broadcast_to(ket[0, n, t * group + r : t * group + r + 1, :], last.shape)
                tile[r * orbitals : (r + 1) * orbitals, n * LANES : (n + 1) * LANES] = (
                    row * last
                ).astype(BF)
        results[t] = lax.dot_general(
            half_rounded, tile[...], (((1,), (1,)), ((), ())), preferred_element_type=F32
        )
        columns = group * orbitals
        copies.append(
            pltpu.make_async_copy(
                results.at[t], out.at[:, pl.ds(t * columns, columns)], sems.at[t]
            )
        )
        copies[-1].start()
    for copy in copies:
        copy.wait()


def last_step(own, other, ket):
    rows, kh = own.shape
    orbitals = ket.shape[2]
    group = 8
    count = orbitals // group
    vmem = pl.BlockSpec(memory_space=pltpu.VMEM)
    return pl.pallas_call(
        last_kernel,
        out_shape=jax.ShapeDtypeStruct((rows, orbitals * orbitals), F32),
        in_specs=[vmem] * 3,
        out_specs=pl.BlockSpec(memory_space=pltpu.HBM),
        scratch_shapes=[
            pltpu.VMEM((2, group * orbitals, 2 * kh), BF),
            pltpu.VMEM((count, rows, group * orbitals), F32),
            pltpu.SemaphoreType.DMA((count,)),
        ],
        compiler_params=pltpu.CompilerParams(vmem_limit_bytes=16 * 2**20),
        name="last_step",
    )(own, other, ket)


def permute(array, mask, count):
    return lax.ppermute(array, "pan", [(i, i ^ mask) for i in range(count)])


def added(*arrays):
    result = arrays[0].astype(F32)
    for array in arrays[1:]:
        result = result + array.astype(F32)
    return result.astype(BF)


def gather_small(mine, nothing, count):
    middle = mine.shape[0] // 2
    a, b = mine[:middle], mine[middle:]
    b_x = permute(b, 2, count)
    a_z = {s: permute(a, 4 * s, count) for s in (3, 2, 1)}
    b_pair = jnp.stack([b, b_x])
    b_z = {s: permute(b_pair, 4 * s, count) for s in (3, 2, 1)}
    near = jnp.stack([a, a_z[1], a_z[2], a_z[3]]) + nothing
    far = permute(near, 2, count)
    rest = jnp.stack([b_pair, b_z[1], b_z[2], b_z[3]])
    upper, lower = pl.ds(0, middle), pl.ds(middle, middle)
    everything = slice(None)
    parts, regions = [], []
    for x, part in ((0, near), (1, far)):
        for core in range(2):
            parts.append(permute(part, 1, count) if core else part)
            regions.append((core, everything, x, upper))
    for core in range(2):
        parts.append(permute(rest, 1, count) if core else rest)
        regions.append((core, everything, everything, lower))
    return parts, regions


def shards(
    count, blocks, first_block, second_block, slot_counts, ket_first, ket_second, coefficients, mo_index
):
    me = lax.axis_index("pan").astype(jnp.int32)
    core = me % 2
    me_array = me.reshape(1)
    capacity, kp, pair = blocks.shape
    kh = kp // 2
    own_ao, nmo = coefficients.shape
    swap = functools.partial(permute, mask=1, count=count)

    numbers = jnp.concatenate([first_block, second_block, slot_counts])
    other_numbers = swap(numbers)
    picks = (mo_index[:, None] == jnp.arange(nmo, dtype=jnp.int32)[None, :]).astype(BF)
    mine = lax.dot_general(
        picks, coefficients, (((1,), (1,)), ((), ())), preferred_element_type=F32
    ).astype(BF)
    orbitals = mine.shape[0]

    units = own_ao // 8
    factor = -(-(2**20) // max(units, 1))
    other = swap(blocks)

    small = count == 16 and own_ao % 16 == 0
    if small:
        nothing = (other_numbers[0] < 0).astype(BF)
        mine = jnp.pad(mine, ((0, 0), (0, -own_ao % LANES)))
        parts, regions = gather_small(mine, nothing, count)

        def locate(unit, me):
            owner = (unit * factor) >> 20
            away = owner ^ me
            return away & 1, away >> 2, (away >> 1) & 1, (unit - owner * units) * 8
    else:
        parts = [lax.all_gather(mine, "pan", axis=1, tiled=True)]
        regions = [(0, 0, 0)]

        def locate(unit, me):
            return 0, 0, 0, unit * 8

    bra = functools.partial(
        bra_transform,
        regions,
        locate,
        parts,
        blocks,
        other,
        (numbers, other_numbers),
        (ket_first, ket_second),
        me_array,
        orbitals,
    )

    if small:
        chunk, side = orbitals // 8, kh // 2
        order = ((3, 0, side), (2, 0, side), (3, side, kh), (2, side, kh), (1, 0, kh), (0, 0, kh))
        pieces = order + tuple((s + 4, a, b) for s, a, b in order)
        *partial, ket = bra(chunk, pieces, BF)
        there, here = partial[:6], partial[6:]
        three_a = added(here[0], permute(there[0], 2, count))
        two_a = added(here[1], permute(there[1], 2, count), permute(three_a, 4, count))
        three_b = added(here[2], permute(there[2], 2, count))
        nothing = (three_a[0, 0] != three_a[0, 0]).astype(BF)
        two_b = added(here[3], permute(there[3] + nothing, 2, count), permute(three_b, 4, count))
        one = permute(added(here[4], permute(there[4], 2, count)), 4, count)
        zero = permute(there[5] + nothing, 2, count)
        two = jnp.concatenate([permute(two_a, 8, count), permute(two_b, 8, count)], axis=1)
        done = added(here[5], zero, one, two)
    else:
        partial, ket = bra(orbitals, ((0, 0, kh),), F32)
        sides = [list(range(c, count, 2)) for c in range(2)]
        done = lax.psum_scatter(
            partial, "pan", scatter_dimension=0, tiled=True, axis_index_groups=sides
        ).astype(BF)
    rows = done.shape[0] // 2
    keep = lax.dynamic_slice_in_dim(done, core * rows, rows, axis=0)
    give = lax.dynamic_slice_in_dim(done, (1 - core) * rows, rows, axis=0)
    return last_step(keep, swap(give), ket)


def solution(mesh):
    placed = (
        P(("grp", "pan"), None, None),
        P(("grp", "pan")),
        P(("grp", "pan")),
        P(("grp", "pan")),
        P("grp"),
        P("grp"),
        P(("grp", "pan"), None),
        P("grp"),
    )
    return jax.shard_map(
        functools.partial(shards, mesh.shape["pan"]),
        mesh=mesh,
        in_specs=placed,
        out_specs=P(("grp", "pan"), None),
        check_vma=False,
    )
```

```python
import functools

import jax
import jax.numpy as jnp
from jax import lax
from jax.experimental import pallas as pl
from jax.experimental.pallas import tpu as pltpu
from jax.sharding import PartitionSpec as P

HALF = 16
STEP = 8
LANES = 128
BF = jnp.bfloat16
F32 = jnp.float32
VMEM_LIMIT = 51 * 2**20


def spread(kind):
    row = lax.broadcasted_iota(jnp.int32, (LANES, LANES), 0)
    col = lax.broadcasted_iota(jnp.int32, (LANES, LANES), 1)
    source = col // 8 if kind == "a" else col % 8
    return (row == source).astype(F32).astype(BF)


def table_piece(table, place, target):
    core, z, x, lane = place
    inside = lane & (LANES - 1)
    start = pl.multiple_of(lane - inside, LANES)
    piece = table[core, z, x, :, pl.ds(start, LANES)].astype(F32)
    return pltpu.roll(piece, (target - inside) & (LANES - 1), 1)


def load_table(regions, parts, table, sems):
    return [
        pltpu.make_async_copy(part, table.at[region], sems.at[n])
        for n, (region, part) in enumerate(zip(regions, parts))
    ]


def bra_kernel(regions, locate, chunk, pieces, me_ref, mine, theirs, firsts, seconds, *refs):
    parts, refs = refs[: len(regions)], refs[len(regions) :]
    own, other = refs[:2]
    outs, ket = refs[2 : 2 + len(pieces)], refs[2 + len(pieces)]
    table, blk, picked_a, wide_a, picked_b, wide_b, half, second, ready = refs[3 + len(pieces) : -3]
    table_sems, block_sems, out_sems = refs[-3:]
    orbitals = second.shape[1]
    capacity = own.shape[0]
    kh = blk.shape[1]
    me = me_ref[0]
    own_live, other_live = mine[2 * capacity], theirs[2 * capacity]
    k_start = pl.multiple_of((me & 1) * kh, LANES)
    live = own_live + other_live

    copies = load_table(regions, parts, table, table_sems)
    for copy in copies:
        copy.start()

    def start_own(n, carry):
        pltpu.make_async_copy(
            own.at[n, pl.ds(k_start, kh)], blk.at[n], block_sems.at[n // STEP]
        ).start()
        return carry

    def start_other(n, carry):
        pltpu.make_async_copy(
            other.at[n - own_live, pl.ds(k_start, kh)], blk.at[n], block_sems.at[n // STEP]
        ).start()
        return carry

    lax.fori_loop(0, own_live, start_own, 0)
    lax.fori_loop(own_live, live, start_other, 0)
    lanes = lax.broadcasted_iota(jnp.int32, (8, LANES), 1)
    diagonal = (lanes % 8 == lax.broadcasted_iota(jnp.int32, (8, LANES), 0)).astype(F32)
    empty = jnp.zeros((8, LANES), F32)
    spread_a = spread("a")
    groups = (live + HALF - 1) // HALF
    steps = (live + STEP - 1) // STEP
    second[...] = jnp.zeros_like(second)

    def number(n, column):
        ours = mine[column * capacity + jnp.minimum(n, own_live - 1)]
        partners = theirs[column * capacity + jnp.maximum(n - own_live, 0)]
        return jnp.where(n < own_live, ours, partners)

    for copy in copies:
        copy.wait()

    count = ket.shape[1]
    for n in range(count):
        kb = (n + (me & 1) * (count // 2)) & (count - 1)
        piece = table_piece(table, locate(firsts[kb] * 2, me), 0)
        ket[0, n] = jnp.dot(piece.astype(BF), spread_a, preferred_element_type=F32)
        piece = table_piece(table, locate(seconds[kb], me), 0)
        ket[1, n] = jnp.dot(piece.astype(BF), spread("b"), preferred_element_type=F32)

    cover = 8 * STEP
    wanted = lax.broadcasted_iota(jnp.int32, (orbitals, LANES), 1)
    place = (wanted & (cover - 1)) >> 3

    def slots_of(o):
        return [jnp.minimum(o * STEP + u, live - 1) for u in range(STEP)]

    def prepare(o, picked, wide):
        slots = slots_of(o)
        for u, n in enumerate(slots):
            piece = table_piece(table, locate(number(n, 0) * 2, me), 0)
            picked[u * orbitals : (u + 1) * orbitals] = piece.astype(BF)
        wide[...] = jnp.dot(picked[...], spread_a, preferred_element_type=F32)
        parity = o & (LANES // cover - 1)
        merged = jnp.zeros((orbitals, LANES), F32)
        for u, n in enumerate(slots):
            where = locate(number(n, 1), me)
            piece = table_piece(table, where, parity * cover + 8 * u)
            merged = jnp.where(place == u, piece, merged)
        keep = (wanted // cover == parity) & (o * STEP + place < live)
        at = o // (LANES // cover)
        second[at] = jnp.where(keep, merged, second[at])

    def products(o, wide):
        slots = slots_of(o)
        for p in range(STEP // 2):
            rows = []
            for i in range(orbitals):
                x, y = (
                    jnp.broadcast_to(wide[u * orbitals + i : u * orbitals + i + 1, :], (8, LANES))
                    * diagonal
                    for u in (2 * p, 2 * p + 1)
                )
                rows.append(jnp.concatenate([x, empty], axis=1))
                rows.append(jnp.concatenate([empty, y], axis=1))
            factor = jnp.concatenate(rows, axis=0).astype(BF)
            data = jnp.concatenate([blk[slots[2 * p]], blk[slots[2 * p + 1]]], axis=1)
            at = pl.multiple_of(o * cover + 16 * p, 16)
            part = orbitals // 2
            for h in range(2):
                result = lax.dot_general(
                    factor[h * part * 16 : (h + 1) * part * 16],
                    data,
                    (((1,), (1,)), ((), ())),
                    preferred_element_type=F32,
                )
                half[h * part : (h + 1) * part, pl.ds(at, 16), :] = result.astype(BF).reshape(
                    part, 16, kh
                )

    def do_step(o, now, later):
        def wait_one(n, carry):
            pltpu.make_async_copy(
                own.at[0, pl.ds(k_start, kh)], blk.at[n], block_sems.at[o]
            ).wait()
            return carry

        lax.fori_loop(o * STEP, jnp.minimum((o + 1) * STEP, live), wait_one, 0)
        prepare(jnp.minimum(o + 1, steps - 1), *later)
        products(o, now[1])

    def two_steps(h, carry):
        do_step(2 * h, (picked_a, wide_a), (picked_b, wide_b))

        @pl.when(2 * h + 1 < steps)
        def _():
            do_step(2 * h + 1, (picked_b, wide_b), (picked_a, wide_a))

        return carry

    prepare(0, picked_a, wide_a)
    lax.fori_loop(0, (steps + 1) // 2, two_steps, 0)

    def clear(o, carry):
        at = pl.multiple_of(o * 8 * STEP, 8 * STEP)
        half[:, pl.ds(at, 8 * STEP), :] = jnp.zeros((orbitals, 8 * STEP, kh), BF)
        return carry

    lax.fori_loop(steps, groups * (HALF // STEP), clear, 0)

    def leave(n):
        s, low, high = pieces[n]
        return pltpu.make_async_copy(
            ready.at[s, :, pl.ds(low, high - low)], outs[n], out_sems.at[n]
        )

    def finish(count):
        weights = jnp.concatenate([second[n] for n in range(count)], axis=1).astype(BF)
        for s in dict.fromkeys(piece[0] for piece in pieces):
            first = 0
            if len(pieces) > 1:
                first = ((me >> 2) ^ (s & 3)) * 2 * chunk + (((me >> 1) & 1) ^ (1 - (s >> 2))) * chunk
            for r in range(chunk):
                piece = half[first + r, 0 : 8 * HALF * count, :]
                ready[s, r * orbitals : (r + 1) * orbitals, :] = jnp.dot(
                    weights, piece, preferred_element_type=F32
                ).astype(ready.dtype)
            for n in range(len(pieces)):
                if pieces[n][0] == s:
                    leave(n).start()

    for count in range(1, half.shape[1] // (8 * HALF) + 1):
        pl.when(groups == count)(functools.partial(finish, count))
    for n in range(len(pieces)):
        leave(n).wait()


def bra_transform(
    regions, locate, parts, own, other, numbers, ket_numbers, me, orbitals, chunk, pieces, kind
):
    capacity, kp, pair = own.shape
    kh = kp // 2
    groups = -(-2 * capacity // HALF)
    rows = chunk * orbitals
    hbm = pl.BlockSpec(memory_space=pltpu.HBM)
    return pl.pallas_call(
        functools.partial(bra_kernel, regions, locate, chunk, pieces),
        out_shape=[jax.ShapeDtypeStruct((rows, high - low), kind) for _, low, high in pieces]
        + [jax.ShapeDtypeStruct((2, kp // LANES, orbitals, LANES), F32)],
        grid_spec=pltpu.PrefetchScalarGridSpec(
            num_scalar_prefetch=5,
            grid=(),
            in_specs=[hbm] * (len(parts) + 2),
            out_specs=[hbm] * len(pieces) + [pl.BlockSpec(memory_space=pltpu.VMEM)],
            scratch_shapes=[
                pltpu.VMEM(table_shape(parts, orbitals), BF),
                pltpu.VMEM((2 * capacity, kh, pair), BF),
                pltpu.VMEM((STEP * orbitals, LANES), BF),
                pltpu.VMEM((STEP * orbitals, LANES), F32),
                pltpu.VMEM((STEP * orbitals, LANES), BF),
                pltpu.VMEM((STEP * orbitals, LANES), F32),
                pltpu.VMEM((orbitals, 8 * HALF * groups, kh), BF),
                pltpu.VMEM((groups, orbitals, LANES), F32),
                pltpu.VMEM((orbitals // chunk, rows, kh), kind),
                pltpu.SemaphoreType.DMA((len(parts),)),
                pltpu.SemaphoreType.DMA((-(-2 * capacity // STEP),)),
                pltpu.SemaphoreType.DMA((len(pieces),)),
            ],
        ),
        compiler_params=pltpu.CompilerParams(vmem_limit_bytes=VMEM_LIMIT),
        cost_estimate=pl.CostEstimate(
            flops=4 * capacity * 8 * orbitals * pair * kh, bytes_accessed=8 * 2**20, transcendentals=0
        ),
        name="bra_transform",
    )(me, *numbers, *ket_numbers, *parts, own, other)


def table_shape(parts, orbitals):
    if len(parts) == 1:
        return (1, 1, 1, orbitals, parts[0].shape[-1])
    return (2, 4, 2, orbitals, parts[0].shape[-1])


def last_kernel(own, other, ket, out, tiles, results, sems):
    count, orbitals = ket.shape[1:3]
    group = tiles.shape[1] // orbitals
    half_rounded = jnp.concatenate([own[...], other[...]], axis=1)
    copies = []
    for t in range(orbitals // group):
        tile = tiles.at[t % 2]
        for n in range(count):
            last = ket[1, n]
            for r in range(group):
                row = jnp.broadcast_to(ket[0, n, t * group + r : t * group + r + 1, :], last.shape)
                tile[r * orbitals : (r + 1) * orbitals, n * LANES : (n + 1) * LANES] = (
                    row * last
                ).astype(BF)
        results[t] = lax.dot_general(
            half_rounded, tile[...], (((1,), (1,)), ((), ())), preferred_element_type=F32
        )
        columns = group * orbitals
        copies.append(
            pltpu.make_async_copy(
                results.at[t], out.at[:, pl.ds(t * columns, columns)], sems.at[t]
            )
        )
        copies[-1].start()
    for copy in copies:
        copy.wait()


def last_step(own, other, ket):
    rows, kh = own.shape
    orbitals = ket.shape[2]
    group = 8
    count = orbitals // group
    vmem = pl.BlockSpec(memory_space=pltpu.VMEM)
    return pl.pallas_call(
        last_kernel,
        out_shape=jax.ShapeDtypeStruct((rows, orbitals * orbitals), F32),
        in_specs=[vmem] * 3,
        out_specs=pl.BlockSpec(memory_space=pltpu.HBM),
        scratch_shapes=[
            pltpu.VMEM((2, group * orbitals, 2 * kh), BF),
            pltpu.VMEM((count, rows, group * orbitals), F32),
            pltpu.SemaphoreType.DMA((count,)),
        ],
        compiler_params=pltpu.CompilerParams(vmem_limit_bytes=16 * 2**20),
        name="last_step",
    )(own, other, ket)


def permute(array, mask, count):
    return lax.ppermute(array, "pan", [(i, i ^ mask) for i in range(count)])


def added(*arrays):
    result = arrays[0].astype(F32)
    for array in arrays[1:]:
        result = result + array.astype(F32)
    return result.astype(BF)


def gather_small(mine, nothing, count):
    middle = mine.shape[0] // 2
    a, b = mine[:middle], mine[middle:]
    b_x = permute(b, 2, count)
    a_z = {s: permute(a, 4 * s, count) for s in (3, 2, 1)}
    b_pair = jnp.stack([b, b_x])
    b_z = {s: permute(b_pair, 4 * s, count) for s in (3, 2, 1)}
    near = jnp.stack([a, a_z[1], a_z[2], a_z[3]]) + nothing
    far = permute(near, 2, count)
    rest = jnp.stack([b_pair, b_z[1], b_z[2], b_z[3]])
    upper, lower = pl.ds(0, middle), pl.ds(middle, middle)
    everything = slice(None)
    parts, regions = [], []
    for x, part in ((0, near), (1, far)):
        for core in range(2):
            parts.append(permute(part, 1, count) if core else part)
            regions.append((core, everything, x, upper))
    for core in range(2):
        parts.append(permute(rest, 1, count) if core else rest)
        regions.append((core, everything, everything, lower))
    return parts, regions


def shards(
    count, blocks, first_block, second_block, slot_counts, ket_first, ket_second, coefficients, mo_index
):
    me = lax.axis_index("pan").astype(jnp.int32)
    core = me % 2
    me_array = me.reshape(1)
    capacity, kp, pair = blocks.shape
    kh = kp // 2
    own_ao, nmo = coefficients.shape
    swap = functools.partial(permute, mask=1, count=count)

    numbers = jnp.concatenate([first_block, second_block, slot_counts])
    other_numbers = swap(numbers)
    picks = (mo_index[:, None] == jnp.arange(nmo, dtype=jnp.int32)[None, :]).astype(BF)
    mine = lax.dot_general(
        picks, coefficients, (((1,), (1,)), ((), ())), preferred_element_type=F32
    ).astype(BF)
    orbitals = mine.shape[0]

    units = own_ao // 8
    factor = -(-(2**20) // max(units, 1))
    other = swap(blocks)

    small = count == 16 and own_ao % 16 == 0
    if small:
        nothing = (other_numbers[0] < 0).astype(BF)
        mine = jnp.pad(mine, ((0, 0), (0, -own_ao % LANES)))
        parts, regions = gather_small(mine, nothing, count)

        def locate(unit, me):
            owner = (unit * factor) >> 20
            away = owner ^ me
            return away & 1, away >> 2, (away >> 1) & 1, (unit - owner * units) * 8
    else:
        parts = [lax.all_gather(mine, "pan", axis=1, tiled=True)]
        regions = [(0, 0, 0)]

        def locate(unit, me):
            return 0, 0, 0, unit * 8

    bra = functools.partial(
        bra_transform,
        regions,
        locate,
        parts,
        blocks,
        other,
        (numbers, other_numbers),
        (ket_first, ket_second),
        me_array,
        orbitals,
    )

    if small:
        chunk, side = orbitals // 8, kh // 2
        order = ((3, 0, side), (2, 0, side), (3, side, kh), (2, side, kh), (1, 0, kh), (0, 0, kh))
        pieces = order + tuple((s + 4, a, b) for s, a, b in order)
        *partial, ket = bra(chunk, pieces, BF)
        there, here = partial[:6], partial[6:]
        three_a = added(here[0], permute(there[0], 2, count))
        two_a = added(here[1], permute(there[1], 2, count), permute(three_a, 4, count))
        three_b = added(here[2], permute(there[2], 2, count))
        nothing = (three_a[0, 0] != three_a[0, 0]).astype(BF)
        two_b = added(here[3], permute(there[3] + nothing, 2, count), permute(three_b, 4, count))
        one = permute(added(here[4], permute(there[4], 2, count)), 4, count)
        zero = permute(there[5] + nothing, 2, count)
        two = jnp.concatenate([permute(two_a, 8, count), permute(two_b, 8, count)], axis=1)
        done = added(here[5], zero, one, two)
    else:
        partial, ket = bra(orbitals, ((0, 0, kh),), F32)
        sides = [list(range(c, count, 2)) for c in range(2)]
        done = lax.psum_scatter(
            partial, "pan", scatter_dimension=0, tiled=True, axis_index_groups=sides
        ).astype(BF)
    rows = done.shape[0] // 2
    keep = lax.dynamic_slice_in_dim(done, core * rows, rows, axis=0)
    give = lax.dynamic_slice_in_dim(done, (1 - core) * rows, rows, axis=0)
    return last_step(keep, swap(give), ket)


def solution(mesh):
    placed = (
        P(("grp", "pan"), None, None),
        P(("grp", "pan")),
        P(("grp", "pan")),
        P(("grp", "pan")),
        P("grp"),
        P("grp"),
        P(("grp", "pan"), None),
        P("grp"),
    )
    return jax.shard_map(
        functools.partial(shards, mesh.shape["pan"]),
        mesh=mesh,
        in_specs=placed,
        out_specs=P(("grp", "pan"), None),
        check_vma=False,
    )
```

```python
import functools

import jax
import jax.numpy as jnp
from jax import lax
from jax.experimental import pallas as pl
from jax.experimental.pallas import tpu as pltpu
from jax.sharding import PartitionSpec as P

HALF = 16
STEP = 8
LANES = 128
BF = jnp.bfloat16
F32 = jnp.float32
VMEM_LIMIT = 51 * 2**20


def spread(kind):
    row = lax.broadcasted_iota(jnp.int32, (LANES, LANES), 0)
    col = lax.broadcasted_iota(jnp.int32, (LANES, LANES), 1)
    source = col // 8 if kind == "a" else col % 8
    return (row == source).astype(F32).astype(BF)


def table_piece(table, place, target):
    core, z, x, lane = place
    inside = lane & (LANES - 1)
    start = pl.multiple_of(lane - inside, LANES)
    piece = table[core, z, x, :, pl.ds(start, LANES)].astype(F32)
    return pltpu.roll(piece, (target - inside) & (LANES - 1), 1)


def load_table(regions, parts, table, sems):
    return [
        pltpu.make_async_copy(part, table.at[region], sems.at[n])
        for n, (region, part) in enumerate(zip(regions, parts))
    ]


def bra_kernel(regions, locate, chunk, pieces, me_ref, mine, theirs, firsts, seconds, *refs):
    parts, refs = refs[: len(regions)], refs[len(regions) :]
    own, other = refs[:2]
    outs, ket = refs[2 : 2 + len(pieces)], refs[2 + len(pieces)]
    table, blk, picked_a, wide_a, picked_b, wide_b, half, second, ready = refs[3 + len(pieces) : -3]
    table_sems, block_sems, out_sems = refs[-3:]
    orbitals = second.shape[1]
    capacity = own.shape[0]
    kh = blk.shape[1]
    me = me_ref[0]
    own_live, other_live = mine[2 * capacity], theirs[2 * capacity]
    k_start = pl.multiple_of((me & 1) * kh, LANES)
    live = own_live + other_live

    copies = load_table(regions, parts, table, table_sems)
    for copy in copies:
        copy.start()

    def start_own(n, carry):
        pltpu.make_async_copy(
            own.at[n, pl.ds(k_start, kh)], blk.at[n], block_sems.at[n // STEP]
        ).start()
        return carry

    def start_other(n, carry):
        pltpu.make_async_copy(
            other.at[n - own_live, pl.ds(k_start, kh)], blk.at[n], block_sems.at[n // STEP]
        ).start()
        return carry

    lax.fori_loop(0, own_live, start_own, 0)
    lax.fori_loop(own_live, live, start_other, 0)
    lanes = lax.broadcasted_iota(jnp.int32, (8, LANES), 1)
    diagonal = (lanes % 8 == lax.broadcasted_iota(jnp.int32, (8, LANES), 0)).astype(F32)
    empty = jnp.zeros((8, LANES), F32)
    spread_a = spread("a")
    groups = (live + HALF - 1) // HALF
    steps = (live + STEP - 1) // STEP
    second[...] = jnp.zeros_like(second)

    def number(n, column):
        ours = mine[column * capacity + jnp.minimum(n, own_live - 1)]
        partners = theirs[column * capacity + jnp.maximum(n - own_live, 0)]
        return jnp.where(n < own_live, ours, partners)

    for copy in copies:
        copy.wait()

    count = ket.shape[1]
    for n in range(count):
        kb = (n + (me & 1) * (count // 2)) & (count - 1)
        piece = table_piece(table, locate(firsts[kb] * 2, me), 0)
        ket[0, n] = jnp.dot(piece.astype(BF), spread_a, preferred_element_type=F32)
        piece = table_piece(table, locate(seconds[kb], me), 0)
        ket[1, n] = jnp.dot(piece.astype(BF), spread("b"), preferred_element_type=F32)

    cover = 8 * STEP
    wanted = lax.broadcasted_iota(jnp.int32, (orbitals, LANES), 1)
    place = (wanted & (cover - 1)) >> 3

    def slots_of(o):
        return [jnp.minimum(o * STEP + u, live - 1) for u in range(STEP)]

    def prepare(o, picked, wide):
        slots = slots_of(o)
        for u, n in enumerate(slots):
            piece = table_piece(table, locate(number(n, 0) * 2, me), 0)
            picked[u * orbitals : (u + 1) * orbitals] = piece.astype(BF)
        wide[...] = jnp.dot(picked[...], spread_a, preferred_element_type=F32)
        parity = o & (LANES // cover - 1)
        merged = jnp.zeros((orbitals, LANES), F32)
        for u, n in enumerate(slots):
            where = locate(number(n, 1), me)
            piece = table_piece(table, where, parity * cover + 8 * u)
            merged = jnp.where(place == u, piece, merged)
        keep = (wanted // cover == parity) & (o * STEP + place < live)
        at = o // (LANES // cover)
        second[at] = jnp.where(keep, merged, second[at])

    def products(o, wide):
        slots = slots_of(o)
        for p in range(STEP // 2):
            rows = []
            for i in range(orbitals):
                x, y = (
                    jnp.broadcast_to(wide[u * orbitals + i : u * orbitals + i + 1, :], (8, LANES))
                    * diagonal
                    for u in (2 * p, 2 * p + 1)
                )
                rows.append(jnp.concatenate([x, empty], axis=1))
                rows.append(jnp.concatenate([empty, y], axis=1))
            factor = jnp.concatenate(rows, axis=0).astype(BF)
            data = jnp.concatenate([blk[slots[2 * p]], blk[slots[2 * p + 1]]], axis=1)
            at = pl.multiple_of(o * cover + 16 * p, 16)
            part = orbitals // 2
            for h in range(2):
                result = lax.dot_general(
                    factor[h * part * 16 : (h + 1) * part * 16],
                    data,
                    (((1,), (1,)), ((), ())),
                    preferred_element_type=F32,
                )
                half[h * part : (h + 1) * part, pl.ds(at, 16), :] = result.astype(BF).reshape(
                    part, 16, kh
                )

    def do_step(o, now, later):
        def wait_one(n, carry):
            pltpu.make_async_copy(
                own.at[0, pl.ds(k_start, kh)], blk.at[n], block_sems.at[o]
            ).wait()
            return carry

        lax.fori_loop(o * STEP, jnp.minimum((o + 1) * STEP, live), wait_one, 0)
        prepare(jnp.minimum(o + 1, steps - 1), *later)
        products(o, now[1])

    def two_steps(h, carry):
        do_step(2 * h, (picked_a, wide_a), (picked_b, wide_b))

        @pl.when(2 * h + 1 < steps)
        def _():
            do_step(2 * h + 1, (picked_b, wide_b), (picked_a, wide_a))

        return carry

    prepare(0, picked_a, wide_a)
    lax.fori_loop(0, (steps + 1) // 2, two_steps, 0)

    def clear(o, carry):
        at = pl.multiple_of(o * 8 * STEP, 8 * STEP)
        half[:, pl.ds(at, 8 * STEP), :] = jnp.zeros((orbitals, 8 * STEP, kh), BF)
        return carry

    lax.fori_loop(steps, groups * (HALF // STEP), clear, 0)

    def leave(n):
        s, low, high = pieces[n]
        return pltpu.make_async_copy(
            ready.at[s, :, pl.ds(low, high - low)], outs[n], out_sems.at[n]
        )

    def finish(count):
        weights = jnp.concatenate([second[n] for n in range(count)], axis=1).astype(BF)
        for s in dict.fromkeys(piece[0] for piece in pieces):
            first = 0
            if len(pieces) > 1:
                first = ((me >> 2) ^ (s & 3)) * 2 * chunk + (((me >> 1) & 1) ^ (1 - (s >> 2))) * chunk
            for r in range(chunk):
                piece = half[first + r, 0 : 8 * HALF * count, :]
                ready[s, r * orbitals : (r + 1) * orbitals, :] = jnp.dot(
                    weights, piece, preferred_element_type=F32
                ).astype(ready.dtype)
            for n in range(len(pieces)):
                if pieces[n][0] == s:
                    leave(n).start()

    for count in range(1, half.shape[1] // (8 * HALF) + 1):
        pl.when(groups == count)(functools.partial(finish, count))
    for n in range(len(pieces)):
        leave(n).wait()


def bra_transform(
    regions, locate, parts, own, other, numbers, ket_numbers, me, orbitals, chunk, pieces, kind
):
    capacity, kp, pair = own.shape
    kh = kp // 2
    groups = -(-2 * capacity // HALF)
    rows = chunk * orbitals
    hbm = pl.BlockSpec(memory_space=pltpu.HBM)
    return pl.pallas_call(
        functools.partial(bra_kernel, regions, locate, chunk, pieces),
        out_shape=[jax.ShapeDtypeStruct((rows, high - low), kind) for _, low, high in pieces]
        + [jax.ShapeDtypeStruct((2, kp // LANES, orbitals, LANES), F32)],
        grid_spec=pltpu.PrefetchScalarGridSpec(
            num_scalar_prefetch=5,
            grid=(),
            in_specs=[hbm] * (len(parts) + 2),
            out_specs=[hbm] * len(pieces) + [pl.BlockSpec(memory_space=pltpu.VMEM)],
            scratch_shapes=[
                pltpu.VMEM(table_shape(parts, orbitals), BF),
                pltpu.VMEM((2 * capacity, kh, pair), BF),
                pltpu.VMEM((STEP * orbitals, LANES), BF),
                pltpu.VMEM((STEP * orbitals, LANES), F32),
                pltpu.VMEM((STEP * orbitals, LANES), BF),
                pltpu.VMEM((STEP * orbitals, LANES), F32),
                pltpu.VMEM((orbitals, 8 * HALF * groups, kh), BF),
                pltpu.VMEM((groups, orbitals, LANES), F32),
                pltpu.VMEM((orbitals // chunk, rows, kh), kind),
                pltpu.SemaphoreType.DMA((len(parts),)),
                pltpu.SemaphoreType.DMA((-(-2 * capacity // STEP),)),
                pltpu.SemaphoreType.DMA((len(pieces),)),
            ],
        ),
        compiler_params=pltpu.CompilerParams(vmem_limit_bytes=VMEM_LIMIT),
        cost_estimate=pl.CostEstimate(
            flops=4 * capacity * 8 * orbitals * pair * kh, bytes_accessed=8 * 2**20, transcendentals=0
        ),
        name="bra_transform",
    )(me, *numbers, *ket_numbers, *parts, own, other)


def table_shape(parts, orbitals):
    if len(parts) == 1:
        return (1, 1, 1, orbitals, parts[0].shape[-1])
    return (2, 4, 2, orbitals, parts[0].shape[-1])


def last_kernel(own, other, ket, out, tiles, results, sems):
    count, orbitals = ket.shape[1:3]
    group = tiles.shape[1] // orbitals
    half_rounded = jnp.concatenate([own[...], other[...]], axis=1)
    copies = []
    for t in range(orbitals // group):
        tile = tiles.at[t % 2]
        for n in range(count):
            last = ket[1, n]
            for r in range(group):
                row = jnp.broadcast_to(ket[0, n, t * group + r : t * group + r + 1, :], last.shape)
                tile[r * orbitals : (r + 1) * orbitals, n * LANES : (n + 1) * LANES] = (
                    row * last
                ).astype(BF)
        results[t] = lax.dot_general(
            half_rounded, tile[...], (((1,), (1,)), ((), ())), preferred_element_type=F32
        )
        columns = group * orbitals
        copies.append(
            pltpu.make_async_copy(
                results.at[t], out.at[:, pl.ds(t * columns, columns)], sems.at[t]
            )
        )
        copies[-1].start()
    for copy in copies:
        copy.wait()


def last_step(own, other, ket):
    rows, kh = own.shape
    orbitals = ket.shape[2]
    group = 8
    count = orbitals // group
    vmem = pl.BlockSpec(memory_space=pltpu.VMEM)
    return pl.pallas_call(
        last_kernel,
        out_shape=jax.ShapeDtypeStruct((rows, orbitals * orbitals), F32),
        in_specs=[vmem] * 3,
        out_specs=pl.BlockSpec(memory_space=pltpu.HBM),
        scratch_shapes=[
            pltpu.VMEM((2, group * orbitals, 2 * kh), BF),
            pltpu.VMEM((count, rows, group * orbitals), F32),
            pltpu.SemaphoreType.DMA((count,)),
        ],
        compiler_params=pltpu.CompilerParams(vmem_limit_bytes=16 * 2**20),
        name="last_step",
    )(own, other, ket)


def permute(array, mask, count):
    return lax.ppermute(array, "pan", [(i, i ^ mask) for i in range(count)])


def added(*arrays):
    result = arrays[0].astype(F32)
    for array in arrays[1:]:
        result = result + array.astype(F32)
    return result.astype(BF)


def gather_small(mine, count):
    middle = mine.shape[0] // 2
    a, b = mine[:middle], mine[middle:]
    b_x = permute(b, 2, count)
    a_z = {s: permute(a, 4 * s, count) for s in (3, 2, 1)}
    b_pair = jnp.stack([b, b_x])
    b_z = {s: permute(b_pair, 4 * s, count) for s in (3, 2, 1)}
    near = jnp.stack([a, a_z[1], a_z[2], a_z[3]])
    far = permute(near, 2, count)
    rest = jnp.stack([b_pair, b_z[1], b_z[2], b_z[3]])
    upper, lower = pl.ds(0, middle), pl.ds(middle, middle)
    everything = slice(None)
    parts, regions = [], []
    for x, part in ((0, near), (1, far)):
        for core in range(2):
            parts.append(permute(part, 1, count) if core else part)
            regions.append((core, everything, x, upper))
    for core in range(2):
        parts.append(permute(rest, 1, count) if core else rest)
        regions.append((core, everything, everything, lower))
    return parts, regions


def shards(
    count, blocks, first_block, second_block, slot_counts, ket_first, ket_second, coefficients, mo_index
):
    me = lax.axis_index("pan").astype(jnp.int32)
    core = me % 2
    me_array = me.reshape(1)
    capacity, kp, pair = blocks.shape
    kh = kp // 2
    own_ao, nmo = coefficients.shape
    swap = functools.partial(permute, mask=1, count=count)

    numbers = jnp.concatenate([first_block, second_block, slot_counts])
    other_numbers = swap(numbers)
    nothing = (other_numbers[0] < 0).astype(BF)
    mine = coefficients.T.at[mo_index].get(mode="promise_in_bounds") + nothing
    orbitals = mine.shape[0]

    units = own_ao // 8
    factor = -(-(2**20) // max(units, 1))
    other = swap(blocks)

    small = count == 16 and own_ao % 16 == 0
    if small:
        mine = jnp.pad(mine, ((0, 0), (0, -own_ao % LANES)))
        parts, regions = gather_small(mine, count)

        def locate(unit, me):
            owner = (unit * factor) >> 20
            away = owner ^ me
            return away & 1, away >> 2, (away >> 1) & 1, (unit - owner * units) * 8
    else:
        parts = [lax.all_gather(mine, "pan", axis=1, tiled=True)]
        regions = [(0, 0, 0)]

        def locate(unit, me):
            return 0, 0, 0, unit * 8

    bra = functools.partial(
        bra_transform,
        regions,
        locate,
        parts,
        blocks,
        other,
        (numbers, other_numbers),
        (ket_first, ket_second),
        me_array,
        orbitals,
    )

    if small:
        chunk, side = orbitals // 8, kh // 2
        order = ((3, 0, side), (2, 0, side), (3, side, kh), (2, side, kh), (1, 0, kh), (0, 0, kh))
        pieces = order + tuple((s + 4, a, b) for s, a, b in order)
        *partial, ket = bra(chunk, pieces, BF)
        there, here = partial[:6], partial[6:]
        three_a = added(here[0], permute(there[0], 2, count))
        two_a = added(here[1], permute(there[1], 2, count), permute(three_a, 4, count))
        three_b = added(here[2], permute(there[2], 2, count))
        nothing = (three_a[0, 0] != three_a[0, 0]).astype(BF)
        two_b = added(here[3], permute(there[3] + nothing, 2, count), permute(three_b, 4, count))
        one = permute(added(here[4], permute(there[4], 2, count)), 4, count)
        zero = permute(there[5] + nothing, 2, count)
        two = jnp.concatenate([permute(two_a, 8, count), permute(two_b, 8, count)], axis=1)
        done = added(here[5], zero, one, two)
    else:
        partial, ket = bra(orbitals, ((0, 0, kh),), F32)
        sides = [list(range(c, count, 2)) for c in range(2)]
        done = lax.psum_scatter(
            partial, "pan", scatter_dimension=0, tiled=True, axis_index_groups=sides
        ).astype(BF)
    rows = done.shape[0] // 2
    keep = lax.dynamic_slice_in_dim(done, core * rows, rows, axis=0)
    give = lax.dynamic_slice_in_dim(done, (1 - core) * rows, rows, axis=0)
    return last_step(keep, swap(give), ket)


def solution(mesh):
    placed = (
        P(("grp", "pan"), None, None),
        P(("grp", "pan")),
        P(("grp", "pan")),
        P(("grp", "pan")),
        P("grp"),
        P("grp"),
        P(("grp", "pan"), None),
        P("grp"),
    )
    return jax.shard_map(
        functools.partial(shards, mesh.shape["pan"]),
        mesh=mesh,
        in_specs=placed,
        out_specs=P(("grp", "pan"), None),
        check_vma=False,
    )
```

```python
import functools

import jax
import jax.numpy as jnp
from jax import lax
from jax.experimental import pallas as pl
from jax.experimental.pallas import tpu as pltpu
from jax.sharding import PartitionSpec as P

HALF = 16
STEP = 8
LANES = 128
BF = jnp.bfloat16
F32 = jnp.float32
VMEM_LIMIT = 51 * 2**20


def spread(kind):
    row = lax.broadcasted_iota(jnp.int32, (LANES, LANES), 0)
    col = lax.broadcasted_iota(jnp.int32, (LANES, LANES), 1)
    source = col // 8 if kind == "a" else col % 8
    return (row == source).astype(F32).astype(BF)


def table_piece(table, place, target):
    core, z, x, lane = place
    inside = lane & (LANES - 1)
    start = pl.multiple_of(lane - inside, LANES)
    piece = table[core, z, x, :, pl.ds(start, LANES)].astype(F32)
    return pltpu.roll(piece, (target - inside) & (LANES - 1), 1)


def load_table(regions, parts, table, sems):
    return [
        pltpu.make_async_copy(part, table.at[region], sems.at[n])
        for n, (region, part) in enumerate(zip(regions, parts))
    ]


def bra_kernel(regions, locate, chunk, pieces, me_ref, mine, theirs, *refs):
    parts, refs = refs[: len(regions)], refs[len(regions) :]
    own, other = refs[:2]
    outs, ket = refs[2 : 2 + len(pieces)], refs[2 + len(pieces)]
    table, blk, picked_a, wide_a, picked_b, wide_b, half, second, ready = refs[3 + len(pieces) : -3]
    table_sems, block_sems, out_sems = refs[-3:]
    orbitals = second.shape[1]
    capacity = own.shape[0]
    kh = blk.shape[1]
    me = me_ref[0]
    own_live, other_live = mine[2 * capacity], theirs[2 * capacity]
    k_start = pl.multiple_of((me & 1) * kh, LANES)
    live = own_live + other_live

    copies = load_table(regions, parts, table, table_sems)
    for copy in copies:
        copy.start()

    def start_own(n, carry):
        pltpu.make_async_copy(
            own.at[n, pl.ds(k_start, kh)], blk.at[n], block_sems.at[n // STEP]
        ).start()
        return carry

    def start_other(n, carry):
        pltpu.make_async_copy(
            other.at[n - own_live, pl.ds(k_start, kh)], blk.at[n], block_sems.at[n // STEP]
        ).start()
        return carry

    lax.fori_loop(0, own_live, start_own, 0)
    lax.fori_loop(own_live, live, start_other, 0)
    lanes = lax.broadcasted_iota(jnp.int32, (8, LANES), 1)
    diagonal = (lanes % 8 == lax.broadcasted_iota(jnp.int32, (8, LANES), 0)).astype(F32)
    empty = jnp.zeros((8, LANES), F32)
    spread_a = spread("a")
    groups = (live + HALF - 1) // HALF
    steps = (live + STEP - 1) // STEP
    second[...] = jnp.zeros_like(second)

    def number(n, column):
        ours = mine[column * capacity + jnp.minimum(n, own_live - 1)]
        partners = theirs[column * capacity + jnp.maximum(n - own_live, 0)]
        return jnp.where(n < own_live, ours, partners)

    for copy in copies:
        copy.wait()

    count = ket.shape[1]
    for n in range(count):
        kb = (n + (me & 1) * (count // 2)) & (count - 1)
        piece = table_piece(table, locate(mine[2 * capacity + 1 + kb] * 2, me), 0)
        ket[0, n] = jnp.dot(piece.astype(BF), spread_a, preferred_element_type=F32)
        piece = table_piece(table, locate(mine[2 * capacity + 1 + count + kb], me), 0)
        ket[1, n] = jnp.dot(piece.astype(BF), spread("b"), preferred_element_type=F32)

    cover = 8 * STEP
    wanted = lax.broadcasted_iota(jnp.int32, (orbitals, LANES), 1)
    place = (wanted & (cover - 1)) >> 3

    def slots_of(o):
        return [jnp.minimum(o * STEP + u, live - 1) for u in range(STEP)]

    def prepare(o, picked, wide):
        slots = slots_of(o)
        for u, n in enumerate(slots):
            piece = table_piece(table, locate(number(n, 0) * 2, me), 0)
            picked[u * orbitals : (u + 1) * orbitals] = piece.astype(BF)
        wide[...] = jnp.dot(picked[...], spread_a, preferred_element_type=F32)
        parity = o & (LANES // cover - 1)
        merged = jnp.zeros((orbitals, LANES), F32)
        for u, n in enumerate(slots):
            where = locate(number(n, 1), me)
            piece = table_piece(table, where, parity * cover + 8 * u)
            merged = jnp.where(place == u, piece, merged)
        keep = (wanted // cover == parity) & (o * STEP + place < live)
        at = o // (LANES // cover)
        second[at] = jnp.where(keep, merged, second[at])

    def products(o, wide):
        slots = slots_of(o)
        for p in range(STEP // 2):
            rows = []
            for i in range(orbitals):
                x, y = (
                    jnp.broadcast_to(wide[u * orbitals + i : u * orbitals + i + 1, :], (8, LANES))
                    * diagonal
                    for u in (2 * p, 2 * p + 1)
                )
                rows.append(jnp.concatenate([x, empty], axis=1))
                rows.append(jnp.concatenate([empty, y], axis=1))
            factor = jnp.concatenate(rows, axis=0).astype(BF)
            data = jnp.concatenate([blk[slots[2 * p]], blk[slots[2 * p + 1]]], axis=1)
            at = pl.multiple_of(o * cover + 16 * p, 16)
            part = orbitals // 2
            for h in range(2):
                result = lax.dot_general(
                    factor[h * part * 16 : (h + 1) * part * 16],
                    data,
                    (((1,), (1,)), ((), ())),
                    preferred_element_type=F32,
                )
                half[h * part : (h + 1) * part, pl.ds(at, 16), :] = result.astype(BF).reshape(
                    part, 16, kh
                )

    def do_step(o, now, later):
        def wait_one(n, carry):
            pltpu.make_async_copy(
                own.at[0, pl.ds(k_start, kh)], blk.at[n], block_sems.at[o]
            ).wait()
            return carry

        lax.fori_loop(o * STEP, jnp.minimum((o + 1) * STEP, live), wait_one, 0)
        prepare(jnp.minimum(o + 1, steps - 1), *later)
        products(o, now[1])

    def two_steps(h, carry):
        do_step(2 * h, (picked_a, wide_a), (picked_b, wide_b))

        @pl.when(2 * h + 1 < steps)
        def _():
            do_step(2 * h + 1, (picked_b, wide_b), (picked_a, wide_a))

        return carry

    prepare(0, picked_a, wide_a)
    lax.fori_loop(0, (steps + 1) // 2, two_steps, 0)

    def clear(o, carry):
        at = pl.multiple_of(o * 8 * STEP, 8 * STEP)
        half[:, pl.ds(at, 8 * STEP), :] = jnp.zeros((orbitals, 8 * STEP, kh), BF)
        return carry

    lax.fori_loop(steps, groups * (HALF // STEP), clear, 0)

    def leave(n):
        s, low, high = pieces[n]
        return pltpu.make_async_copy(
            ready.at[s, :, pl.ds(low, high - low)], outs[n], out_sems.at[n]
        )

    def finish(count):
        weights = jnp.concatenate([second[n] for n in range(count)], axis=1).astype(BF)
        for s in dict.fromkeys(piece[0] for piece in pieces):
            first = 0
            if len(pieces) > 1:
                first = ((me >> 2) ^ (s & 3)) * 2 * chunk + (((me >> 1) & 1) ^ (1 - (s >> 2))) * chunk
            for r in range(chunk):
                piece = half[first + r, 0 : 8 * HALF * count, :]
                ready[s, r * orbitals : (r + 1) * orbitals, :] = jnp.dot(
                    weights, piece, preferred_element_type=F32
                ).astype(ready.dtype)
            for n in range(len(pieces)):
                if pieces[n][0] == s:
                    leave(n).start()

    for count in range(1, half.shape[1] // (8 * HALF) + 1):
        pl.when(groups == count)(functools.partial(finish, count))
    for n in range(len(pieces)):
        leave(n).wait()


def bra_transform(
    regions, locate, parts, own, other, numbers, me, orbitals, chunk, pieces, kind
):
    capacity, kp, pair = own.shape
    kh = kp // 2
    groups = -(-2 * capacity // HALF)
    rows = chunk * orbitals
    hbm = pl.BlockSpec(memory_space=pltpu.HBM)
    return pl.pallas_call(
        functools.partial(bra_kernel, regions, locate, chunk, pieces),
        out_shape=[jax.ShapeDtypeStruct((rows, high - low), kind) for _, low, high in pieces]
        + [jax.ShapeDtypeStruct((2, kp // LANES, orbitals, LANES), F32)],
        grid_spec=pltpu.PrefetchScalarGridSpec(
            num_scalar_prefetch=3,
            grid=(),
            in_specs=[hbm] * (len(parts) + 2),
            out_specs=[hbm] * len(pieces) + [pl.BlockSpec(memory_space=pltpu.VMEM)],
            scratch_shapes=[
                pltpu.VMEM(table_shape(parts, orbitals), BF),
                pltpu.VMEM((2 * capacity, kh, pair), BF),
                pltpu.VMEM((STEP * orbitals, LANES), BF),
                pltpu.VMEM((STEP * orbitals, LANES), F32),
                pltpu.VMEM((STEP * orbitals, LANES), BF),
                pltpu.VMEM((STEP * orbitals, LANES), F32),
                pltpu.VMEM((orbitals, 8 * HALF * groups, kh), BF),
                pltpu.VMEM((groups, orbitals, LANES), F32),
                pltpu.VMEM((orbitals // chunk, rows, kh), kind),
                pltpu.SemaphoreType.DMA((len(parts),)),
                pltpu.SemaphoreType.DMA((-(-2 * capacity // STEP),)),
                pltpu.SemaphoreType.DMA((len(pieces),)),
            ],
        ),
        compiler_params=pltpu.CompilerParams(vmem_limit_bytes=VMEM_LIMIT),
        cost_estimate=pl.CostEstimate(
            flops=4 * capacity * 8 * orbitals * pair * kh, bytes_accessed=8 * 2**20, transcendentals=0
        ),
        name="bra_transform",
    )(me, *numbers, *parts, own, other)


def table_shape(parts, orbitals):
    if len(parts) == 1:
        return (1, 1, 1, orbitals, parts[0].shape[-1])
    return (2, 4, 2, orbitals, parts[0].shape[-1])


def last_kernel(own, other, ket, out, tiles, results, sems):
    count, orbitals = ket.shape[1:3]
    group = tiles.shape[1] // orbitals
    half_rounded = jnp.concatenate([own[...], other[...]], axis=1)
    copies = []
    for t in range(orbitals // group):
        tile = tiles.at[t % 2]
        for n in range(count):
            last = ket[1, n]
            for r in range(group):
                row = jnp.broadcast_to(ket[0, n, t * group + r : t * group + r + 1, :], last.shape)
                tile[r * orbitals : (r + 1) * orbitals, n * LANES : (n + 1) * LANES] = (
                    row * last
                ).astype(BF)
        results[t] = lax.dot_general(
            half_rounded, tile[...], (((1,), (1,)), ((), ())), preferred_element_type=F32
        )
        columns = group * orbitals
        copies.append(
            pltpu.make_async_copy(
                results.at[t], out.at[:, pl.ds(t * columns, columns)], sems.at[t]
            )
        )
        copies[-1].start()
    for copy in copies:
        copy.wait()


def last_step(own, other, ket):
    rows, kh = own.shape
    orbitals = ket.shape[2]
    group = 8
    count = orbitals // group
    vmem = pl.BlockSpec(memory_space=pltpu.VMEM)
    return pl.pallas_call(
        last_kernel,
        out_shape=jax.ShapeDtypeStruct((rows, orbitals * orbitals), F32),
        in_specs=[vmem] * 3,
        out_specs=pl.BlockSpec(memory_space=pltpu.HBM),
        scratch_shapes=[
            pltpu.VMEM((2, group * orbitals, 2 * kh), BF),
            pltpu.VMEM((count, rows, group * orbitals), F32),
            pltpu.SemaphoreType.DMA((count,)),
        ],
        compiler_params=pltpu.CompilerParams(vmem_limit_bytes=16 * 2**20),
        name="last_step",
    )(own, other, ket)


def permute(array, mask, count):
    return lax.ppermute(array, "pan", [(i, i ^ mask) for i in range(count)])


def added(*arrays):
    result = arrays[0].astype(F32)
    for array in arrays[1:]:
        result = result + array.astype(F32)
    return result.astype(BF)


def gather_small(mine, numbers, other, count):
    middle = mine.shape[0] // 2
    a, b = mine[:middle], mine[middle:]
    b_x = permute(b, 2, count)
    a_z = {s: permute(a, 4 * s, count) for s in (3, 2, 1)}
    b_pair = jnp.stack([b, b_x])
    b_z = {s: permute(b_pair, 4 * s, count) for s in (3, 2, 1)}
    near = jnp.stack([a, a_z[1], a_z[2], a_z[3]])
    far = permute(near, 2, count)
    late = (other[0, 0, 0] != other[0, 0, 0]).astype(jnp.int32)
    other_numbers = permute(numbers + late, 1, count)
    nothing = (other_numbers[0] < 0).astype(BF)
    rest = jnp.stack([b_pair, b_z[1], b_z[2], b_z[3]]) + nothing
    upper, lower = pl.ds(0, middle), pl.ds(middle, middle)
    everything = slice(None)
    parts, regions = [], []
    for x, part in ((0, near), (1, far)):
        for core in range(2):
            parts.append(permute(part, 1, count) if core else part)
            regions.append((core, everything, x, upper))
    for core in range(2):
        parts.append(permute(rest, 1, count) if core else rest)
        regions.append((core, everything, everything, lower))
    return parts, regions, other_numbers


def shards(
    count, blocks, first_block, second_block, slot_counts, ket_first, ket_second, coefficients, mo_index
):
    me = lax.axis_index("pan").astype(jnp.int32)
    core = me % 2
    me_array = me.reshape(1)
    capacity, kp, pair = blocks.shape
    kh = kp // 2
    own_ao, nmo = coefficients.shape
    swap = functools.partial(permute, mask=1, count=count)

    numbers = jnp.concatenate([first_block, second_block, slot_counts, ket_first, ket_second])
    mine = coefficients.T.at[mo_index].get(
        mode="promise_in_bounds", wrap_negative_indices=False
    )
    orbitals = mine.shape[0]

    units = own_ao // 8
    factor = -(-(2**20) // max(units, 1))
    other = swap(blocks)

    small = count == 16 and own_ao % 16 == 0
    if small:
        mine = jnp.pad(mine, ((0, 0), (0, -own_ao % LANES)))
        parts, regions, other_numbers = gather_small(mine, numbers, other, count)

        def locate(unit, me):
            owner = (unit * factor) >> 20
            away = owner ^ me
            return away & 1, away >> 2, (away >> 1) & 1, (unit - owner * units) * 8
    else:
        other_numbers = swap(numbers)
        parts = [lax.all_gather(mine, "pan", axis=1, tiled=True)]
        regions = [(0, 0, 0)]

        def locate(unit, me):
            return 0, 0, 0, unit * 8

    bra = functools.partial(
        bra_transform,
        regions,
        locate,
        parts,
        blocks,
        other,
        (numbers, other_numbers),
        me_array,
        orbitals,
    )

    if small:
        chunk, side = orbitals // 8, kh // 2
        order = ((3, 0, side), (2, 0, side), (3, side, kh), (2, side, kh), (1, 0, kh), (0, 0, kh))
        pieces = order + tuple((s + 4, a, b) for s, a, b in order)
        *partial, ket = bra(chunk, pieces, BF)
        there, here = partial[:6], partial[6:]
        three_a = added(here[0], permute(there[0], 2, count))
        two_a = added(here[1], permute(there[1], 2, count), permute(three_a, 4, count))
        three_b = added(here[2], permute(there[2], 2, count))
        nothing = (three_a[0, 0] != three_a[0, 0]).astype(BF)
        two_b = added(here[3], permute(there[3] + nothing, 2, count), permute(three_b, 4, count))
        one = permute(added(here[4], permute(there[4], 2, count)), 4, count)
        zero = permute(there[5] + nothing, 2, count)
        two = jnp.concatenate([permute(two_a, 8, count), permute(two_b, 8, count)], axis=1)
        done = added(here[5], zero, one, two)
    else:
        partial, ket = bra(orbitals, ((0, 0, kh),), F32)
        sides = [list(range(c, count, 2)) for c in range(2)]
        done = lax.psum_scatter(
            partial, "pan", scatter_dimension=0, tiled=True, axis_index_groups=sides
        ).astype(BF)
    rows = done.shape[0] // 2
    keep = lax.dynamic_slice_in_dim(done, core * rows, rows, axis=0)
    give = lax.dynamic_slice_in_dim(done, (1 - core) * rows, rows, axis=0)
    return last_step(keep, swap(give), ket)


def solution(mesh):
    placed = (
        P(("grp", "pan"), None, None),
        P(("grp", "pan")),
        P(("grp", "pan")),
        P(("grp", "pan")),
        P("grp"),
        P("grp"),
        P(("grp", "pan"), None),
        P("grp"),
    )
    return jax.shard_map(
        functools.partial(shards, mesh.shape["pan"]),
        mesh=mesh,
        in_specs=placed,
        out_specs=P(("grp", "pan"), None),
        check_vma=False,
    )
```

```python
import functools

import jax
import jax.numpy as jnp
from jax import lax
from jax.experimental import pallas as pl
from jax.experimental.pallas import tpu as pltpu
from jax.sharding import PartitionSpec as P

HALF = 16
STEP = 8
LANES = 128
BF = jnp.bfloat16
F32 = jnp.float32
VMEM_LIMIT = 51 * 2**20


def spread(kind):
    row = lax.broadcasted_iota(jnp.int32, (LANES, LANES), 0)
    col = lax.broadcasted_iota(jnp.int32, (LANES, LANES), 1)
    source = col // 8 if kind == "a" else col % 8
    return (row == source).astype(F32).astype(BF)


def table_piece(table, place, target):
    core, z, x, lane = place
    inside = lane & (LANES - 1)
    start = pl.multiple_of(lane - inside, LANES)
    piece = table[core, z, x, :, pl.ds(start, LANES)].astype(F32)
    return pltpu.roll(piece, (target - inside) & (LANES - 1), 1)


def load_table(regions, parts, table, sems):
    return [
        pltpu.make_async_copy(part, table.at[region], sems.at[n])
        for n, (region, part) in enumerate(zip(regions, parts))
    ]


def bra_kernel(regions, locate, chunk, pieces, me_ref, mine, theirs, *refs):
    parts, refs = refs[: len(regions)], refs[len(regions) :]
    own, other = refs[:2]
    outs, ket = refs[2 : 2 + len(pieces)], refs[2 + len(pieces)]
    table, blk, picked_a, wide_a, picked_b, wide_b, half, second, ready = refs[3 + len(pieces) : -3]
    table_sems, block_sems, out_sems = refs[-3:]
    orbitals = second.shape[1]
    capacity = own.shape[0]
    kh = blk.shape[1]
    me = me_ref[0]
    own_live, other_live = mine[2 * capacity], theirs[2 * capacity]
    k_start = pl.multiple_of((me & 1) * kh, LANES)
    live = own_live + other_live

    copies = load_table(regions, parts, table, table_sems)
    for copy in copies:
        copy.start()

    def start_own(n, carry):
        pltpu.make_async_copy(
            own.at[n, pl.ds(k_start, kh)], blk.at[n], block_sems.at[n // STEP]
        ).start()
        return carry

    def start_other(n, carry):
        pltpu.make_async_copy(
            other.at[n - own_live, pl.ds(k_start, kh)], blk.at[n], block_sems.at[n // STEP]
        ).start()
        return carry

    lax.fori_loop(0, own_live, start_own, 0)
    lax.fori_loop(own_live, live, start_other, 0)
    lanes = lax.broadcasted_iota(jnp.int32, (8, LANES), 1)
    diagonal = (lanes % 8 == lax.broadcasted_iota(jnp.int32, (8, LANES), 0)).astype(F32)
    empty = jnp.zeros((8, LANES), F32)
    spread_a = spread("a")
    groups = (live + HALF - 1) // HALF
    steps = (live + STEP - 1) // STEP
    second[...] = jnp.zeros_like(second)

    def number(n, column):
        ours = mine[column * capacity + jnp.minimum(n, own_live - 1)]
        partners = theirs[column * capacity + jnp.maximum(n - own_live, 0)]
        return jnp.where(n < own_live, ours, partners)

    for copy in copies:
        copy.wait()

    count = ket.shape[1]
    for n in range(count):
        kb = (n + (me & 1) * (count // 2)) & (count - 1)
        piece = table_piece(table, locate(mine[2 * capacity + 1 + kb] * 2, me), 0)
        ket[0, n] = jnp.dot(piece.astype(BF), spread_a, preferred_element_type=F32)
        piece = table_piece(table, locate(mine[2 * capacity + 1 + count + kb], me), 0)
        ket[1, n] = jnp.dot(piece.astype(BF), spread("b"), preferred_element_type=F32)

    cover = 8 * STEP
    wanted = lax.broadcasted_iota(jnp.int32, (orbitals, LANES), 1)
    place = (wanted & (cover - 1)) >> 3

    def slots_of(o):
        return [jnp.minimum(o * STEP + u, live - 1) for u in range(STEP)]

    def prepare(o, picked, wide):
        slots = slots_of(o)
        for u, n in enumerate(slots):
            piece = table_piece(table, locate(number(n, 0) * 2, me), 0)
            picked[u * orbitals : (u + 1) * orbitals] = piece.astype(BF)
        wide[...] = jnp.dot(picked[...], spread_a, preferred_element_type=F32)
        parity = o & (LANES // cover - 1)
        merged = jnp.zeros((orbitals, LANES), F32)
        for u, n in enumerate(slots):
            where = locate(number(n, 1), me)
            piece = table_piece(table, where, parity * cover + 8 * u)
            merged = jnp.where(place == u, piece, merged)
        keep = (wanted // cover == parity) & (o * STEP + place < live)
        at = o // (LANES // cover)
        second[at] = jnp.where(keep, merged, second[at])

    def products(o, wide):
        slots = slots_of(o)
        for p in range(STEP // 2):
            rows = []
            for i in range(orbitals):
                x, y = (
                    jnp.broadcast_to(wide[u * orbitals + i : u * orbitals + i + 1, :], (8, LANES))
                    * diagonal
                    for u in (2 * p, 2 * p + 1)
                )
                rows.append(jnp.concatenate([x, empty], axis=1))
                rows.append(jnp.concatenate([empty, y], axis=1))
            factor = jnp.concatenate(rows, axis=0).astype(BF)
            data = jnp.concatenate([blk[slots[2 * p]], blk[slots[2 * p + 1]]], axis=1)
            at = pl.multiple_of(o * cover + 16 * p, 16)
            part = orbitals // 2
            for h in range(2):
                result = lax.dot_general(
                    factor[h * part * 16 : (h + 1) * part * 16],
                    data,
                    (((1,), (1,)), ((), ())),
                    preferred_element_type=F32,
                )
                half[h * part : (h + 1) * part, pl.ds(at, 16), :] = result.astype(BF).reshape(
                    part, 16, kh
                )

    def do_step(o, now, later):
        def wait_one(n, carry):
            pltpu.make_async_copy(
                own.at[0, pl.ds(k_start, kh)], blk.at[n], block_sems.at[o]
            ).wait()
            return carry

        lax.fori_loop(o * STEP, jnp.minimum((o + 1) * STEP, live), wait_one, 0)
        prepare(jnp.minimum(o + 1, steps - 1), *later)
        products(o, now[1])

    def two_steps(h, carry):
        do_step(2 * h, (picked_a, wide_a), (picked_b, wide_b))

        @pl.when(2 * h + 1 < steps)
        def _():
            do_step(2 * h + 1, (picked_b, wide_b), (picked_a, wide_a))

        return carry

    prepare(0, picked_a, wide_a)
    lax.fori_loop(0, (steps + 1) // 2, two_steps, 0)

    def clear(o, carry):
        at = pl.multiple_of(o * 8 * STEP, 8 * STEP)
        half[:, pl.ds(at, 8 * STEP), :] = jnp.zeros((orbitals, 8 * STEP, kh), BF)
        return carry

    lax.fori_loop(steps, groups * (HALF // STEP), clear, 0)

    def leave(n):
        s, low, high = pieces[n]
        return pltpu.make_async_copy(
            ready.at[s, :, pl.ds(low, high - low)], outs[n], out_sems.at[n]
        )

    def finish(count):
        weights = jnp.concatenate([second[n] for n in range(count)], axis=1).astype(BF)
        for s in dict.fromkeys(piece[0] for piece in pieces):
            first = 0
            if len(pieces) > 1:
                first = ((me >> 2) ^ (s & 3)) * 2 * chunk + (((me >> 1) & 1) ^ (1 - (s >> 2))) * chunk
            for r in range(chunk):
                piece = half[first + r, 0 : 8 * HALF * count, :]
                ready[s, r * orbitals : (r + 1) * orbitals, :] = jnp.dot(
                    weights, piece, preferred_element_type=F32
                ).astype(ready.dtype)
            for n in range(len(pieces)):
                if pieces[n][0] == s:
                    leave(n).start()

    for count in range(1, half.shape[1] // (8 * HALF) + 1):
        pl.when(groups == count)(functools.partial(finish, count))
    for n in range(len(pieces)):
        leave(n).wait()


def bra_transform(
    regions, locate, parts, own, other, numbers, me, orbitals, chunk, pieces, kind
):
    capacity, kp, pair = own.shape
    kh = kp // 2
    groups = -(-2 * capacity // HALF)
    rows = chunk * orbitals
    hbm = pl.BlockSpec(memory_space=pltpu.HBM)
    return pl.pallas_call(
        functools.partial(bra_kernel, regions, locate, chunk, pieces),
        out_shape=[jax.ShapeDtypeStruct((rows, high - low), kind) for _, low, high in pieces]
        + [jax.ShapeDtypeStruct((2, kp // LANES, orbitals, LANES), F32)],
        grid_spec=pltpu.PrefetchScalarGridSpec(
            num_scalar_prefetch=3,
            grid=(),
            in_specs=[hbm] * (len(parts) + 2),
            out_specs=[hbm] * len(pieces) + [pl.BlockSpec(memory_space=pltpu.VMEM)],
            scratch_shapes=[
                pltpu.VMEM(table_shape(parts, orbitals), BF),
                pltpu.VMEM((2 * capacity, kh, pair), BF),
                pltpu.VMEM((STEP * orbitals, LANES), BF),
                pltpu.VMEM((STEP * orbitals, LANES), F32),
                pltpu.VMEM((STEP * orbitals, LANES), BF),
                pltpu.VMEM((STEP * orbitals, LANES), F32),
                pltpu.VMEM((orbitals, 8 * HALF * groups, kh), BF),
                pltpu.VMEM((groups, orbitals, LANES), F32),
                pltpu.VMEM((orbitals // chunk, rows, kh), kind),
                pltpu.SemaphoreType.DMA((len(parts),)),
                pltpu.SemaphoreType.DMA((-(-2 * capacity // STEP),)),
                pltpu.SemaphoreType.DMA((len(pieces),)),
            ],
        ),
        compiler_params=pltpu.CompilerParams(vmem_limit_bytes=VMEM_LIMIT),
        cost_estimate=pl.CostEstimate(
            flops=4 * capacity * 8 * orbitals * pair * kh, bytes_accessed=8 * 2**20, transcendentals=0
        ),
        name="bra_transform",
    )(me, *numbers, *parts, own, other)


def table_shape(parts, orbitals):
    if len(parts) == 1:
        return (1, 1, 1, orbitals, parts[0].shape[-1])
    return (2, 4, 2, orbitals, parts[0].shape[-1])


def last_kernel(own, other, ket, out, tiles, results, sems):
    count, orbitals = ket.shape[1:3]
    group = tiles.shape[1] // orbitals
    half_rounded = jnp.concatenate([own[...], other[...]], axis=1)
    copies = []
    for t in range(orbitals // group):
        tile = tiles.at[t % 2]
        for n in range(count):
            last = ket[1, n]
            for r in range(group):
                row = jnp.broadcast_to(ket[0, n, t * group + r : t * group + r + 1, :], last.shape)
                tile[r * orbitals : (r + 1) * orbitals, n * LANES : (n + 1) * LANES] = (
                    row * last
                ).astype(BF)
        results[t] = lax.dot_general(
            half_rounded, tile[...], (((1,), (1,)), ((), ())), preferred_element_type=F32
        )
        columns = group * orbitals
        copies.append(
            pltpu.make_async_copy(
                results.at[t], out.at[:, pl.ds(t * columns, columns)], sems.at[t]
            )
        )
        copies[-1].start()
    for copy in copies:
        copy.wait()


def last_step(own, other, ket):
    rows, kh = own.shape
    orbitals = ket.shape[2]
    group = 8
    count = orbitals // group
    vmem = pl.BlockSpec(memory_space=pltpu.VMEM)
    return pl.pallas_call(
        last_kernel,
        out_shape=jax.ShapeDtypeStruct((rows, orbitals * orbitals), F32),
        in_specs=[vmem] * 3,
        out_specs=pl.BlockSpec(memory_space=pltpu.HBM),
        scratch_shapes=[
            pltpu.VMEM((2, group * orbitals, 2 * kh), BF),
            pltpu.VMEM((count, rows, group * orbitals), F32),
            pltpu.SemaphoreType.DMA((count,)),
        ],
        compiler_params=pltpu.CompilerParams(vmem_limit_bytes=16 * 2**20),
        name="last_step",
    )(own, other, ket)


def permute(array, mask, count):
    return lax.ppermute(array, "pan", [(i, i ^ mask) for i in range(count)])


def added(*arrays):
    result = arrays[0].astype(F32)
    for array in arrays[1:]:
        result = result + array.astype(F32)
    return result.astype(BF)


def gather_small(mine, numbers, other, count):
    middle = mine.shape[0] // 2
    a, b = mine[:middle], mine[middle:]
    b_x = permute(b, 2, count)
    a_z = {s: permute(a, 4 * s, count) for s in (3, 2, 1)}
    b_pair = jnp.stack([b, b_x])
    b_z = {s: permute(b_pair, 4 * s, count) for s in (3, 2, 1)}
    near = jnp.stack([a, a_z[1], a_z[2], a_z[3]])
    far = permute(near, 2, count)
    line = other[0, 0, : numbers.shape[0]]
    late = (line != line).astype(jnp.int32)
    other_numbers = permute(numbers + late, 1, count)
    nothing = (other_numbers[0] < 0).astype(BF)
    rest = jnp.stack([b_pair, b_z[1], b_z[2], b_z[3]]) + nothing
    upper, lower = pl.ds(0, middle), pl.ds(middle, middle)
    everything = slice(None)
    parts, regions = [], []
    for x, part in ((0, near), (1, far)):
        for core in range(2):
            parts.append(permute(part, 1, count) if core else part)
            regions.append((core, everything, x, upper))
    for core in range(2):
        parts.append(permute(rest, 1, count) if core else rest)
        regions.append((core, everything, everything, lower))
    return parts, regions, other_numbers


def shards(
    count, blocks, first_block, second_block, slot_counts, ket_first, ket_second, coefficients, mo_index
):
    me = lax.axis_index("pan").astype(jnp.int32)
    core = me % 2
    me_array = me.reshape(1)
    capacity, kp, pair = blocks.shape
    kh = kp // 2
    own_ao, nmo = coefficients.shape
    swap = functools.partial(permute, mask=1, count=count)

    numbers = jnp.concatenate([first_block, second_block, slot_counts, ket_first, ket_second])
    mine = coefficients.T.at[mo_index].get(
        mode="promise_in_bounds", wrap_negative_indices=False
    )
    orbitals = mine.shape[0]

    units = own_ao // 8
    factor = -(-(2**20) // max(units, 1))
    other = swap(blocks)

    small = count == 16 and own_ao % 16 == 0
    if small:
        mine = jnp.pad(mine, ((0, 0), (0, -own_ao % LANES)))
        parts, regions, other_numbers = gather_small(mine, numbers, other, count)

        def locate(unit, me):
            owner = (unit * factor) >> 20
            away = owner ^ me
            return away & 1, away >> 2, (away >> 1) & 1, (unit - owner * units) * 8
    else:
        other_numbers = swap(numbers)
        parts = [lax.all_gather(mine, "pan", axis=1, tiled=True)]
        regions = [(0, 0, 0)]

        def locate(unit, me):
            return 0, 0, 0, unit * 8

    bra = functools.partial(
        bra_transform,
        regions,
        locate,
        parts,
        blocks,
        other,
        (numbers, other_numbers),
        me_array,
        orbitals,
    )

    if small:
        chunk, side = orbitals // 8, kh // 2
        order = ((3, 0, side), (2, 0, side), (3, side, kh), (2, side, kh), (1, 0, kh), (0, 0, kh))
        pieces = order + tuple((s + 4, a, b) for s, a, b in order)
        *partial, ket = bra(chunk, pieces, BF)
        there, here = partial[:6], partial[6:]
        three_a = added(here[0], permute(there[0], 2, count))
        two_a = added(here[1], permute(there[1], 2, count), permute(three_a, 4, count))
        three_b = added(here[2], permute(there[2], 2, count))
        nothing = (three_a[0, 0] != three_a[0, 0]).astype(BF)
        two_b = added(here[3], permute(there[3] + nothing, 2, count), permute(three_b, 4, count))
        one = permute(added(here[4], permute(there[4], 2, count)), 4, count)
        zero = permute(there[5] + nothing, 2, count)
        two = jnp.concatenate([permute(two_a, 8, count), permute(two_b, 8, count)], axis=1)
        done = added(here[5], zero, one, two)
    else:
        partial, ket = bra(orbitals, ((0, 0, kh),), F32)
        sides = [list(range(c, count, 2)) for c in range(2)]
        done = lax.psum_scatter(
            partial, "pan", scatter_dimension=0, tiled=True, axis_index_groups=sides
        ).astype(BF)
    rows = done.shape[0] // 2
    keep = lax.dynamic_slice_in_dim(done, core * rows, rows, axis=0)
    give = lax.dynamic_slice_in_dim(done, (1 - core) * rows, rows, axis=0)
    return last_step(keep, swap(give), ket)


def solution(mesh):
    placed = (
        P(("grp", "pan"), None, None),
        P(("grp", "pan")),
        P(("grp", "pan")),
        P(("grp", "pan")),
        P("grp"),
        P("grp"),
        P(("grp", "pan"), None),
        P("grp"),
    )
    return jax.shard_map(
        functools.partial(shards, mesh.shape["pan"]),
        mesh=mesh,
        in_specs=placed,
        out_specs=P(("grp", "pan"), None),
        check_vma=False,
    )
```

```python
import functools

import jax
import jax.numpy as jnp
from jax import lax
from jax.experimental import pallas as pl
from jax.experimental.pallas import tpu as pltpu
from jax.sharding import PartitionSpec as P

HALF = 16
STEP = 8
LANES = 128
BF = jnp.bfloat16
F32 = jnp.float32
VMEM_LIMIT = 51 * 2**20


def spread(kind):
    row = lax.broadcasted_iota(jnp.int32, (LANES, LANES), 0)
    col = lax.broadcasted_iota(jnp.int32, (LANES, LANES), 1)
    source = col // 8 if kind == "a" else col % 8
    return (row == source).astype(F32).astype(BF)


def table_piece(table, place, target):
    core, z, x, lane = place
    inside = lane & (LANES - 1)
    start = pl.multiple_of(lane - inside, LANES)
    piece = table[core, z, x, :, pl.ds(start, LANES)].astype(F32)
    return pltpu.roll(piece, (target - inside) & (LANES - 1), 1)


def load_table(regions, parts, table, sems):
    return [
        pltpu.make_async_copy(part, table.at[region], sems.at[n])
        for n, (region, part) in enumerate(zip(regions, parts))
    ]


def bra_kernel(regions, locate, chunk, pieces, me_ref, mine, theirs, *refs):
    parts, refs = refs[: len(regions)], refs[len(regions) :]
    own, other = refs[:2]
    outs, ket = refs[2 : 2 + len(pieces)], refs[2 + len(pieces)]
    table, blk, picked_a, wide_a, picked_b, wide_b, half, second, ready = refs[3 + len(pieces) : -3]
    table_sems, block_sems, out_sems = refs[-3:]
    orbitals = second.shape[1]
    capacity = own.shape[0]
    kh = blk.shape[1]
    me = me_ref[0]
    own_live, other_live = mine[2 * capacity], theirs[2 * capacity]
    k_start = pl.multiple_of((me & 1) * kh, LANES)
    live = own_live + other_live

    copies = load_table(regions, parts, table, table_sems)
    for copy in copies:
        copy.start()

    def start_own(n, carry):
        pltpu.make_async_copy(
            own.at[n, pl.ds(k_start, kh)], blk.at[n], block_sems.at[n // STEP]
        ).start()
        return carry

    def start_other(n, carry):
        pltpu.make_async_copy(
            other.at[n - own_live, pl.ds(k_start, kh)], blk.at[n], block_sems.at[n // STEP]
        ).start()
        return carry

    lax.fori_loop(0, own_live, start_own, 0)
    lax.fori_loop(own_live, live, start_other, 0)
    lanes = lax.broadcasted_iota(jnp.int32, (8, LANES), 1)
    diagonal = (lanes % 8 == lax.broadcasted_iota(jnp.int32, (8, LANES), 0)).astype(F32)
    empty = jnp.zeros((8, LANES), F32)
    spread_a = spread("a")
    groups = (live + HALF - 1) // HALF
    steps = (live + STEP - 1) // STEP
    second[...] = jnp.zeros_like(second)

    def number(n, column):
        ours = mine[column * capacity + jnp.minimum(n, own_live - 1)]
        partners = theirs[column * capacity + jnp.maximum(n - own_live, 0)]
        return jnp.where(n < own_live, ours, partners)

    for copy in copies:
        copy.wait()

    count = ket.shape[1]
    for n in range(count):
        kb = (n + (me & 1) * (count // 2)) & (count - 1)
        piece = table_piece(table, locate(mine[2 * capacity + 1 + kb] * 2, me), 0)
        ket[0, n] = jnp.dot(piece.astype(BF), spread_a, preferred_element_type=F32)
        piece = table_piece(table, locate(mine[2 * capacity + 1 + count + kb], me), 0)
        ket[1, n] = jnp.dot(piece.astype(BF), spread("b"), preferred_element_type=F32)

    cover = 8 * STEP
    wanted = lax.broadcasted_iota(jnp.int32, (orbitals, LANES), 1)
    place = (wanted & (cover - 1)) >> 3

    def slots_of(o):
        return [jnp.minimum(o * STEP + u, live - 1) for u in range(STEP)]

    def prepare(o, picked, wide):
        slots = slots_of(o)
        for u, n in enumerate(slots):
            piece = table_piece(table, locate(number(n, 0) * 2, me), 0)
            picked[u * orbitals : (u + 1) * orbitals] = piece.astype(BF)
        wide[...] = jnp.dot(picked[...], spread_a, preferred_element_type=F32)
        parity = o & (LANES // cover - 1)
        merged = jnp.zeros((orbitals, LANES), F32)
        for u, n in enumerate(slots):
            where = locate(number(n, 1), me)
            piece = table_piece(table, where, parity * cover + 8 * u)
            merged = jnp.where(place == u, piece, merged)
        keep = (wanted // cover == parity) & (o * STEP + place < live)
        at = o // (LANES // cover)
        second[at] = jnp.where(keep, merged, second[at])

    def products(o, wide):
        slots = slots_of(o)
        for p in range(STEP // 2):
            rows = []
            for i in range(orbitals):
                x, y = (
                    jnp.broadcast_to(wide[u * orbitals + i : u * orbitals + i + 1, :], (8, LANES))
                    * diagonal
                    for u in (2 * p, 2 * p + 1)
                )
                rows.append(jnp.concatenate([x, empty], axis=1))
                rows.append(jnp.concatenate([empty, y], axis=1))
            factor = jnp.concatenate(rows, axis=0).astype(BF)
            data = jnp.concatenate([blk[slots[2 * p]], blk[slots[2 * p + 1]]], axis=1)
            at = pl.multiple_of(o * cover + 16 * p, 16)
            part = orbitals // 2
            for h in range(2):
                result = lax.dot_general(
                    factor[h * part * 16 : (h + 1) * part * 16],
                    data,
                    (((1,), (1,)), ((), ())),
                    preferred_element_type=F32,
                )
                half[h * part : (h + 1) * part, pl.ds(at, 16), :] = result.astype(BF).reshape(
                    part, 16, kh
                )

    def do_step(o, now, later):
        def wait_one(n, carry):
            pltpu.make_async_copy(
                own.at[0, pl.ds(k_start, kh)], blk.at[n], block_sems.at[o]
            ).wait()
            return carry

        lax.fori_loop(o * STEP, jnp.minimum((o + 1) * STEP, live), wait_one, 0)
        prepare(jnp.minimum(o + 1, steps - 1), *later)
        products(o, now[1])

    def two_steps(h, carry):
        do_step(2 * h, (picked_a, wide_a), (picked_b, wide_b))

        @pl.when(2 * h + 1 < steps)
        def _():
            do_step(2 * h + 1, (picked_b, wide_b), (picked_a, wide_a))

        return carry

    prepare(0, picked_a, wide_a)
    lax.fori_loop(0, (steps + 1) // 2, two_steps, 0)

    def clear(o, carry):
        at = pl.multiple_of(o * 8 * STEP, 8 * STEP)
        half[:, pl.ds(at, 8 * STEP), :] = jnp.zeros((orbitals, 8 * STEP, kh), BF)
        return carry

    lax.fori_loop(steps, groups * (HALF // STEP), clear, 0)

    def leave(n):
        s, low, high = pieces[n]
        return pltpu.make_async_copy(
            ready.at[s, :, pl.ds(low, high - low)], outs[n], out_sems.at[n]
        )

    def finish(count):
        weights = jnp.concatenate([second[n] for n in range(count)], axis=1).astype(BF)
        for s in dict.fromkeys(piece[0] for piece in pieces):
            first = 0
            if len(pieces) > 1:
                first = ((me >> 2) ^ (s & 3)) * 2 * chunk + (((me >> 1) & 1) ^ (1 - (s >> 2))) * chunk
            for r in range(chunk):
                piece = half[first + r, 0 : 8 * HALF * count, :]
                ready[s, r * orbitals : (r + 1) * orbitals, :] = jnp.dot(
                    weights, piece, preferred_element_type=F32
                ).astype(ready.dtype)
            for n in range(len(pieces)):
                if pieces[n][0] == s:
                    leave(n).start()

    for count in range(1, half.shape[1] // (8 * HALF) + 1):
        pl.when(groups == count)(functools.partial(finish, count))
    for n in range(len(pieces)):
        leave(n).wait()


def bra_transform(
    regions, locate, parts, own, other, numbers, me, orbitals, chunk, pieces, kind
):
    capacity, kp, pair = own.shape
    kh = kp // 2
    groups = -(-2 * capacity // HALF)
    rows = chunk * orbitals
    hbm = pl.BlockSpec(memory_space=pltpu.HBM)
    return pl.pallas_call(
        functools.partial(bra_kernel, regions, locate, chunk, pieces),
        out_shape=[jax.ShapeDtypeStruct((rows, high - low), kind) for _, low, high in pieces]
        + [jax.ShapeDtypeStruct((2, kp // LANES, orbitals, LANES), F32)],
        grid_spec=pltpu.PrefetchScalarGridSpec(
            num_scalar_prefetch=3,
            grid=(),
            in_specs=[hbm] * (len(parts) + 2),
            out_specs=[hbm] * len(pieces) + [pl.BlockSpec(memory_space=pltpu.VMEM)],
            scratch_shapes=[
                pltpu.VMEM(table_shape(parts, orbitals), BF),
                pltpu.VMEM((2 * capacity, kh, pair), BF),
                pltpu.VMEM((STEP * orbitals, LANES), BF),
                pltpu.VMEM((STEP * orbitals, LANES), F32),
                pltpu.VMEM((STEP * orbitals, LANES), BF),
                pltpu.VMEM((STEP * orbitals, LANES), F32),
                pltpu.VMEM((orbitals, 8 * HALF * groups, kh), BF),
                pltpu.VMEM((groups, orbitals, LANES), F32),
                pltpu.VMEM((orbitals // chunk, rows, kh), kind),
                pltpu.SemaphoreType.DMA((len(parts),)),
                pltpu.SemaphoreType.DMA((-(-2 * capacity // STEP),)),
                pltpu.SemaphoreType.DMA((len(pieces),)),
            ],
        ),
        compiler_params=pltpu.CompilerParams(vmem_limit_bytes=VMEM_LIMIT),
        cost_estimate=pl.CostEstimate(
            flops=4 * capacity * 8 * orbitals * pair * kh, bytes_accessed=8 * 2**20, transcendentals=0
        ),
        name="bra_transform",
    )(me, *numbers, *parts, own, other)


def table_shape(parts, orbitals):
    if len(parts) == 1:
        return (1, 1, 1, orbitals, parts[0].shape[-1])
    return (2, 4, 2, orbitals, parts[0].shape[-1])


def last_kernel(own, other, ket, out, tiles, results, sems):
    count, orbitals = ket.shape[1:3]
    group = tiles.shape[1] // orbitals
    half_rounded = jnp.concatenate([own[...], other[...]], axis=1)
    copies = []
    for t in range(orbitals // group):
        tile = tiles.at[t % 2]
        for n in range(count):
            last = ket[1, n]
            for r in range(group):
                row = jnp.broadcast_to(ket[0, n, t * group + r : t * group + r + 1, :], last.shape)
                tile[r * orbitals : (r + 1) * orbitals, n * LANES : (n + 1) * LANES] = (
                    row * last
                ).astype(BF)
        results[t] = lax.dot_general(
            half_rounded, tile[...], (((1,), (1,)), ((), ())), preferred_element_type=F32
        )
        columns = group * orbitals
        copies.append(
            pltpu.make_async_copy(
                results.at[t], out.at[:, pl.ds(t * columns, columns)], sems.at[t]
            )
        )
        copies[-1].start()
    for copy in copies:
        copy.wait()


def last_step(own, other, ket):
    rows, kh = own.shape
    orbitals = ket.shape[2]
    group = 4
    count = orbitals // group
    vmem = pl.BlockSpec(memory_space=pltpu.VMEM)
    return pl.pallas_call(
        last_kernel,
        out_shape=jax.ShapeDtypeStruct((rows, orbitals * orbitals), F32),
        in_specs=[vmem] * 3,
        out_specs=pl.BlockSpec(memory_space=pltpu.HBM),
        scratch_shapes=[
            pltpu.VMEM((2, group * orbitals, 2 * kh), BF),
            pltpu.VMEM((count, rows, group * orbitals), F32),
            pltpu.SemaphoreType.DMA((count,)),
        ],
        compiler_params=pltpu.CompilerParams(vmem_limit_bytes=16 * 2**20),
        name="last_step",
    )(own, other, ket)


def permute(array, mask, count):
    return lax.ppermute(array, "pan", [(i, i ^ mask) for i in range(count)])


def added(*arrays):
    result = arrays[0].astype(F32)
    for array in arrays[1:]:
        result = result + array.astype(F32)
    return result.astype(BF)


def gather_small(mine, numbers, other, count):
    middle = mine.shape[0] // 2
    a, b = mine[:middle], mine[middle:]
    b_x = permute(b, 2, count)
    a_z = {s: permute(a, 4 * s, count) for s in (3, 2, 1)}
    b_pair = jnp.stack([b, b_x])
    b_z = {s: permute(b_pair, 4 * s, count) for s in (3, 2, 1)}
    near = jnp.stack([a, a_z[1], a_z[2], a_z[3]])
    far = permute(near, 2, count)
    line = other[0, 0, : numbers.shape[0]]
    late = (line != line).astype(jnp.int32)
    other_numbers = permute(numbers + late, 1, count)
    nothing = (other_numbers[0] < 0).astype(BF)
    rest = jnp.stack([b_pair, b_z[1], b_z[2], b_z[3]]) + nothing
    upper, lower = pl.ds(0, middle), pl.ds(middle, middle)
    everything = slice(None)
    parts, regions = [], []
    for x, part in ((0, near), (1, far)):
        for core in range(2):
            parts.append(permute(part, 1, count) if core else part)
            regions.append((core, everything, x, upper))
    for core in range(2):
        parts.append(permute(rest, 1, count) if core else rest)
        regions.append((core, everything, everything, lower))
    return parts, regions, other_numbers


def shards(
    count, blocks, first_block, second_block, slot_counts, ket_first, ket_second, coefficients, mo_index
):
    me = lax.axis_index("pan").astype(jnp.int32)
    core = me % 2
    me_array = me.reshape(1)
    capacity, kp, pair = blocks.shape
    kh = kp // 2
    own_ao, nmo = coefficients.shape
    swap = functools.partial(permute, mask=1, count=count)

    numbers = jnp.concatenate([first_block, second_block, slot_counts, ket_first, ket_second])
    wanted = mo_index + (numbers[-mo_index.shape[0] :] < 0).astype(jnp.int32)
    mine = coefficients.T.at[wanted].get(
        mode="promise_in_bounds", wrap_negative_indices=False
    )
    orbitals = mine.shape[0]

    units = own_ao // 8
    factor = -(-(2**20) // max(units, 1))
    other = swap(blocks)

    small = count == 16 and own_ao % 16 == 0
    if small:
        mine = jnp.pad(mine, ((0, 0), (0, -own_ao % LANES)))
        parts, regions, other_numbers = gather_small(mine, numbers, other, count)

        def locate(unit, me):
            owner = (unit * factor) >> 20
            away = owner ^ me
            return away & 1, away >> 2, (away >> 1) & 1, (unit - owner * units) * 8
    else:
        other_numbers = swap(numbers)
        parts = [lax.all_gather(mine, "pan", axis=1, tiled=True)]
        regions = [(0, 0, 0)]

        def locate(unit, me):
            return 0, 0, 0, unit * 8

    bra = functools.partial(
        bra_transform,
        regions,
        locate,
        parts,
        blocks,
        other,
        (numbers, other_numbers),
        me_array,
        orbitals,
    )

    if small:
        chunk, side = orbitals // 8, kh // 2
        order = ((3, 0, side), (2, 0, side), (3, side, kh), (2, side, kh), (1, 0, kh), (0, 0, kh))
        pieces = order + tuple((s + 4, a, b) for s, a, b in order)
        *partial, ket = bra(chunk, pieces, BF)
        there, here = partial[:6], partial[6:]
        three_a = added(here[0], permute(there[0], 2, count))
        two_a = added(here[1], permute(there[1], 2, count), permute(three_a, 4, count))
        three_b = added(here[2], permute(there[2], 2, count))
        nothing = (three_a[0, 0] != three_a[0, 0]).astype(BF)
        two_b = added(here[3], permute(there[3] + nothing, 2, count), permute(three_b, 4, count))
        one = permute(added(here[4], permute(there[4], 2, count)), 4, count)
        zero = permute(there[5] + nothing, 2, count)
        two = jnp.concatenate([permute(two_a, 8, count), permute(two_b, 8, count)], axis=1)
        done = added(here[5], zero, one, two)
    else:
        partial, ket = bra(orbitals, ((0, 0, kh),), F32)
        sides = [list(range(c, count, 2)) for c in range(2)]
        done = lax.psum_scatter(
            partial, "pan", scatter_dimension=0, tiled=True, axis_index_groups=sides
        ).astype(BF)
    rows = done.shape[0] // 2
    keep = lax.dynamic_slice_in_dim(done, core * rows, rows, axis=0)
    give = lax.dynamic_slice_in_dim(done, (1 - core) * rows, rows, axis=0)
    return last_step(keep, swap(give), ket)


def solution(mesh):
    placed = (
        P(("grp", "pan"), None, None),
        P(("grp", "pan")),
        P(("grp", "pan")),
        P(("grp", "pan")),
        P("grp"),
        P("grp"),
        P(("grp", "pan"), None),
        P("grp"),
    )
    return jax.shard_map(
        functools.partial(shards, mesh.shape["pan"]),
        mesh=mesh,
        in_specs=placed,
        out_specs=P(("grp", "pan"), None),
        check_vma=False,
    )
```

```python
import functools

import jax
import jax.numpy as jnp
from jax import lax
from jax.experimental import pallas as pl
from jax.experimental.pallas import tpu as pltpu
from jax.sharding import PartitionSpec as P

HALF = 16
STEP = 8
LANES = 128
BF = jnp.bfloat16
F32 = jnp.float32
VMEM_LIMIT = 51 * 2**20


def spread(kind):
    row = lax.broadcasted_iota(jnp.int32, (LANES, LANES), 0)
    col = lax.broadcasted_iota(jnp.int32, (LANES, LANES), 1)
    source = col // 8 if kind == "a" else col % 8
    return (row == source).astype(F32).astype(BF)


def table_piece(table, place, target):
    core, z, x, lane = place
    inside = lane & (LANES - 1)
    start = pl.multiple_of(lane - inside, LANES)
    piece = table[core, z, x, :, pl.ds(start, LANES)].astype(F32)
    return pltpu.roll(piece, (target - inside) & (LANES - 1), 1)


def load_table(regions, parts, table, sems):
    return [
        pltpu.make_async_copy(part, table.at[region], sems.at[n])
        for n, (region, part) in enumerate(zip(regions, parts))
    ]


def bra_kernel(regions, locate, chunk, pieces, me_ref, mine, theirs, *refs):
    parts, refs = refs[: len(regions)], refs[len(regions) :]
    own, other = refs[:2]
    outs, ket = refs[2 : 2 + len(pieces)], refs[2 + len(pieces)]
    table, blk, picked_a, wide_a, picked_b, wide_b, half, second, ready = refs[3 + len(pieces) : -3]
    table_sems, block_sems, out_sems = refs[-3:]
    orbitals = second.shape[1]
    capacity = own.shape[0]
    kh = blk.shape[1]
    me = me_ref[0]
    own_live, other_live = mine[2 * capacity], theirs[2 * capacity]
    k_start = pl.multiple_of((me & 1) * kh, LANES)
    live = own_live + other_live

    copies = load_table(regions, parts, table, table_sems)
    for copy in copies:
        copy.start()

    def start_own(n, carry):
        pltpu.make_async_copy(
            own.at[n, pl.ds(k_start, kh)], blk.at[n], block_sems.at[n // STEP]
        ).start()
        return carry

    def start_other(n, carry):
        pltpu.make_async_copy(
            other.at[n - own_live, pl.ds(k_start, kh)], blk.at[n], block_sems.at[n // STEP]
        ).start()
        return carry

    lax.fori_loop(0, own_live, start_own, 0)
    lax.fori_loop(own_live, live, start_other, 0)
    lanes = lax.broadcasted_iota(jnp.int32, (8, LANES), 1)
    diagonal = (lanes % 8 == lax.broadcasted_iota(jnp.int32, (8, LANES), 0)).astype(F32)
    empty = jnp.zeros((8, LANES), F32)
    spread_a = spread("a")
    groups = (live + HALF - 1) // HALF
    steps = (live + STEP - 1) // STEP
    second[...] = jnp.zeros_like(second)

    def number(n, column):
        ours = mine[column * capacity + jnp.minimum(n, own_live - 1)]
        partners = theirs[column * capacity + jnp.maximum(n - own_live, 0)]
        return jnp.where(n < own_live, ours, partners)

    for copy in copies:
        copy.wait()

    count = ket.shape[1]
    for n in range(count):
        kb = (n + (me & 1) * (count // 2)) & (count - 1)
        piece = table_piece(table, locate(mine[2 * capacity + 1 + kb] * 2, me), 0)
        ket[0, n] = jnp.dot(piece.astype(BF), spread_a, preferred_element_type=F32)
        piece = table_piece(table, locate(mine[2 * capacity + 1 + count + kb], me), 0)
        ket[1, n] = jnp.dot(piece.astype(BF), spread("b"), preferred_element_type=F32)

    cover = 8 * STEP
    wanted = lax.broadcasted_iota(jnp.int32, (orbitals, LANES), 1)
    place = (wanted & (cover - 1)) >> 3

    def slots_of(o):
        return [jnp.minimum(o * STEP + u, live - 1) for u in range(STEP)]

    def prepare(o, picked, wide):
        slots = slots_of(o)
        for u, n in enumerate(slots):
            piece = table_piece(table, locate(number(n, 0) * 2, me), 0)
            picked[u * orbitals : (u + 1) * orbitals] = piece.astype(BF)
        wide[...] = jnp.dot(picked[...], spread_a, preferred_element_type=F32)
        parity = o & (LANES // cover - 1)
        merged = jnp.zeros((orbitals, LANES), F32)
        for u, n in enumerate(slots):
            where = locate(number(n, 1), me)
            piece = table_piece(table, where, parity * cover + 8 * u)
            merged = jnp.where(place == u, piece, merged)
        keep = (wanted // cover == parity) & (o * STEP + place < live)
        at = o // (LANES // cover)
        second[at] = jnp.where(keep, merged, second[at])

    def products(o, wide):
        slots = slots_of(o)
        for p in range(STEP // 2):
            rows = []
            for i in range(orbitals):
                x, y = (
                    jnp.broadcast_to(wide[u * orbitals + i : u * orbitals + i + 1, :], (8, LANES))
                    * diagonal
                    for u in (2 * p, 2 * p + 1)
                )
                rows.append(jnp.concatenate([x, empty], axis=1))
                rows.append(jnp.concatenate([empty, y], axis=1))
            factor = jnp.concatenate(rows, axis=0).astype(BF)
            data = jnp.concatenate([blk[slots[2 * p]], blk[slots[2 * p + 1]]], axis=1)
            at = pl.multiple_of(o * cover + 16 * p, 16)
            part = orbitals // 2
            for h in range(2):
                result = lax.dot_general(
                    factor[h * part * 16 : (h + 1) * part * 16],
                    data,
                    (((1,), (1,)), ((), ())),
                    preferred_element_type=F32,
                )
                half[h * part : (h + 1) * part, pl.ds(at, 16), :] = result.astype(BF).reshape(
                    part, 16, kh
                )

    def do_step(o, now, later):
        def wait_one(n, carry):
            pltpu.make_async_copy(
                own.at[0, pl.ds(k_start, kh)], blk.at[n], block_sems.at[o]
            ).wait()
            return carry

        lax.fori_loop(o * STEP, jnp.minimum((o + 1) * STEP, live), wait_one, 0)
        prepare(jnp.minimum(o + 1, steps - 1), *later)
        products(o, now[1])

    def two_steps(h, carry):
        do_step(2 * h, (picked_a, wide_a), (picked_b, wide_b))

        @pl.when(2 * h + 1 < steps)
        def _():
            do_step(2 * h + 1, (picked_b, wide_b), (picked_a, wide_a))

        return carry

    prepare(0, picked_a, wide_a)
    lax.fori_loop(0, (steps + 1) // 2, two_steps, 0)

    def clear(o, carry):
        at = pl.multiple_of(o * 8 * STEP, 8 * STEP)
        half[:, pl.ds(at, 8 * STEP), :] = jnp.zeros((orbitals, 8 * STEP, kh), BF)
        return carry

    lax.fori_loop(steps, groups * (HALF // STEP), clear, 0)

    def leave(n):
        s, low, high = pieces[n]
        return pltpu.make_async_copy(
            ready.at[s, :, pl.ds(low, high - low)], outs[n], out_sems.at[n]
        )

    def finish(count):
        weights = jnp.concatenate([second[n] for n in range(count)], axis=1).astype(BF)
        for s in dict.fromkeys(piece[0] for piece in pieces):
            first = 0
            if len(pieces) > 1:
                first = ((me >> 2) ^ (s & 3)) * 2 * chunk + (((me >> 1) & 1) ^ (1 - (s >> 2))) * chunk
            for r in range(chunk):
                piece = half[first + r, 0 : 8 * HALF * count, :]
                ready[s, r * orbitals : (r + 1) * orbitals, :] = jnp.dot(
                    weights, piece, preferred_element_type=F32
                ).astype(ready.dtype)
            for n in range(len(pieces)):
                if pieces[n][0] == s:
                    leave(n).start()

    for count in range(1, half.shape[1] // (8 * HALF) + 1):
        pl.when(groups == count)(functools.partial(finish, count))
    for n in range(len(pieces)):
        leave(n).wait()


def bra_transform(
    regions, locate, parts, own, other, numbers, me, orbitals, chunk, pieces, kind
):
    capacity, kp, pair = own.shape
    kh = kp // 2
    groups = -(-2 * capacity // HALF)
    rows = chunk * orbitals
    hbm = pl.BlockSpec(memory_space=pltpu.HBM)
    return pl.pallas_call(
        functools.partial(bra_kernel, regions, locate, chunk, pieces),
        out_shape=[jax.ShapeDtypeStruct((rows, high - low), kind) for _, low, high in pieces]
        + [jax.ShapeDtypeStruct((2, kp // LANES, orbitals, LANES), F32)],
        grid_spec=pltpu.PrefetchScalarGridSpec(
            num_scalar_prefetch=3,
            grid=(),
            in_specs=[hbm] * (len(parts) + 2),
            out_specs=[hbm] * len(pieces) + [pl.BlockSpec(memory_space=pltpu.VMEM)],
            scratch_shapes=[
                pltpu.VMEM(table_shape(parts, orbitals), BF),
                pltpu.VMEM((2 * capacity, kh, pair), BF),
                pltpu.VMEM((STEP * orbitals, LANES), BF),
                pltpu.VMEM((STEP * orbitals, LANES), F32),
                pltpu.VMEM((STEP * orbitals, LANES), BF),
                pltpu.VMEM((STEP * orbitals, LANES), F32),
                pltpu.VMEM((orbitals, 8 * HALF * groups, kh), BF),
                pltpu.VMEM((groups, orbitals, LANES), F32),
                pltpu.VMEM((orbitals // chunk, rows, kh), kind),
                pltpu.SemaphoreType.DMA((len(parts),)),
                pltpu.SemaphoreType.DMA((-(-2 * capacity // STEP),)),
                pltpu.SemaphoreType.DMA((len(pieces),)),
            ],
        ),
        compiler_params=pltpu.CompilerParams(vmem_limit_bytes=VMEM_LIMIT),
        cost_estimate=pl.CostEstimate(
            flops=4 * capacity * 8 * orbitals * pair * kh, bytes_accessed=8 * 2**20, transcendentals=0
        ),
        name="bra_transform",
    )(me, *numbers, *parts, own, other)


def table_shape(parts, orbitals):
    if len(parts) == 1:
        return (1, 1, 1, orbitals, parts[0].shape[-1])
    return (2, 4, 2, orbitals, parts[0].shape[-1])


def last_kernel(own, other, ket, out, tiles, results, sems):
    count, orbitals = ket.shape[1:3]
    group = tiles.shape[1] // orbitals
    half_rounded = jnp.concatenate([own[...], other[...]], axis=1)
    copies = []
    for t in range(orbitals // group):
        tile = tiles.at[t % 2]
        for n in range(count):
            last = ket[1, n]
            for r in range(group):
                row = jnp.broadcast_to(ket[0, n, t * group + r : t * group + r + 1, :], last.shape)
                tile[r * orbitals : (r + 1) * orbitals, n * LANES : (n + 1) * LANES] = (
                    row * last
                ).astype(BF)
        results[t] = lax.dot_general(
            half_rounded, tile[...], (((1,), (1,)), ((), ())), preferred_element_type=F32
        )
        columns = group * orbitals
        copies.append(
            pltpu.make_async_copy(
                results.at[t], out.at[:, pl.ds(t * columns, columns)], sems.at[t]
            )
        )
        copies[-1].start()
    for copy in copies:
        copy.wait()


def last_step(own, other, ket):
    rows, kh = own.shape
    orbitals = ket.shape[2]
    group = 4
    count = orbitals // group
    vmem = pl.BlockSpec(memory_space=pltpu.VMEM)
    return pl.pallas_call(
        last_kernel,
        out_shape=jax.ShapeDtypeStruct((rows, orbitals * orbitals), F32),
        in_specs=[vmem] * 3,
        out_specs=pl.BlockSpec(memory_space=pltpu.HBM),
        scratch_shapes=[
            pltpu.VMEM((2, group * orbitals, 2 * kh), BF),
            pltpu.VMEM((count, rows, group * orbitals), F32),
            pltpu.SemaphoreType.DMA((count,)),
        ],
        compiler_params=pltpu.CompilerParams(vmem_limit_bytes=16 * 2**20),
        name="last_step",
    )(own, other, ket)


def permute(array, mask, count):
    return lax.ppermute(array, "pan", [(i, i ^ mask) for i in range(count)])


def added(*arrays):
    result = arrays[0].astype(F32)
    for array in arrays[1:]:
        result = result + array.astype(F32)
    return result.astype(BF)


def gather_small(mine, numbers, other, count):
    middle = mine.shape[0] // 2
    a, b = mine[:middle], mine[middle:]
    b_x = permute(b, 2, count)
    a_z = {s: permute(a, 4 * s, count) for s in (3, 2, 1)}
    b_pair = jnp.stack([b, b_x])
    b_z = {s: permute(b_pair, 4 * s, count) for s in (3, 2, 1)}
    near = jnp.stack([a, a_z[1], a_z[2], a_z[3]])
    far = permute(near, 2, count)
    line = other[0, 0, : numbers.shape[0]]
    late = (line != line).astype(jnp.int32)
    other_numbers = permute(numbers + late, 1, count)
    nothing = (other_numbers[0] < 0).astype(BF)
    rest = jnp.stack([b_pair, b_z[1], b_z[2], b_z[3]]) + nothing
    upper, lower = pl.ds(0, middle), pl.ds(middle, middle)
    everything = slice(None)
    parts, regions = [], []
    for x, part in ((0, near), (1, far)):
        for core in range(2):
            parts.append(permute(part, 1, count) if core else part)
            regions.append((core, everything, x, upper))
    for core in range(2):
        parts.append(permute(rest, 1, count) if core else rest)
        regions.append((core, everything, everything, lower))
    return parts, regions, other_numbers


def shards(
    count, blocks, first_block, second_block, slot_counts, ket_first, ket_second, coefficients, mo_index
):
    me = lax.axis_index("pan").astype(jnp.int32)
    core = me % 2
    me_array = me.reshape(1)
    capacity, kp, pair = blocks.shape
    kh = kp // 2
    own_ao, nmo = coefficients.shape
    swap = functools.partial(permute, mask=1, count=count)

    numbers = jnp.concatenate([first_block, second_block, slot_counts, ket_first, ket_second])
    wanted = mo_index + (numbers[-mo_index.shape[0] :] < 0).astype(jnp.int32)
    mine = coefficients.T.at[wanted].get(
        mode="promise_in_bounds", wrap_negative_indices=False
    )
    orbitals = mine.shape[0]

    units = own_ao // 8
    factor = -(-(2**20) // max(units, 1))
    other = swap(blocks)

    small = count == 16 and own_ao % 16 == 0
    if small:
        mine = jnp.pad(mine, ((0, 0), (0, -own_ao % LANES)))
        parts, regions, other_numbers = gather_small(mine, numbers, other, count)

        def locate(unit, me):
            owner = (unit * factor) >> 20
            away = owner ^ me
            return away & 1, away >> 2, (away >> 1) & 1, (unit - owner * units) * 8
    else:
        other_numbers = swap(numbers)
        parts = [lax.all_gather(mine, "pan", axis=1, tiled=True)]
        regions = [(0, 0, 0)]

        def locate(unit, me):
            return 0, 0, 0, unit * 8

    bra = functools.partial(
        bra_transform,
        regions,
        locate,
        parts,
        blocks,
        other,
        (numbers, other_numbers),
        me_array,
        orbitals,
    )

    if small:
        chunk, side = orbitals // 8, kh // 2
        order = ((3, 0, side), (2, 0, side), (3, side, kh), (2, side, kh), (1, 0, kh), (0, 0, kh))
        pieces = order + tuple((s + 4, a, b) for s, a, b in order[:5])
        pieces += ((4, 0, side), (4, side, kh))
        *partial, ket = bra(chunk, pieces, BF)
        there, here = partial[:6], partial[6:]
        three_a = added(here[0], permute(there[0], 2, count))
        two_a = added(here[1], permute(there[1], 2, count), permute(three_a, 4, count))
        three_b = added(here[2], permute(there[2], 2, count))
        nothing = (three_a[0, 0] != three_a[0, 0]).astype(BF)
        two_b = added(here[3], permute(there[3] + nothing, 2, count), permute(three_b, 4, count))
        one = permute(added(here[4], permute(there[4], 2, count)), 4, count)
        zero = permute(there[5] + nothing, 2, count)
        two = jnp.concatenate([permute(two_a, 8, count), permute(two_b, 8, count)], axis=1)
        done = added(jnp.concatenate(here[5:], axis=1), zero, one, two)
    else:
        partial, ket = bra(orbitals, ((0, 0, kh),), F32)
        sides = [list(range(c, count, 2)) for c in range(2)]
        done = lax.psum_scatter(
            partial, "pan", scatter_dimension=0, tiled=True, axis_index_groups=sides
        ).astype(BF)
    rows = done.shape[0] // 2
    keep = lax.dynamic_slice_in_dim(done, core * rows, rows, axis=0)
    give = lax.dynamic_slice_in_dim(done, (1 - core) * rows, rows, axis=0)
    return last_step(keep, swap(give), ket)


def solution(mesh):
    placed = (
        P(("grp", "pan"), None, None),
        P(("grp", "pan")),
        P(("grp", "pan")),
        P(("grp", "pan")),
        P("grp"),
        P("grp"),
        P(("grp", "pan"), None),
        P("grp"),
    )
    return jax.shard_map(
        functools.partial(shards, mesh.shape["pan"]),
        mesh=mesh,
        in_specs=placed,
        out_specs=P(("grp", "pan"), None),
        check_vma=False,
    )
```
